128 devices in a mesh: group: 4 (over x), seq: 32 (over y, z, core).
Axes of the slice: x: 4, y: 4, z: 4, core: 2. Of those that a mesh axis runs over, the one named last changes fastest.
Arguments:
- layer_input: bfloat16 [4, 24576, 5120], P('group', 'seq'), may hold values from -6 to 6
- x_values: bfloat16 [4, 24576, 2560], P('group', 'seq'), may hold values from -6 to 6
- out_grad: bfloat16 [4, 24576, 2560], P('group', 'seq'), may hold values from -0.29882812 to 0.29882812
- b_values: bfloat16 [4, 24576, 128], P('group', 'seq'), may hold values from -0.3 to 0.3
- c_values: bfloat16 [4, 24576, 128], P('group', 'seq'), may hold values from -0.29882812 to 0.29882812
- step_sizes: float32 [4, 40, 24576], P('group', None, 'seq'), may hold values from 0.5 to 36866
- decay_rates: float32 [40], replicated, may hold values from 4.06901042e-06 to 0.06
- prompt_state: float32 [4, 2560, 128], P('group', 'seq'), may hold values from -6 to 6
- lengths: int32 [4, 4], P('group'), may hold values from 1 to 48, 96 in all within a row
Outputs:
- x_grad: bfloat16 [4, 24576, 2560], P('group', 'seq')
- prompt_grad: float32 [4, 2560, 128], P('group', 'seq')
- weight_grad: float32 [5120, 256], P(('group', 'seq'))
The draws below stay inside these ranges and needn't reach their ends.
Inputs may be any that keep to these rules, and one draw needn't show every extreme that they name: The 4 lengths of a prompt sum to 96, and the longest is exactly 48.
All inputs are finite; a program needn't handle non-finite values.
Results may differ from the reference program's by a relative error of at most 0.0062.
Values sent between devices are 32-bit elements; how exact they have to be, the bound alone decides.
A program may use at most 320 MiB of HBM per device.

```python
import math
import jax
import jax.numpy as jnp
import numpy as np
from jax import lax

D = 5120
HEADS = 40
HDIM = 64
STATE = 128
BLOCK = 256
SAMPLES = 4
GROUP_BLOCKS = 96
LONGEST = 48
TOKENS = 24576
PROMPTS = 4


def spurt_token_rows(key):
    linked_sequence = 1.0 * LONGEST * BLOCK
    return jax.random.bernoulli(jax.random.fold_in(key, 97), 2.0 / linked_sequence, (PROMPTS, TOKENS))


def input_factor(key):
    linked_sequence = 1.0 * LONGEST * BLOCK
    return jnp.where(spurt_token_rows(key), 1.0 / (3.0 * linked_sequence), 1.0).astype(jnp.float32)


def draw_step_sizes(key, part):
    token_spurts = spurt_token_rows(key)
    key = jax.random.fold_in(key, 11)
    shape = (PROMPTS, HEADS, TOKENS)
    linked_sequence = 1.0 * LONGEST * BLOCK
    base_offset = jnp.exp(jax.random.uniform(key, shape, jnp.float32, math.log(0.5), math.log(2.0)))
    return base_offset + jnp.where(token_spurts[:, None, :], 3.0 * linked_sequence, 0.0).astype(jnp.float32)


def draw_x_values(key, part):
    factor = input_factor(key)
    key = jax.random.fold_in(key, 31)
    shape = (PROMPTS, TOKENS, HEADS * HDIM)
    values = jax.random.truncated_normal(key, -6.0, 6.0, shape, jnp.float32)
    return (values * factor[:, :, None]).astype(jnp.bfloat16)


def draw_b_values(key, part):
    factor = input_factor(key)
    key = jax.random.fold_in(key, 41)
    shape = (PROMPTS, TOKENS, STATE)
    values = jax.random.truncated_normal(key, -6.0, 6.0, shape, jnp.float32)
    return (0.05 * values * factor[:, :, None]).astype(jnp.bfloat16)


def draw_decay_rates(key, part):
    key = jax.random.fold_in(key, 23)
    secondary_random_key, fast_key, pick_key = jax.random.split(key, 3)
    linked_sequence = 1.0 * LONGEST * BLOCK
    slow = jnp.exp(jax.random.uniform(secondary_random_key, (HEADS,), jnp.float32, math.log(0.05), math.log(0.5))) / linked_sequence
    fast = jnp.exp(jax.random.uniform(fast_key, (HEADS,), jnp.float32, math.log(0.02), math.log(0.06)))
    picked = jax.random.bernoulli(pick_key, 0.5, (HEADS,))
    return jnp.where(picked, slow, fast).astype(jnp.float32)


def with_spikes(entries, rng, source, target, blocks, factor):
    owner, partner = [(jnp.arange(entries.shape[dim]) // (entries.shape[dim] // blocks)).reshape([-1 if axis == dim else 1 for axis in range(entries.ndim)]) for dim in (source, target)]
    chosen = jax.random.permutation(rng, blocks)[partner]
    strong = (owner == chosen) | (owner == (partner + blocks // 2) % blocks)
    return jnp.where(strong, factor * entries, entries)


def block_scale(key, shape, pieces, least, top_value):
    def one(dim, blocks):
        draws = jax.random.uniform(jax.random.fold_in(jax.random.fold_in(key, 6), dim), (blocks,), jnp.float32, least / len(pieces), top_value / len(pieces))
        return jnp.repeat(jnp.exp(draws), shape[dim] // blocks).reshape((-1,) + (1,) * (len(shape) - dim - 1))

    loudness = one(*pieces[0])
    for cut in pieces[1:]:
        loudness = loudness * one(*cut)
    return loudness


def split_up(count, total, most, skew):
    loads = [(1 << 20) // math.isqrt(grade ** skew) + 1 for grade in range(2, count + 1)]
    spare, counts = total - most - (count - 1), [1] * (count - 1)
    while spare > 0:
        free = [i for i in range(count - 1) if counts[i] < most]
        whole, left = sum([loads[i] for i in free]), spare
        for i in free:
            more = min(most - counts[i], max(1, left * loads[i] // whole), spare)
            counts[i] = counts[i] + more
            spare = spare - more
    return np.array([most] + counts)


def uneven_parts(stream_key, count, total, reach, slope):
    if count == 2:
        one = jax.random.randint(stream_key, (), max(1, total - reach), min(reach, total - 1) + 1)
        return jnp.stack([one, total - one])
    tallies = jnp.asarray(split_up(count, total, reach, slope), jnp.int32)
    pairs = (count - 1) // 2
    giver, receiver = tallies[1:1 + 2 * pairs:2], tallies[2:2 + 2 * pairs:2]
    margin = jnp.minimum(giver - 1, reach - receiver)
    moved = jax.random.randint(jax.random.fold_in(stream_key, 1), (pairs,), 0, 1 << 20) % (margin + 1)
    tallies = tallies.at[1:1 + 2 * pairs:2].set(giver - moved).at[2:2 + 2 * pairs:2].set(receiver + moved)
    return tallies[jax.random.permutation(jax.random.fold_in(stream_key, 2), count)]


def gaussian(stream_key, dims, scale, bound, pieces=(), held_as=jnp.bfloat16):
    gain = block_scale(stream_key, dims, pieces, -0.22, 0.18) if pieces else 1.0
    entries = jax.random.normal(stream_key, dims, jnp.float32) * scale * gain
    return jnp.minimum(jnp.maximum(entries, -bound), bound).astype(held_as)


def noise_with(own_key, extent, scale, most, cuts, heavy, dtype=jnp.bfloat16):
    array = scale * jax.random.normal(own_key, extent, jnp.float32)
    if cuts:
        array = array * block_scale(own_key, extent, cuts, -0.22, 0.18)
    return jnp.clip(with_spikes(array, jax.random.fold_in(own_key, 3), *heavy), -most, most).astype(dtype)


def setup_inputs(seed: int = 0) -> dict:
    key_of = jax.random.split(jax.random.key(seed), 10)
    layer_input = noise_with(key_of[0], (PROMPTS, TOKENS, D), 1.0, 6.0, ((0, 4), (1, 32)), (1, 2, 32, 2.75))
    x_values = draw_x_values(jax.random.fold_in(key_of[9], 71), 0)
    out_grad = gaussian(key_of[2], (PROMPTS, TOKENS, HEADS * HDIM), 0.05, 0.29882812, ((0, 4), (1, 32)))
    b_values = draw_b_values(jax.random.fold_in(key_of[9], 71), 0)
    c_values = gaussian(key_of[4], (PROMPTS, TOKENS, STATE), 0.05, 0.29882812, ((0, 4), (1, 32)))
    step_sizes = draw_step_sizes(jax.random.fold_in(key_of[9], 71), 0)
    decay_rates = draw_decay_rates(jax.random.fold_in(key_of[9], 71), 0)
    prompt_state = gaussian(key_of[7], (PROMPTS, HEADS * HDIM, STATE), 1.0, 6.0, ((0, 4), (1, 32)), jnp.float32)
    lengths = jax.vmap(lambda own: uneven_parts(own, SAMPLES, GROUP_BLOCKS, LONGEST, 2))(jax.random.split(key_of[8], PROMPTS)).reshape((PROMPTS, SAMPLES)).astype(jnp.int32)
    return dict(layer_input=layer_input, x_values=x_values, out_grad=out_grad, b_values=b_values, c_values=c_values, step_sizes=step_sizes, decay_rates=decay_rates, prompt_state=prompt_state, lengths=lengths)


def block_logs(step_block, decay_rates):
    return jnp.cumsum(-step_block * decay_rates[:, None], axis=1)


def summarize(x_block, grad_block, b_block, c_block, step_block, decay_rates):
    log_decay = block_logs(step_block, decay_rates)
    block_end = log_decay[:, -1:]
    rescaled_input = (x_block * (jnp.exp(block_end - log_decay) * step_block).T[:, :, None]).astype(jnp.bfloat16)
    rescaled_gradient = (grad_block * jnp.exp(log_decay).T[:, :, None]).astype(jnp.bfloat16)
    local_state = jnp.einsum("lhp,ln->hpn", rescaled_input.astype(jnp.float32), b_block.astype(jnp.float32))
    local_grad = jnp.einsum("lhp,ln->hpn", rescaled_gradient.astype(jnp.float32), c_block.astype(jnp.float32))
    return jnp.exp(block_end[:, 0]), rescaled_input, rescaled_gradient, local_state, local_grad


def process(x_block, grad_block, b_block, c_block, step_block, rescaled_input, rescaled_gradient, entering, leaving, decay_rates):
    log_decay = block_logs(step_block, decay_rates)
    block_end = log_decay[:, -1:]
    width = step_block.shape[1]
    places = jnp.arange(width)
    causal = places[:, None] >= places[None, :]
    gap_matrix = log_decay[:, :, None] - log_decay[:, None, :]
    masked = jnp.exp(jnp.where(causal[None], gap_matrix, -jnp.inf))
    x_wide = x_block.astype(jnp.float32)
    grad_wide = grad_block.astype(jnp.float32)
    b_wide = b_block.astype(jnp.float32)
    c_wide = c_block.astype(jnp.float32)
    products = jnp.einsum("thp,shp->hts", grad_wide, x_wide)
    inner = jnp.dot(c_wide, b_wide.T)
    dx_weights = (masked * inner[None]).astype(jnp.bfloat16)
    leaving_low = leaving.astype(jnp.bfloat16)
    entering_low = entering.astype(jnp.bfloat16)
    dx_inner = jnp.einsum("hst,shp->thp", dx_weights.astype(jnp.float32), grad_wide)
    dx_outer = jnp.einsum("tn,hpn->thp", b_wide, leaving_low.astype(jnp.float32))
    x_grad = step_block.T[:, :, None] * (dx_inner + jnp.exp(block_end - log_decay).T[:, :, None] * dx_outer)
    pair_weights = jnp.sum(masked * products * step_block[:, None, :], axis=0).astype(jnp.bfloat16)
    pair_wide = pair_weights.astype(jnp.float32)
    b_gradient = jnp.einsum("st,sn->tn", pair_wide, c_wide) + jnp.einsum("thp,hpn->tn", rescaled_input.astype(jnp.float32), leaving_low.astype(jnp.float32))
    readout_gradient = jnp.einsum("ts,sn->tn", pair_wide, b_wide) + jnp.einsum("thp,hpn->tn", rescaled_gradient.astype(jnp.float32), entering_low.astype(jnp.float32))
    return x_grad.astype(jnp.bfloat16), jnp.concatenate([b_gradient, readout_gradient], axis=1).astype(jnp.bfloat16)


def group_flags(sample_lengths, block_ids):
    sample_ends = jnp.cumsum(sample_lengths)
    sample_starts = sample_ends - sample_lengths
    is_start = jnp.any(sample_starts[:, None] == block_ids[None, :], axis=0)
    is_last = jnp.any((sample_ends - 1)[:, None] == block_ids[None, :], axis=0)
    return is_start, is_last


def forward_step(prompt, carry, items):
    start, decay, local = items
    entering = jnp.where(start, prompt, carry)
    return decay[:, None, None] * entering + local, entering


def backward_step(carry, items):
    last, decay, local = items
    leaving = jnp.where(last, jnp.zeros_like(carry), carry)
    passed = decay[:, None, None] * leaving + local
    return passed, (leaving, passed)


def reference(layer_input, x_values, out_grad, b_values, c_values, step_sizes, decay_rates, prompt_state, lengths):
    n_blocks = TOKENS // BLOCK
    weight_grad = jnp.zeros((D, 2 * STATE), jnp.float32)
    x_grads = []
    prompt_grads = []
    for group in range(PROMPTS):
        x_blocks = x_values[group].reshape(n_blocks, BLOCK, HEADS, HDIM)
        grad_blocks = out_grad[group].reshape(n_blocks, BLOCK, HEADS, HDIM)
        b_blocks = b_values[group].reshape(n_blocks, BLOCK, STATE)
        c_blocks = c_values[group].reshape(n_blocks, BLOCK, STATE)
        step_blocks = step_sizes[group].reshape(HEADS, n_blocks, BLOCK).transpose(1, 0, 2)
        decays, rescaled_input, rescaled_gradient, local_state, local_grad = lax.map(
            lambda items: summarize(*items, decay_rates), (x_blocks, grad_blocks, b_blocks, c_blocks, step_blocks))
        is_start, is_last = group_flags(lengths[group], jnp.arange(n_blocks).astype(jnp.int32))
        prompt = prompt_state[group].reshape(HEADS, HDIM, STATE)
        zeros = jnp.zeros((HEADS, HDIM, STATE), jnp.float32)
        _, entering = lax.scan(lambda carry, items: forward_step(prompt, carry, items), zeros, (is_start, decays, local_state))
        _, (leaving, passed) = lax.scan(backward_step, zeros, (is_last, decays, local_grad), reverse=True)
        prompt_sum = jnp.sum(jnp.where(is_start[:, None, None, None], passed, jnp.zeros_like(passed)), axis=0)
        prompt_grads.append(prompt_sum.reshape(HEADS * HDIM, STATE))
        x_grad, bc_grad = lax.map(
            lambda items: process(*items, decay_rates),
            (x_blocks, grad_blocks, b_blocks, c_blocks, step_blocks, rescaled_input, rescaled_gradient, entering, leaving))
        x_grads.append(x_grad.reshape(TOKENS, HEADS * HDIM))
        weight_grad = weight_grad + jnp.einsum("td,tk->dk", layer_input[group].astype(jnp.float32), bc_grad.reshape(TOKENS, 2 * STATE).astype(jnp.float32))
    return jnp.stack(x_grads), jnp.stack(prompt_grads), weight_grad
```

```python
from functools import partial

import jax
import jax.numpy as jnp
from jax import lax
from jax.experimental import pallas as pl
from jax.experimental.pallas import tpu as pltpu
from jax.sharding import PartitionSpec as P

BLOCK = 256
NBLK = 3
TOK = BLOCK * NBLK
HEADS = 40
PAIRS = HEADS // 2
STATE = 128
WIDTH = 2560
DMODEL = 5120
CHUNK = 80
MESSAGE = 3 * CHUNK + 8
F32 = jnp.float32
BF16 = jnp.bfloat16
MESH = pl.DeviceIdType.MESH
TN = (((0,), (0,)), ((), ()))
NT = (((1,), (1,)), ((), ()))
VMEM_LIMIT = 56 * 1024 * 1024


def dot(a, b, dims=(((1,), (0,)), ((), ()))):
    return lax.dot_general(a, b, dims, preferred_element_type=F32)


def iota(shape, dim):
    return lax.broadcasted_iota(jnp.int32, shape, dim)


def flags(lens_ref):
    first = lax.axis_index("seq") * NBLK
    e1 = lens_ref[0, 0]
    e2 = e1 + lens_ref[0, 1]
    e3 = e2 + lens_ref[0, 2]
    e4 = e3 + lens_ref[0, 3]
    not_start, not_last = [], []
    for k in range(NBLK):
        at = first + k
        start = (at == 0) | (at == e1) | (at == e2) | (at == e3)
        last = (at == e1 - 1) | (at == e2 - 1) | (at == e3 - 1) | (at == e4 - 1)
        not_start.append(jnp.where(start, 0.0, 1.0).astype(F32))
        not_last.append(jnp.where(last, 0.0, 1.0).astype(F32))
    return not_start, not_last


def parts_of(value, count):
    out = []
    for _ in range(count):
        high = value.astype(BF16).astype(F32)
        out.append(high)
        value = value - high
    return out


def columns(value, count):
    pieces = parts_of(value, count)
    pieces.append(jnp.zeros((128 - HEADS * count, value.shape[1]), F32))
    return jnp.concatenate(pieces, axis=0).T.astype(BF16)


def selector(first_head, count, lanes_per_head, width):
    row, lane = iota((128, width), 0), iota((128, width), 1)
    head = first_head + lane // lanes_per_head
    hit = row == head
    for n in range(1, count):
        hit = hit | (row == head + HEADS * n)
    return jnp.where(hit, 1.0, 0.0).astype(BF16)


def pair_decays(la_ref, pair):
    out = []
    rows = [la_ref[pl.ds(2 * pair + j, 1), :] for j in range(2)]
    for k in range(NBLK):
        at = BLOCK * (k + 1) - 1
        out.append(
            jnp.concatenate(
                [jnp.broadcast_to(jnp.exp(r[:, at : at + 1]), (64, 128)) for r in rows], axis=0
            )
        )
    return out


def summary_kernel(
    lens_ref, step_ref, rate_ref, x_ref, g_ref, b_ref, c_ref,
    f_ref, r_ref, u_ref, loc_ref, coef_ref, la_ref, w3_ref, s2_ref, x2_ref, g2_ref, all_ref,
):
    pair = pl.program_id(0)
    ns, nl = flags(lens_ref)

    @pl.when(pair == 0)
    def _():
        step = step_ref[...]
        la = -step * rate_ref[...]
        place = iota((HEADS, TOK), 1) % BLOCK
        shift = 1
        while shift < BLOCK:
            la = la + jnp.where(place >= shift, pltpu.roll(la, shift, 1), 0.0)
            shift *= 2
        la_ref[...] = la
        ends = [la[:, BLOCK * (k + 1) - 1 : BLOCK * (k + 1)] for k in range(NBLK)]
        end = jnp.concatenate([jnp.broadcast_to(e, (HEADS, BLOCK)) for e in ends], axis=1)
        w3_ref[...] = columns(la, 3)
        s2_ref[...] = columns(step, 2)
        x2_ref[...] = columns(jnp.exp(end - la) * step, 2)
        g2_ref[...] = columns(jnp.exp(la), 2)
        dec = [jnp.broadcast_to(jnp.exp(e), (HEADS, 128)) for e in ends]
        af = jnp.ones((HEADS, 128), F32)
        pc = jnp.zeros((HEADS, 128), F32)
        for k in range(NBLK):
            af = af * dec[k] * ns[k]
            pc = dec[k] * (pc * ns[k] + (1.0 - ns[k]))
        ab = jnp.ones((HEADS, 128), F32)
        uc = jnp.zeros((HEADS, 128), F32)
        for k in reversed(range(NBLK)):
            ab = ab * dec[k] * nl[k]
            uc = uc + ab * (1.0 - ns[k])
        for n, value in enumerate((af, pc, ab, uc)):
            all_ref[n] = value
        for o in range(32):
            h = CHUNK * o // 64
            for n in range(4):
                coef_ref[o, 2 * n : 2 * n + 2, :] = all_ref[n, h : h + 2, :]

    sel = selector(2 * pair, 2, 64, 128)
    sx = (x_ref[...].astype(F32) * dot(x2_ref[...], sel)).astype(BF16)
    sg = (g_ref[...].astype(F32) * dot(g2_ref[...], sel)).astype(BF16)
    dec = pair_decays(la_ref, pair)
    ls, lg = [], []
    for k in range(NBLK):
        rows = slice(BLOCK * k, BLOCK * (k + 1))
        ls.append(dot(sx[rows], b_ref[rows, :], TN))
        lg.append(dot(sg[rows], c_ref[rows, :], TN))
    f = ls[0]
    for k in range(1, NBLK):
        f = (dec[k] * ns[k]) * f + ls[k]
    f_ref[...] = f
    r = lg[2]
    u = r * (1.0 - ns[2])
    for k in (1, 0):
        r = dec[k] * (r * nl[k]) + lg[k]
        u = u + r * (1.0 - ns[k])
    r_ref[...] = r
    u_ref[...] = u
    loc_ref[0] = ls[0]
    loc_ref[1] = ls[1]
    loc_ref[2] = lg[1]
    loc_ref[3] = lg[2]


def summarize(lens, step, rates, x, g, b, c):
    whole = lambda *shape: pl.BlockSpec(shape, lambda i: (0,) * len(shape))
    lanes = pl.BlockSpec((TOK, 128), lambda i: (0, i))
    rows = pl.BlockSpec((128, 128), lambda i: (i, 0))
    state = jax.ShapeDtypeStruct((WIDTH, STATE), F32)
    cols = jax.ShapeDtypeStruct((TOK, 128), BF16)
    return pl.pallas_call(
        summary_kernel,
        grid=(PAIRS,),
        in_specs=[
            pl.BlockSpec(memory_space=pltpu.SMEM),
            whole(HEADS, TOK), whole(HEADS, 1), lanes, lanes, whole(TOK, 128), whole(TOK, 128),
        ],
        out_specs=[
            rows, rows, rows, pl.BlockSpec((4, 128, 128), lambda i: (0, i, 0)),
            whole(32, 8, 128), whole(HEADS, TOK),
            whole(TOK, 128), whole(TOK, 128), whole(TOK, 128), whole(TOK, 128),
        ],
        out_shape=[
            state, state, state, jax.ShapeDtypeStruct((4, WIDTH, STATE), F32),
            jax.ShapeDtypeStruct((32, 8, 128), F32), jax.ShapeDtypeStruct((HEADS, TOK), F32),
            cols, cols, cols, cols,
        ],
        scratch_shapes=[pltpu.VMEM((4, HEADS, 128), F32)],
        compiler_params=pltpu.CompilerParams(vmem_limit_bytes=VMEM_LIMIT),
    )(lens, step, rates, x, g, b, c)


def inside_unit(u, x_v, g_v, b_ref, c_ref, la_ref, w3_ref, s2_ref, inner_v, pt_v, dx_v):
    k, pair = u // PAIRS, u % PAIRS
    r = pl.ds(pl.multiple_of(k * BLOCK, BLOCK), BLOCK)
    l = pl.ds(pl.multiple_of(pair * 128, 128), 128)

    @pl.when(pair == 0)
    def _():
        keep = iota((BLOCK, BLOCK), 1) >= iota((BLOCK, BLOCK), 0)
        inner_v[...] = jnp.where(keep, dot(b_ref[r, :], c_ref[r, :], NT), 0.0)
        pt_v[k] = jnp.zeros((BLOCK, BLOCK), F32)

    g = g_v[r, l]
    col = dot(w3_ref[r, :], selector(2 * pair, 3, 128, 256))
    xs = (x_v[r, l].astype(F32) * dot(s2_ref[r, :], selector(2 * pair, 2, 64, 128))).astype(BF16)
    lane = iota((1, 128), 1)
    a00 = a01 = a11 = d0 = d1 = None
    plus = lambda a, b: b if a is None else a + b
    for j in range(2):
        gj = g * jnp.where((lane >= 64) == bool(j), 1.0, 0.0).astype(BF16)
        p0 = dot(xs[:128], gj, NT)
        p1 = dot(xs[128:], gj[128:], NT)
        row = la_ref[pl.ds(2 * pair + j, 1), r]
        cj = col[:, 128 * j : 128 * (j + 1)]
        q00 = jnp.exp(jnp.minimum(row[:, :128] - cj[:128], 0.0))
        q01 = jnp.exp(jnp.minimum(row[:, 128:] - cj[:128], 0.0))
        q11 = jnp.exp(jnp.minimum(row[:, 128:] - cj[128:], 0.0))
        a00 = plus(a00, q00 * p0[:, :128])
        a01 = plus(a01, q01 * p0[:, 128:])
        a11 = plus(a11, q11 * p1)
        w00 = (q00 * inner_v[:128, :128]).astype(BF16)
        w01 = (q01 * inner_v[:128, 128:]).astype(BF16)
        w11 = (q11 * inner_v[128:, 128:]).astype(BF16)
        d0 = plus(d0, dot(jnp.concatenate([w00, w01], axis=1), gj))
        d1 = plus(d1, dot(w11, gj[128:]))
    pt_v[k, :128, :128] += a00
    pt_v[k, :128, 128:] += a01
    pt_v[k, 128:, 128:] += a11
    dx_v[r, l] = jnp.concatenate([d0, d1], axis=0).astype(BF16)


def spread(tile, n, split):
    return jnp.where(iota((CHUNK, 128), 0) < split, tile[2 * n : 2 * n + 1], tile[2 * n + 1 : 2 * n + 2])


def split_of(owner):
    return 64 - (CHUNK * owner) % 64


def carry_kernel(
    f_ref, r_ref, u_ref, coef_ref, p_ref, x_hbm, g_hbm, b_ref, c_ref, la_ref, w3_ref, s2_ref,
    e_ref, l_ref, pr_ref, pg_ref, pt_ref, dx_hbm,
    x_v, g_v, dx_v, inner_v, pt_v,
    sf, sr, su, sc, prompts, comb, got, back, ret, sib_e, sib_l, sib_p,
    load_sem, sib_send, sib_recv, p_send, p_recv, a_send, a_recv, b_send, b_recv,
):
    group, seq = lax.axis_index("group"), lax.axis_index("seq")
    core = seq % 2
    chip = seq // 2
    y, z = chip // 4, chip % 4
    sibling = (group, chip * 2 + (1 - core))

    def peer(d):
        return (group, (((y + d // 4) % 4) * 4 + (z + d % 4) % 4) * 2 + core)

    def send(src, dst, s, r, to):
        return pltpu.make_async_remote_copy(
            src_ref=src, dst_ref=dst, send_sem=s, recv_sem=r, device_id=to, device_id_type=MESH
        )

    loads = [
        pltpu.make_async_copy(x_hbm, x_v, load_sem.at[0]),
        pltpu.make_async_copy(g_hbm, g_v, load_sem.at[1]),
    ]
    for c in loads:
        c.start()

    barrier = pltpu.get_barrier_semaphore()
    pl.semaphore_signal(barrier, inc=1, device_id=sibling, device_id_type=MESH)

    def greet(d, _):
        pl.semaphore_signal(barrier, inc=1, device_id=peer(d), device_id_type=MESH)
        return 0

    lax.fori_loop(1, 16, greet, 0)
    pl.semaphore_wait(barrier, 16)

    first = [
        send(a.at[:, 1 - core], t, sib_send.at[n], sib_recv.at[n], sibling)
        for n, (a, t) in enumerate(((f_ref, sf), (r_ref, sr), (u_ref, su), (coef_ref, sc)))
    ]
    for c in first:
        c.start()

    def prompt_copy(d):
        return send(p_ref, prompts.at[chip], p_send.at[d], p_recv.at[d], peer(d))

    lax.fori_loop(1, 16, lambda d, _: (prompt_copy(d).start(), 0)[1], 0)
    prompts[chip] = p_ref[...]

    unit = lambda u, _: (
        inside_unit(u, x_v, g_v, b_ref, c_ref, la_ref, w3_ref, s2_ref, inner_v, pt_v, dx_v), 0
    )[1]
    for c in loads:
        c.wait()
    lax.fori_loop(0, 8, unit, 0)

    for c in first:
        c.wait()
    is0 = core == 0
    pick = lambda mine, theirs: (jnp.where(is0, mine, theirs), jnp.where(is0, theirs, mine))

    def combine(q, _):
        split = split_of(2 * q + core)
        t0, t1 = pick(coef_ref[q, core], sc[q])
        f0, f1 = pick(f_ref[q, core], sf[q])
        r0, r1 = pick(r_ref[q, core], sr[q])
        comb[q, 0:CHUNK, :] = f1 + spread(t1, 0, split) * f0
        comb[q, CHUNK : 2 * CHUNK, :] = r0 + spread(t0, 2, split) * r1
        comb[q, 2 * CHUNK : 3 * CHUNK, :] = (
            u_ref[q, core] + su[q] + spread(t0, 3, split) * r1
        )
        comb[q, 3 * CHUNK :, :] = jnp.concatenate(
            [
                t0[0:2] * t1[0:2],
                t1[2:4] + t1[0:2] * t0[2:4],
                t0[4:6] * t1[4:6],
                t1[6:8] + t0[6:8] * t1[4:6],
            ],
            axis=0,
        )
        return 0

    lax.fori_loop(0, 16, combine, 0)

    def out_copy(d):
        to = peer(d)
        return send(comb.at[to[1] // 2], got.at[d], a_send.at[d], a_recv.at[d], to)

    lax.fori_loop(1, 16, lambda d, _: (out_copy(d).start(), 0)[1], 0)
    got[0] = comb[chip]

    lax.fori_loop(8, 34, unit, 0)

    lax.fori_loop(1, 16, lambda d, _: (out_copy(d).wait(), 0)[1], 0)
    split = split_of(seq)

    def slot(q):
        return ((y + 4 - q // 4) % 4) * 4 + (z + 4 - q % 4) % 4

    own = p_ref[...]

    def forward(q, e):
        s = slot(q)
        back[q, 0:CHUNK, :] = e
        t = got[s, 3 * CHUNK :, :]
        return spread(t, 0, split) * e + spread(t, 1, split) * own + got[s, 0:CHUNK, :]

    lax.fori_loop(0, 16, forward, jnp.zeros((CHUNK, 128), F32))

    def backward(n, carry):
        lv, total = carry
        q = 15 - n
        s = slot(q)
        back[q, CHUNK:, :] = lv
        t = got[s, 3 * CHUNK :, :]
        total = total + got[s, 2 * CHUNK : 3 * CHUNK, :] + spread(t, 3, split) * lv
        return spread(t, 2, split) * lv + got[s, CHUNK : 2 * CHUNK, :], total

    zero = jnp.zeros((CHUNK, 128), F32)
    _, total = lax.fori_loop(0, 16, backward, (zero, zero))
    pg_ref[...] = total

    def back_copy(d):
        to = peer(d)
        return send(back.at[to[1] // 2], ret.at[chip], b_send.at[d], b_recv.at[d], to)

    lax.fori_loop(1, 16, lambda d, _: (back_copy(d).start(), 0)[1], 0)
    ret[chip] = back[chip]

    lax.fori_loop(34, NBLK * PAIRS, unit, 0)
    for k in range(NBLK):
        keep = iota((BLOCK, BLOCK), 1) >= iota((BLOCK, BLOCK), 0)
        pt_ref[k] = jnp.where(keep, pt_v[k], 0.0).astype(BF16)
    store = pltpu.make_async_copy(dx_v, dx_hbm, load_sem.at[2])
    store.start()

    lax.fori_loop(1, 16, lambda d, _: (prompt_copy(d).wait(), 0)[1], 0)
    lax.fori_loop(1, 16, lambda d, _: (back_copy(d).wait(), 0)[1], 0)

    def finish(q, _):
        split = split_of(2 * q + core)
        t0, t1 = pick(coef_ref[q, core], sc[q])
        f0, _ = pick(f_ref[q, core], sf[q])
        _, r1 = pick(r_ref[q, core], sr[q])
        e0 = ret[q, 0:CHUNK, :]
        l1 = ret[q, CHUNK:, :]
        prompt = prompts[q]
        e1 = spread(t0, 0, split) * e0 + spread(t0, 1, split) * prompt + f0
        l0 = spread(t1, 2, split) * l1 + r1
        e_ref[q, core], sib_e[q] = pick(e0, e1)
        l_ref[q, core], sib_l[q] = pick(l0, l1)
        pr_ref[q, core] = prompt
        return 0

    lax.fori_loop(0, 16, finish, 0)
    last = [
        send(s, t.at[:, core], sib_send.at[4 + n], sib_recv.at[4 + n], sibling)
        for n, (s, t) in enumerate(((sib_e, e_ref), (sib_l, l_ref), (prompts, pr_ref)))
    ]
    for c in last:
        c.start()
    for c in last:
        c.wait()
    store.wait()


def carry(f, r, u, coef, p, x, g, b, c, la, w3, s2):
    v = pl.BlockSpec(memory_space=pltpu.VMEM)
    a = pl.BlockSpec(memory_space=pl.ANY)
    split = lambda s: s.reshape(16, 2, CHUNK, 128)
    st = jax.ShapeDtypeStruct((16, 2, CHUNK, 128), F32)
    half = pltpu.VMEM((16, CHUNK, 128), F32)
    dma = lambda n: pltpu.SemaphoreType.DMA((n,))
    return pl.pallas_call(
        carry_kernel,
        in_specs=[v] * 5 + [a, a] + [v] * 5,
        out_specs=[v] * 5 + [a],
        out_shape=[
            st, st, st, jax.ShapeDtypeStruct((CHUNK, 128), F32),
            jax.ShapeDtypeStruct((NBLK, BLOCK, BLOCK), BF16),
            jax.ShapeDtypeStruct((TOK, WIDTH), BF16),
        ],
        scratch_shapes=[
            pltpu.VMEM((TOK, WIDTH), BF16), pltpu.VMEM((TOK, WIDTH), BF16), pltpu.VMEM((TOK, WIDTH), BF16),
            pltpu.VMEM((BLOCK, BLOCK), F32), pltpu.VMEM((NBLK, BLOCK, BLOCK), F32),
            half, half, half, pltpu.VMEM((16, 8, 128), F32), half,
            pltpu.VMEM((16, MESSAGE, 128), F32), pltpu.VMEM((16, MESSAGE, 128), F32),
            pltpu.VMEM((16, 2 * CHUNK, 128), F32), pltpu.VMEM((16, 2 * CHUNK, 128), F32),
            half, half, half,
            dma(3), dma(7), dma(7), dma(16), dma(16), dma(16), dma(16), dma(16), dma(16),
        ],
        compiler_params=pltpu.CompilerParams(
            collective_id=0, has_side_effects=True, vmem_limit_bytes=VMEM_LIMIT
        ),
    )(split(f), split(r), split(u), coef.reshape(16, 2, 8, 128), p, x, g, b, c, la, w3, s2)


def gradient_kernel(
    lens_ref, x_ref, g_ref, dx_ref, e_ref, l_ref, p_ref, loc_ref,
    b_ref, c_ref, la_ref, s2_ref, x2_ref, g2_ref, pt_ref, out_ref, bc_ref, acc_ref,
):
    pair = pl.program_id(0)
    ns, nl = flags(lens_ref)

    @pl.when(pair == 0)
    def _():
        for k in range(NBLK):
            rows = slice(BLOCK * k, BLOCK * (k + 1))
            acc_ref[rows, :128] = dot(pt_ref[k], c_ref[rows, :])
            acc_ref[rows, 128:] = dot(pt_ref[k], b_ref[rows, :], TN)

    sel = selector(2 * pair, 2, 64, 128)
    wx = dot(x2_ref[...], sel)
    sx = (x_ref[...].astype(F32) * wx).astype(BF16)
    sg = (g_ref[...].astype(F32) * dot(g2_ref[...], sel)).astype(BF16)
    st = dot(s2_ref[...], sel)
    dec = pair_decays(la_ref, pair)
    prompt = p_ref[...]
    entering = []
    state = e_ref[...]
    for k in range(NBLK):
        state = state * ns[k] + prompt * (1.0 - ns[k])
        entering.append(state.astype(BF16))
        if k < NBLK - 1:
            state = dec[k] * state + loc_ref[k]
    leaving = [None] * NBLK
    state = l_ref[...]
    for k in reversed(range(NBLK)):
        state = state * nl[k]
        leaving[k] = state.astype(BF16)
        if k > 0:
            state = dec[k] * state + loc_ref[k + 1]
    for k in range(NBLK):
        rows = slice(BLOCK * k, BLOCK * (k + 1))
        outer = dot(b_ref[rows, :], leaving[k], NT)
        out_ref[rows, :] = (st[rows] * dx_ref[rows, :].astype(F32) + wx[rows] * outer).astype(BF16)
        acc_ref[rows, :128] += dot(sx[rows], leaving[k])
        acc_ref[rows, 128:] += dot(sg[rows], entering[k])

    @pl.when(pair == PAIRS - 1)
    def _():
        bc_ref[...] = acc_ref[...].astype(BF16)


def gradients(lens, x, g, dx, e, l, p, loc, b, c, la, s2, x2, g2, pt):
    whole = lambda *shape: pl.BlockSpec(shape, lambda i: (0,) * len(shape))
    lanes = pl.BlockSpec((TOK, 128), lambda i: (0, i))
    rows = pl.BlockSpec((128, 128), lambda i: (i, 0))
    flat = lambda s: s.reshape(WIDTH, STATE)
    cols = whole(TOK, 128)
    return pl.pallas_call(
        gradient_kernel,
        grid=(PAIRS,),
        in_specs=[
            pl.BlockSpec(memory_space=pltpu.SMEM), lanes, lanes, lanes, rows, rows, rows,
            pl.BlockSpec((4, 128, 128), lambda i: (0, i, 0)),
            cols, cols, whole(HEADS, TOK), cols, cols, cols, whole(NBLK, BLOCK, BLOCK),
        ],
        out_specs=[lanes, whole(TOK, 256)],
        out_shape=[
            jax.ShapeDtypeStruct((TOK, WIDTH), BF16), jax.ShapeDtypeStruct((TOK, 256), BF16)
        ],
        scratch_shapes=[pltpu.VMEM((TOK, 256), F32)],
        compiler_params=pltpu.CompilerParams(vmem_limit_bytes=VMEM_LIMIT),
    )(lens, x, g, dx, flat(e), flat(l), flat(p), loc, b, c, la, s2, x2, g2, pt)


SLABS = 8
SLAB = DMODEL // SLABS
ROWS = ((0, 16), (16, 32), (32, 40))


def weight_kernel(
    li_hbm, bc_ref, out_ref,
    li_v, part, sib, h,
    r1a, r1b, r1c, s1a, s1b, s1c, r2a, r2b, r2c, s2a, s2b, s2c, r3a, r3b, r3c,
    load_sem, sib_send, sib_recv, sends, recvs,
):
    x, seq = lax.axis_index("group"), lax.axis_index("seq")
    core = seq % 2
    y, z = seq // 8, (seq // 2) % 4
    sibling = (x, seq + 1 - 2 * core)

    def index(yy, zz):
        return (yy * 4 + zz) * 2 + core

    def to_x(d):
        return ((x + d) % 4, seq)

    def to_y(d):
        return (x, index((y + d) % 4, z))

    def to_z(d):
        return (x, index(y, (z + d) % 4))

    def load(m):
        return pltpu.make_async_copy(
            li_hbm.at[:, SLAB * m : SLAB * (m + 1)], li_v.at[m], load_sem.at[m]
        )

    for m in range(SLABS):
        load(m).start()
    barrier = pltpu.get_barrier_semaphore()
    targets = [sibling] + [to(d) for to in (to_x, to_y, to_z) for d in (1, 2, 3)]
    for t in targets:
        pl.semaphore_signal(barrier, inc=1, device_id=t, device_id_type=MESH)
    pl.semaphore_wait(barrier, len(targets))

    def sib_copy(m):
        return pltpu.make_async_remote_copy(
            src_ref=part.at[m, :, 1 - core], dst_ref=sib.at[m],
            send_sem=sib_send.at[m], recv_sem=sib_recv.at[m],
            device_id=sibling, device_id_type=MESH,
        )

    bc = bc_ref[...]
    for m in range(SLABS):
        load(m).wait()
        part[m] = dot(li_v[m], bc, TN).reshape(8, 2, 40, 256)
        sib_copy(m).start()
    for m in range(SLABS):
        sib_copy(m).wait()
        h[m // 2, 2 * (m % 2) : 2 * (m % 2) + 2] = (part[m, :, core] + sib[m]).reshape(2, 4, 40, 256)

    def copy(n, stage, d, src, dst, to):
        return pltpu.make_async_remote_copy(
            src_ref=src, dst_ref=dst, send_sem=sends.at[n, stage, d], recv_sem=recvs.at[n, stage, d],
            device_id=to, device_id_type=MESH,
        )

    me = lambda v, d: (v + d) % 4

    def first(n, d):
        lo, hi = ROWS[n]
        size = hi - lo
        rows = pl.ds(lo, size)
        if n == 0:
            return copy(n, 0, d, h.at[me(x, d), :, :, rows], r1a.at[d], to_x(d))
        if n == 1:
            return copy(n, 0, d, h.at[:, me(y, d), :, rows], r1b.at[d], to_y(d))
        return copy(n, 0, d, h.at[:, :, me(z, d), rows], r1c.at[d], to_z(d))

    def second(n, d):
        if n == 0:
            return copy(n, 1, d, s1a.at[me(y, d)], r2a.at[d], to_y(d))
        if n == 1:
            return copy(n, 1, d, s1b.at[:, me(z, d)], r2b.at[d], to_z(d))
        return copy(n, 1, d, s1c.at[me(x, d)], r2c.at[d], to_x(d))

    def third(n, d):
        if n == 0:
            return copy(n, 2, d, s2a.at[me(z, d)], r3a.at[d], to_z(d))
        if n == 1:
            return copy(n, 2, d, s2b.at[me(x, d)], r3b.at[d], to_x(d))
        return copy(n, 2, d, s2c.at[me(y, d)], r3c.at[d], to_y(d))

    each = [(n, d) for d in (1, 3, 2) for n in range(3)]
    for n, d in each:
        first(n, d).start()
    for n in range(3):
        for d in (1, 2, 3):
            first(n, d).wait()
        if n == 0:
            s1a[...] = h[x, :, :, 0:16] + r1a[1] + r1a[2] + r1a[3]
        elif n == 1:
            s1b[...] = h[:, y, :, 16:32] + r1b[1] + r1b[2] + r1b[3]
        else:
            s1c[...] = h[:, :, z, 32:40] + r1c[1] + r1c[2] + r1c[3]
        for d in (1, 3, 2):
            second(n, d).start()
    for n in range(3):
        for d in (1, 2, 3):
            second(n, d).wait()
        if n == 0:
            s2a[...] = s1a[y] + r2a[1] + r2a[2] + r2a[3]
        elif n == 1:
            s2b[...] = s1b[:, z] + r2b[1] + r2b[2] + r2b[3]
        else:
            s2c[...] = s1c[x] + r2c[1] + r2c[2] + r2c[3]
        for d in (1, 3, 2):
            third(n, d).start()
    for n, (mine, r, at) in enumerate(((s2a, r3a, z), (s2b, r3b, x), (s2c, r3c, y))):
        for d in (1, 2, 3):
            third(n, d).wait()
        out_ref[ROWS[n][0] : ROWS[n][1], :] = mine[at] + r[1] + r[2] + r[3]


def weight_gradient(li, bc):
    v = lambda *shape: pltpu.VMEM(shape, F32)
    dma = lambda *n: pltpu.SemaphoreType.DMA(n)
    return pl.pallas_call(
        weight_kernel,
        in_specs=[pl.BlockSpec(memory_space=pl.ANY), pl.BlockSpec(memory_space=pltpu.VMEM)],
        out_specs=pl.BlockSpec(memory_space=pltpu.VMEM),
        out_shape=jax.ShapeDtypeStruct((40, 256), F32),
        scratch_shapes=[
            pltpu.VMEM((SLABS, TOK, SLAB), BF16),
            v(SLABS, 8, 2, 40, 256), v(SLABS, 8, 40, 256), v(4, 4, 4, 40, 256),
            v(4, 4, 4, 16, 256), v(4, 4, 4, 16, 256), v(4, 4, 4, 8, 256),
            v(4, 4, 16, 256), v(4, 4, 16, 256), v(4, 4, 8, 256),
            v(4, 4, 16, 256), v(4, 4, 16, 256), v(4, 4, 8, 256),
            v(4, 16, 256), v(4, 16, 256), v(4, 8, 256),
            v(4, 16, 256), v(4, 16, 256), v(4, 8, 256),
            dma(SLABS), dma(SLABS), dma(SLABS), dma(3, 3, 4), dma(3, 3, 4),
        ],
        compiler_params=pltpu.CompilerParams(
            collective_id=1, has_side_effects=True, vmem_limit_bytes=VMEM_LIMIT
        ),
    )(li, bc)


def body(li, x, g, b, c, step, rates, prompt, lens):
    li, x, g, b, c, step, prompt = li[0], x[0], g[0], b[0], c[0], step[0], prompt[0]
    f, r, u, loc, coef, la, w3, s2, x2, g2 = summarize(lens, step, rates.reshape(HEADS, 1), x, g, b, c)
    e, l, p, prompt_grad, pt, dx = carry(f, r, u, coef, prompt, x, g, b, c, la, w3, s2)
    x_grad, bc = gradients(lens, x, g, dx, e, l, p, loc, b, c, la, s2, x2, g2, pt)
    weight_grad = weight_gradient(li, bc)
    return x_grad[None], prompt_grad[None], weight_grad


def solution(mesh):
    in_specs = (
        P("group", "seq", None),
        P("group", "seq", None),
        P("group", "seq", None),
        P("group", "seq", None),
        P("group", "seq", None),
        P("group", None, "seq"),
        P(),
        P("group", "seq", None),
        P("group", None),
    )
    out_specs = (P("group", "seq", None), P("group", "seq", None), P(("group", "seq"), None))
    return jax.shard_map(body, mesh=mesh, in_specs=in_specs, out_specs=out_specs, check_vma=False)
```

```python
from functools import partial

import jax
import jax.numpy as jnp
from jax import lax
from jax.experimental import pallas as pl
from jax.experimental.pallas import tpu as pltpu
from jax.sharding import PartitionSpec as P

BLOCK = 256
NBLK = 3
TOK = BLOCK * NBLK
HEADS = 40
STATE = 128
WIDTH = 2560
DMODEL = 5120
PHASES = 5
PHEADS = HEADS // PHASES
PLANES = PHEADS * 64
PPAIRS = PHEADS // 2
PUNITS = NBLK * PPAIRS
F32 = jnp.float32
BF16 = jnp.bfloat16
MESH = pl.DeviceIdType.MESH
NN = (((1,), (0,)), ((), ()))
TN = (((0,), (0,)), ((), ()))
NT = (((1,), (1,)), ((), ()))
LOG2E = 1.4426950408889634
VMEM_LIMIT = 60 * 1024 * 1024


def dot(a, b, dims=NN):
    return lax.dot_general(a, b, dims, preferred_element_type=F32)


def iota(shape, dim):
    return lax.broadcasted_iota(jnp.int32, shape, dim)


def flags(lens_ref):
    first = lax.axis_index("seq") * NBLK
    e1 = lens_ref[0, 0]
    e2 = e1 + lens_ref[0, 1]
    e3 = e2 + lens_ref[0, 2]
    e4 = e3 + lens_ref[0, 3]
    not_start, not_last = [], []
    for k in range(NBLK):
        at = first + k
        start = (at == 0) | (at == e1) | (at == e2) | (at == e3)
        last = (at == e1 - 1) | (at == e2 - 1) | (at == e3 - 1) | (at == e4 - 1)
        not_start.append(jnp.where(start, 0.0, 1.0).astype(F32))
        not_last.append(jnp.where(last, 0.0, 1.0).astype(F32))
    return not_start, not_last


def blockrows(k):
    return slice(BLOCK * k, BLOCK * (k + 1))


def gather(table, index):
    return jnp.take_along_axis(table, index, axis=1)


def half_heads(pair, rows):
    return 2 * pair + iota((rows, 128), 1) // 64


def prepare(step_ref, rate_ref, b_ref, c_ref, la_v, t1_v, t2_v, inner_v, pt_v, acc_v):
    step = step_ref[...]
    same = iota((HEADS, HEADS), 0) == iota((HEADS, HEADS), 1)
    spread = jnp.broadcast_to(rate_ref[...], (HEADS, HEADS))
    rate = jnp.sum(jnp.where(same, spread, 0.0), axis=1, keepdims=True)
    la = -step * rate
    place = iota((HEADS, TOK), 1) % BLOCK
    shift = 1
    while shift < BLOCK:
        la = la + jnp.where(place >= shift, pltpu.roll(la, shift, 1), 0.0)
        shift *= 2
    la = la * LOG2E
    la_v[...] = la
    ends = [la[:, BLOCK * (k + 1) - 1 : BLOCK * (k + 1)] for k in range(NBLK)]
    end = jnp.concatenate([jnp.broadcast_to(e, (HEADS, BLOCK)) for e in ends], axis=1)
    empty = jnp.zeros((8, TOK), F32)
    t1_v[...] = jnp.concatenate([la, step, jnp.exp2(end - la) * step, empty], axis=0).T
    t2_v[...] = jnp.concatenate([jnp.exp2(la), jnp.zeros((88, TOK), F32)], axis=0).T
    keep = iota((BLOCK, BLOCK), 1) >= iota((BLOCK, BLOCK), 0)
    for k in range(NBLK):
        inner_v[k] = jnp.where(keep, dot(b_ref[blockrows(k), :], c_ref[blockrows(k), :], NT), 0.0)
        pt_v[k] = jnp.zeros((BLOCK, BLOCK), F32)
    acc_v[...] = jnp.zeros_like(acc_v)


def phase_decays(la_v, j):
    la = la_v[pl.ds(pl.multiple_of(PHEADS * j, PHEADS), PHEADS), :]
    out = []
    for k in range(NBLK):
        at = BLOCK * (k + 1) - 1
        out.append(jnp.broadcast_to(jnp.exp2(la[:, at : at + 1]), (PHEADS, 128))[:, None, :])
    return out


def summarize(j, ns, nl, x_v, g_v, b_ref, c_ref, la_v, t1_v, t2_v, sx_v, sg_v, loc_v, mine):
    ls, lg = [], []
    for k in range(NBLK):
        rows = blockrows(k)
        sx, sg = [], []
        for p in range(PPAIRS):
            lanes = pl.ds(pl.multiple_of(PLANES * j + 128 * p, 128), 128)
            heads = half_heads(PPAIRS * j + p, BLOCK)
            sx.append((x_v[rows, lanes].astype(F32) * gather(t1_v[rows, :], heads + 2 * HEADS)).astype(BF16))
            sg.append((g_v[rows, lanes].astype(F32) * gather(t2_v[rows, :], heads)).astype(BF16))
            sx_v[rows, lanes] = sx[p]
            sg_v[rows, lanes] = sg[p]
        ls.append(dot(jnp.concatenate(sx, axis=1), b_ref[rows, :], TN).reshape(PHEADS, 64, 128))
        lg.append(dot(jnp.concatenate(sg, axis=1), c_ref[rows, :], TN).reshape(PHEADS, 64, 128))
    for n, value in enumerate((ls[0], ls[1], lg[0], lg[1], lg[2])):
        loc_v[j, n] = value
    dec = phase_decays(la_v, j)
    f = ls[0]
    for k in range(1, NBLK):
        f = (dec[k] * ns[k]) * f + ls[k]
    r = lg[2]
    for k in (1, 0):
        r = (dec[k] * nl[k]) * r + lg[k]
    mine[j, :, :, 0:16, :] = f.reshape(16, 2, 16, 128)
    mine[j, :, :, 16:32, :] = r.reshape(16, 2, 16, 128)
    af = ab = jnp.ones((PHEADS, 1, 128), F32)
    pc = jnp.zeros((PHEADS, 1, 128), F32)
    for k in range(NBLK):
        af = af * (dec[k] * ns[k])
        pc = dec[k] * (pc * ns[k] + (1.0 - ns[k]))
        ab = ab * (dec[k] * nl[k])
    empty = jnp.zeros((5, 128), F32)
    for h in range(PHEADS):
        tile = jnp.concatenate([af[h], pc[h], ab[h], empty], axis=0)
        for q in (2 * h, 2 * h + 1):
            for c in range(2):
                mine[j, q, c, 32:40, :] = tile


def inside_unit(u, x_v, g_v, la_v, t1_v, inner_v, pt_v, dx_v):
    j, v = u // PUNITS, u % PUNITS
    k, pair = v // PPAIRS, PPAIRS * j + v % PPAIRS
    r = pl.ds(pl.multiple_of(k * BLOCK, BLOCK), BLOCK)
    l = pl.ds(pl.multiple_of(pair * 128, 128), 128)
    g = g_v[r, l]
    table = t1_v[r, :]
    xs = (x_v[r, l].astype(F32) * gather(table, half_heads(pair, BLOCK) + HEADS)).astype(BF16)
    lane = iota((1, 128), 1)
    masks = [jnp.where((lane >= 64) == bool(n), 1.0, 0.0).astype(BF16) for n in range(2)]
    gs = [g * m for m in masks]
    low = jnp.concatenate([gs[0][128:], gs[1][128:]], axis=0)
    p0 = dot(jnp.concatenate([xs[:128] * masks[0], xs[:128] * masks[1]], axis=0), g, NT)
    p1 = dot(xs[128:], low, NT)
    a00, a01, a11, w11, d0 = [], [], [], [], []
    for n in range(2):
        row = la_v[pl.ds(2 * pair + n, 1), r]
        col = gather(table, jnp.full((BLOCK, 128), 2 * pair + n, jnp.int32))
        pn = p0[128 * n : 128 * (n + 1)]
        q00 = jnp.exp2(jnp.minimum(row[:, :128] - col[:128], 0.0))
        q01 = jnp.exp2(jnp.minimum(row[:, 128:] - col[:128], 0.0))
        q11 = jnp.exp2(jnp.minimum(row[:, 128:] - col[128:], 0.0))
        a00.append(q00 * pn[:, :128])
        a01.append(q01 * pn[:, 128:])
        a11.append(q11 * p1[:, 128 * n : 128 * (n + 1)])
        w00 = (q00 * inner_v[k, :128, :128]).astype(BF16)
        w01 = (q01 * inner_v[k, :128, 128:]).astype(BF16)
        w11.append((q11 * inner_v[k, 128:, 128:]).astype(BF16))
        d0.append(dot(jnp.concatenate([w00, w01], axis=1), gs[n]))
    pt_v[k, :128, :128] += a00[0] + a00[1]
    pt_v[k, :128, 128:] += a01[0] + a01[1]
    pt_v[k, 128:, 128:] += a11[0] + a11[1]
    d1 = dot(jnp.concatenate(w11, axis=1), low)
    dx_v[r, l] = jnp.concatenate([d0[0] + d0[1], d1], axis=0).astype(BF16)


def gradients(j, ns, nl, b_ref, la_v, t1_v, sx_v, sg_v, loc_v, prompt, el_v, dx_v, acc_v, pterm_ref):
    dec = phase_decays(la_v, j)
    el = el_v[j]
    shape = (PHEADS, 64, 128)
    prompt = prompt.reshape(shape)
    state = el[:, :, 0:16].reshape(shape)
    entering = []
    for k in range(NBLK):
        state = state * ns[k] + prompt * (1.0 - ns[k])
        entering.append(state.reshape(PLANES, 128).astype(BF16))
        if k < NBLK - 1:
            state = dec[k] * state + loc_v[j, k]
    state = el[:, :, 16:32].reshape(shape)
    leaving = [None] * NBLK
    total = None
    for k in reversed(range(NBLK)):
        state = state * nl[k]
        leaving[k] = state.reshape(PLANES, 128).astype(BF16)
        state = dec[k] * state + loc_v[j, 2 + k]
        at_start = state * (1.0 - ns[k])
        total = at_start if total is None else total + at_start
    pterm_ref[j] = total
    lanes = pl.ds(pl.multiple_of(PLANES * j, PLANES), PLANES)
    for k in range(NBLK):
        rows = blockrows(k)
        outer = dot(b_ref[rows, :], leaving[k], NT)
        table = t1_v[rows, :]
        for p in range(PPAIRS):
            at = pl.ds(pl.multiple_of(PLANES * j + 128 * p, 128), 128)
            heads = half_heads(PPAIRS * j + p, BLOCK)
            near = gather(table, heads + HEADS) * dx_v[rows, at].astype(F32)
            far = gather(table, heads + 2 * HEADS) * outer[:, 128 * p : 128 * (p + 1)]
            dx_v[rows, at] = (near + far).astype(BF16)
        acc_v[rows, :128] += dot(sx_v[rows, lanes], leaving[k])
        acc_v[rows, 128:] += dot(sg_v[rows, lanes], entering[k])


TICKS = PHASES + 6
STEP_UNITS = 3


def scan_kernel(
    lens_ref, step_ref, rate_ref, x_hbm, g_hbm, b_ref, c_ref, p_ref,
    xg_hbm, bc_ref, pterm_ref,
    x_v, g_v, dx_v, sx_v, sg_v, la_v, t1_v, t2_v, inner_v, pt_v, acc_v, loc_v,
    mine, sib_in, comb, got, back, ret, sib_out, el_v, prompts,
    x_sem, g_sem, o_sem, f_send, f_recv, l_send, l_recv, p_send, p_recv, a_send, a_recv, b_send, b_recv,
):
    group, seq = lax.axis_index("group"), lax.axis_index("seq")
    core = seq % 2
    chip = seq // 2
    y, z = chip // 4, chip % 4
    sibling = (group, chip * 2 + (1 - core))
    is0 = core == 0

    def chip_at(d):
        return ((y + d // 4) % 4) * 4 + (z + d % 4) % 4

    def send(src, dst, s, r, to):
        return pltpu.make_async_remote_copy(
            src_ref=src, dst_ref=dst, send_sem=s, recv_sem=r, device_id=to, device_id_type=MESH
        )

    def lanes(j):
        return pl.ds(pl.multiple_of(PLANES * j, PLANES), PLANES)

    def load_x(j):
        return pltpu.make_async_copy(x_hbm.at[:, lanes(j)], x_v.at[:, lanes(j)], x_sem.at[j])

    def load_g(j):
        return pltpu.make_async_copy(g_hbm.at[:, lanes(j)], g_v.at[:, lanes(j)], g_sem.at[j])

    def store(j):
        return pltpu.make_async_copy(dx_v.at[:, lanes(j)], xg_hbm.at[:, lanes(j)], o_sem.at[j])

    def each(lo, hi, f):
        def step(i, _):
            f(i)
            return 0

        lax.fori_loop(lo, hi, step, 0)

    def begin(j):
        load_x(j).start()
        load_g(j).start()

    each(0, PHASES, begin)

    barrier = pltpu.get_barrier_semaphore()
    pl.semaphore_signal(barrier, inc=1, device_id=sibling, device_id_type=MESH)
    each(1, 16, lambda d: pl.semaphore_signal(
        barrier, inc=1, device_id=(group, chip_at(d) * 2 + core), device_id_type=MESH
    ))
    pl.semaphore_wait(barrier, 16)

    def prompt_copy(d):
        return send(p_ref, prompts.at[chip, core], p_send.at[d], p_recv.at[d], (group, chip_at(d) * 2 + core))

    def prompt_pass():
        half = prompts.at[:, core]
        return send(half, half, p_send.at[0], p_recv.at[0], sibling)

    def chip_copy(j):
        return send(mine.at[j, :, 1 - core], sib_in.at[j], f_send.at[j], f_recv.at[j], sibling)

    def out_copy(j, d):
        to = chip_at(d)
        return send(comb.at[j, to], got.at[j, d], a_send.at[j, d], a_recv.at[j, d], (group, to * 2 + core))

    def back_copy(j, d):
        to = chip_at(d)
        return send(back.at[j, to], ret.at[j, chip], b_send.at[j, d], b_recv.at[j, d], (group, to * 2 + core))

    def last_copy(j):
        return send(sib_out.at[j], el_v.at[j, :, core], l_send.at[j], l_recv.at[j], sibling)

    each(1, 16, lambda d: prompt_copy(d).start())
    prompts[chip, core] = p_ref[...]

    prepare(step_ref, rate_ref, b_ref, c_ref, la_v, t1_v, t2_v, inner_v, pt_v, acc_v)
    ns, nl = flags(lens_ref)

    def pick(a, b):
        return jnp.where(is0, a, b), jnp.where(is0, b, a)

    def both(j):
        return pick(mine[j, :, core], sib_in[j])

    def combine(j):
        a, b = both(j)
        af0, pc0, ab0 = a[:, 32:33], a[:, 33:34], a[:, 34:35]
        af1, pc1, ab1 = b[:, 32:33], b[:, 33:34], b[:, 34:35]
        comb[j, :, 0:16, :] = b[:, 0:16] + af1 * a[:, 0:16]
        comb[j, :, 16:32, :] = a[:, 16:32] + ab0 * b[:, 16:32]
        comb[j, :, 32:40, :] = jnp.concatenate(
            [af0 * af1, pc1 + af1 * pc0, ab0 * ab1, jnp.zeros((16, 5, 128), F32)], axis=1
        )

    def prompt_rows(j, owner):
        at = 32 * j + owner
        return prompts[at // 10, (at // 5) % 2, pl.ds(pl.multiple_of(16 * (at % 5), 16), 16), :]

    def slot(q):
        return ((y + 4 - q // 4) % 4) * 4 + (z + 4 - q % 4) % 4

    def scan(j):
        own = prompt_rows(j, seq)
        e = jnp.zeros((16, 128), F32)
        for q in range(16):
            s = slot(q)
            back[j, q, 0:16, :] = e
            e = got[j, s, 32:33, :] * e + (got[j, s, 33:34, :] * own + got[j, s, 0:16, :])
        lv = jnp.zeros((16, 128), F32)
        for q in reversed(range(16)):
            s = slot(q)
            back[j, q, 16:32, :] = lv
            lv = got[j, s, 34:35, :] * lv + got[j, s, 16:32, :]

    def finish(j):
        a, b = both(j)
        e0, l1 = ret[j, :, 0:16, :], ret[j, :, 16:32, :]
        prompt = jnp.stack([prompt_rows(j, 2 * q + core) for q in range(16)], axis=0)
        e1 = a[:, 32:33] * e0 + (a[:, 33:34] * prompt + a[:, 0:16])
        l0 = b[:, 34:35] * l1 + b[:, 16:32]
        e_mine, e_other = pick(e0, e1)
        l_mine, l_other = pick(l0, l1)
        el_v[j, :, core, 0:16, :] = e_mine
        el_v[j, :, core, 16:32, :] = l_mine
        sib_out[j, :, 0:16, :] = e_other
        sib_out[j, :, 16:32, :] = l_other

    def units(lo):
        each(lo, lo + STEP_UNITS, lambda u: inside_unit(
            u, x_v, g_v, la_v, t1_v, inner_v, pt_v, dx_v
        ))

    def tick(t):
        @pl.when(t < PHASES)
        def _():
            load_x(t).wait()
            load_g(t).wait()
            summarize(t, ns, nl, x_v, g_v, b_ref, c_ref, la_v, t1_v, t2_v, sx_v, sg_v, loc_v, mine)
            chip_copy(t).start()

        @pl.when(t == 0)
        def _():
            each(1, 16, lambda d: prompt_copy(d).wait())
            prompt_pass().start()

        @pl.when((t >= 1) & (t < PHASES + 1))
        def _():
            j = t - 1
            chip_copy(j).wait()
            combine(j)
            each(1, 16, lambda d: out_copy(j, d).start())
            got[j, 0] = comb[j, chip]

        @pl.when(t < 10)
        def _():
            units(2 * STEP_UNITS * t)

        @pl.when(t == 2)
        def _():
            prompt_pass().wait()

        @pl.when((t >= 3) & (t < PHASES + 3))
        def _():
            j = t - 3
            each(1, 16, lambda d: out_copy(j, d).wait())
            scan(j)
            each(1, 16, lambda d: back_copy(j, d).start())
            ret[j, chip] = back[j, chip]

        @pl.when(t < 10)
        def _():
            units(2 * STEP_UNITS * t + STEP_UNITS)

        @pl.when((t >= 5) & (t < PHASES + 5))
        def _():
            j = t - 5
            each(1, 16, lambda d: back_copy(j, d).wait())
            finish(j)
            last_copy(j).start()

        @pl.when(t >= 6)
        def _():
            j = t - 6
            last_copy(j).wait()
            prompt = jnp.stack([prompt_rows(j, o) for o in range(32)], axis=0)
            gradients(j, ns, nl, b_ref, la_v, t1_v, sx_v, sg_v, loc_v, prompt, el_v, dx_v, acc_v, pterm_ref)
            store(j).start()

    each(0, TICKS, tick)

    keep = iota((BLOCK, BLOCK), 1) >= iota((BLOCK, BLOCK), 0)
    for k in range(NBLK):
        rows = blockrows(k)
        pt = jnp.where(keep, pt_v[k], 0.0).astype(BF16)
        bc_ref[rows, :128] = (acc_v[rows, :128] + dot(pt, c_ref[rows, :])).astype(BF16)
        bc_ref[rows, 128:] = (acc_v[rows, 128:] + dot(pt, b_ref[rows, :], TN)).astype(BF16)
    each(0, PHASES, lambda j: store(j).wait())


def scans(lens, step, rates, x, g, b, c, p):
    v = pl.BlockSpec(memory_space=pltpu.VMEM)
    a = pl.BlockSpec(memory_space=pl.ANY)
    wide = pltpu.VMEM((TOK, WIDTH), BF16)
    square = pltpu.VMEM((NBLK, BLOCK, BLOCK), F32)
    f = lambda *shape: pltpu.VMEM(shape, F32)
    dma = lambda *n: pltpu.SemaphoreType.DMA(n)
    return pl.pallas_call(
        scan_kernel,
        in_specs=[pl.BlockSpec(memory_space=pltpu.SMEM), v, v, a, a, v, v, v],
        out_specs=[a, v, v],
        out_shape=[
            jax.ShapeDtypeStruct((TOK, WIDTH), BF16),
            jax.ShapeDtypeStruct((TOK, 256), BF16),
            jax.ShapeDtypeStruct((PHASES, PHEADS, 64, 128), F32),
        ],
        scratch_shapes=[
            wide, wide, wide, wide, wide,
            f(HEADS, TOK), f(TOK, 128), f(TOK, 128), square, square, f(TOK, 256),
            f(PHASES, 5, PHEADS, 64, 128),
            f(PHASES, 16, 2, 40, 128), f(PHASES, 16, 40, 128), f(PHASES, 16, 40, 128), f(PHASES, 16, 40, 128),
            f(PHASES, 16, 32, 128), f(PHASES, 16, 32, 128), f(PHASES, 16, 32, 128),
            f(PHASES, 16, 2, 32, 128), f(16, 2, 80, 128),
            dma(PHASES), dma(PHASES), dma(PHASES), dma(PHASES), dma(PHASES), dma(PHASES), dma(PHASES),
            dma(16), dma(16), dma(PHASES, 16), dma(PHASES, 16), dma(PHASES, 16), dma(PHASES, 16),
        ],
        compiler_params=pltpu.CompilerParams(
            collective_id=0, has_side_effects=True, vmem_limit_bytes=VMEM_LIMIT
        ),
    )(lens, step, rates, x, g, b, c, p)


SLABS = 8
SLAB = DMODEL // SLABS
ROWS = ((0, 16), (16, 40), (16, 40))
COLS = ((0, 256), (0, 128), (128, 256))


def weight_kernel(
    li_hbm, bc_ref, pt_ref, out_ref, pg_ref,
    li_v, part, sib, h, sib_p, hp, pr1a, pr1b, ps1a, ps1b, pr2a, pr2b,
    r1a, r1b, r1c, s1a, s1b, s1c, r2a, r2b, r2c, s2a, s2b, s2c, r3a, r3b, r3c,
    load_sem, sib_send, sib_recv, sends, recvs, p_sends, p_recvs,
):
    x, seq = lax.axis_index("group"), lax.axis_index("seq")
    core = seq % 2
    y, z = seq // 8, (seq // 2) % 4
    sibling = (x, seq + 1 - 2 * core)

    def index(yy, zz):
        return (yy * 4 + zz) * 2 + core

    def to_x(d):
        return ((x + d) % 4, seq)

    def to_y(d):
        return (x, index((y + d) % 4, z))

    def to_z(d):
        return (x, index(y, (z + d) % 4))

    def load(m):
        return pltpu.make_async_copy(
            li_hbm.at[:, SLAB * m : SLAB * (m + 1)], li_v.at[m], load_sem.at[m]
        )

    for m in range(SLABS):
        load(m).start()
    barrier = pltpu.get_barrier_semaphore()
    targets = [sibling] + [to(d) for to in (to_x, to_y, to_z) for d in (1, 2, 3)]
    for t in targets:
        pl.semaphore_signal(barrier, inc=1, device_id=t, device_id_type=MESH)
    pl.semaphore_wait(barrier, len(targets))

    def sib_copy(m):
        return pltpu.make_async_remote_copy(
            src_ref=part.at[m, :, 1 - core], dst_ref=sib.at[m],
            send_sem=sib_send.at[m], recv_sem=sib_recv.at[m],
            device_id=sibling, device_id_type=MESH,
        )

    def p_copy(n, stage, d, src, dst, to):
        return pltpu.make_async_remote_copy(
            src_ref=src, dst_ref=dst, send_sem=p_sends.at[n, stage, d], recv_sem=p_recvs.at[n, stage, d],
            device_id=to, device_id_type=MESH,
        )

    def p_first(n, d):
        if n == 0:
            return p_copy(n, 0, d, hp.at[(y + d) % 4, :, 0:40], pr1a.at[d], to_y(d))
        return p_copy(n, 0, d, hp.at[:, (z + d) % 4, 40:80], pr1b.at[d], to_z(d))

    def p_second(n, d):
        if n == 0:
            return p_copy(n, 1, d, ps1a.at[(z + d) % 4], pr2a.at[d], to_z(d))
        return p_copy(n, 1, d, ps1b.at[(y + d) % 4], pr2b.at[d], to_y(d))

    p_sib = p_copy(0, 0, 0, pt_ref.at[:, :, 1 - core], sib_p, sibling)
    p_sib.start()

    bc = bc_ref[...]
    for m in range(SLABS):
        load(m).wait()
        part[m] = dot(li_v[m], bc, TN).reshape(8, 2, 40, 256)
        sib_copy(m).start()
        if m == 1:
            p_sib.wait()
            hp[...] = pt_ref[:, :, core] + sib_p[...]
            for d in (1, 3, 2):
                for n in range(2):
                    p_first(n, d).start()
        if m == 6:
            for n in range(2):
                for d in (1, 2, 3):
                    p_first(n, d).wait()
            ps1a[...] = hp[y, :, 0:40] + pr1a[1] + pr1a[2] + pr1a[3]
            ps1b[...] = hp[:, z, 40:80] + pr1b[1] + pr1b[2] + pr1b[3]
            for d in (1, 3, 2):
                for n in range(2):
                    p_second(n, d).start()
    for m in range(SLABS):
        sib_copy(m).wait()
        h[m // 2, 2 * (m % 2) : 2 * (m % 2) + 2] = (part[m, :, core] + sib[m]).reshape(2, 4, 40, 256)

    def copy(n, stage, d, src, dst, to):
        return pltpu.make_async_remote_copy(
            src_ref=src, dst_ref=dst, send_sem=sends.at[n, stage, d], recv_sem=recvs.at[n, stage, d],
            device_id=to, device_id_type=MESH,
        )

    me = lambda v, d: (v + d) % 4

    def first(n, d):
        lo, hi = ROWS[n]
        size = hi - lo
        rows, cols = pl.ds(lo, size), pl.ds(COLS[n][0], COLS[n][1] - COLS[n][0])
        if n == 0:
            return copy(n, 0, d, h.at[me(x, d), :, :, rows, cols], r1a.at[d], to_x(d))
        if n == 1:
            return copy(n, 0, d, h.at[:, me(y, d), :, rows, cols], r1b.at[d], to_y(d))
        return copy(n, 0, d, h.at[:, :, me(z, d), rows, cols], r1c.at[d], to_z(d))

    def second(n, d):
        if n == 0:
            return copy(n, 1, d, s1a.at[me(y, d)], r2a.at[d], to_y(d))
        if n == 1:
            return copy(n, 1, d, s1b.at[:, me(z, d)], r2b.at[d], to_z(d))
        return copy(n, 1, d, s1c.at[me(x, d)], r2c.at[d], to_x(d))

    def third(n, d):
        if n == 0:
            return copy(n, 2, d, s2a.at[me(z, d)], r3a.at[d], to_z(d))
        if n == 1:
            return copy(n, 2, d, s2b.at[me(x, d)], r3b.at[d], to_x(d))
        return copy(n, 2, d, s2c.at[me(y, d)], r3c.at[d], to_y(d))

    for n in range(2):
        for d in (1, 2, 3):
            p_second(n, d).wait()
    pg_ref[0:40, :] = ps1a[z] + pr2a[1] + pr2a[2] + pr2a[3]
    pg_ref[40:80, :] = ps1b[y] + pr2b[1] + pr2b[2] + pr2b[3]

    each = [(n, d) for d in (1, 3, 2) for n in range(3)]
    for n, d in each:
        first(n, d).start()
    for n in range(3):
        for d in (1, 2, 3):
            first(n, d).wait()
        if n == 0:
            s1a[...] = h[x, :, :, 0:16] + r1a[1] + r1a[2] + r1a[3]
        elif n == 1:
            s1b[...] = h[:, y, :, 16:40, 0:128] + r1b[1] + r1b[2] + r1b[3]
        else:
            s1c[...] = h[:, :, z, 16:40, 128:256] + r1c[1] + r1c[2] + r1c[3]
        for d in (1, 3, 2):
            second(n, d).start()
    for n in range(3):
        for d in (1, 2, 3):
            second(n, d).wait()
        if n == 0:
            s2a[...] = s1a[y] + r2a[1] + r2a[2] + r2a[3]
        elif n == 1:
            s2b[...] = s1b[:, z] + r2b[1] + r2b[2] + r2b[3]
        else:
            s2c[...] = s1c[x] + r2c[1] + r2c[2] + r2c[3]
        for d in (1, 3, 2):
            third(n, d).start()
    for n, (mine, r, at) in enumerate(((s2a, r3a, z), (s2b, r3b, x), (s2c, r3c, y))):
        for d in (1, 2, 3):
            third(n, d).wait()
        out_ref[ROWS[n][0] : ROWS[n][1], COLS[n][0] : COLS[n][1]] = mine[at] + r[1] + r[2] + r[3]


def weight_gradient(li, bc, pterm):
    v = lambda *shape: pltpu.VMEM(shape, F32)
    dma = lambda *n: pltpu.SemaphoreType.DMA(n)
    here = pl.BlockSpec(memory_space=pltpu.VMEM)
    return pl.pallas_call(
        weight_kernel,
        in_specs=[pl.BlockSpec(memory_space=pl.ANY), here, here],
        out_specs=[here, here],
        out_shape=[jax.ShapeDtypeStruct((40, 256), F32), jax.ShapeDtypeStruct((80, 128), F32)],
        scratch_shapes=[
            pltpu.VMEM((SLABS, TOK, SLAB), BF16),
            v(SLABS, 8, 2, 40, 256), v(SLABS, 8, 40, 256), v(4, 4, 4, 40, 256),
            v(4, 4, 80, 128), v(4, 4, 80, 128), v(4, 4, 40, 128), v(4, 4, 40, 128),
            v(4, 40, 128), v(4, 40, 128), v(4, 40, 128), v(4, 40, 128),
            v(4, 4, 4, 16, 256), v(4, 4, 4, 24, 128), v(4, 4, 4, 24, 128),
            v(4, 4, 16, 256), v(4, 4, 24, 128), v(4, 4, 24, 128),
            v(4, 4, 16, 256), v(4, 4, 24, 128), v(4, 4, 24, 128),
            v(4, 16, 256), v(4, 24, 128), v(4, 24, 128),
            v(4, 16, 256), v(4, 24, 128), v(4, 24, 128),
            dma(SLABS), dma(SLABS), dma(SLABS), dma(3, 3, 4), dma(3, 3, 4), dma(2, 2, 4), dma(2, 2, 4),
        ],
        compiler_params=pltpu.CompilerParams(
            collective_id=1, has_side_effects=True, vmem_limit_bytes=VMEM_LIMIT
        ),
    )(li, bc, pterm)


def body(li, x, g, b, c, step, rates, prompt, lens):
    li, x, g, b, c, step, prompt = li[0], x[0], g[0], b[0], c[0], step[0], prompt[0]
    x_grad, bc, pterm = scans(lens, step, rates.reshape(1, HEADS), x, g, b, c, prompt)
    weight_grad, prompt_grad = weight_gradient(li, bc, pterm.reshape(4, 4, 2, 80, 128))
    return x_grad[None], prompt_grad[None], weight_grad


def solution(mesh):
    in_specs = (
        P("group", "seq", None),
        P("group", "seq", None),
        P("group", "seq", None),
        P("group", "seq", None),
        P("group", "seq", None),
        P("group", None, "seq"),
        P(),
        P("group", "seq", None),
        P("group", None),
    )
    out_specs = (P("group", "seq", None), P("group", "seq", None), P(("group", "seq"), None))
    return jax.shard_map(body, mesh=mesh, in_specs=in_specs, out_specs=out_specs, check_vma=False)
```

```python
from functools import partial

import jax
import jax.numpy as jnp
from jax import lax
from jax.experimental import pallas as pl
from jax.experimental.pallas import tpu as pltpu
from jax.sharding import PartitionSpec as P

BLOCK = 256
NBLK = 3
TOK = BLOCK * NBLK
HEADS = 40
STATE = 128
WIDTH = 2560
DMODEL = 5120
PHASES = 5
PHEADS = HEADS // PHASES
PLANES = PHEADS * 64
PPAIRS = PHEADS // 2
ROWS = ((0, 16), (16, 40), (16, 40))
COLS = ((0, 256), (0, 128), (128, 256))
SLAB = 640
F32 = jnp.float32
BF16 = jnp.bfloat16
MESH = pl.DeviceIdType.MESH
NN = (((1,), (0,)), ((), ()))
TN = (((0,), (0,)), ((), ()))
NT = (((1,), (1,)), ((), ()))
LOG2E = 1.4426950408889634
VMEM_LIMIT = 62 * 1024 * 1024


def dot(a, b, dims=NN):
    return lax.dot_general(a, b, dims, preferred_element_type=F32)


def iota(shape, dim):
    return lax.broadcasted_iota(jnp.int32, shape, dim)


def flags(lens_ref):
    first = lax.axis_index("seq") * NBLK
    e1 = lens_ref[0, 0]
    e2 = e1 + lens_ref[0, 1]
    e3 = e2 + lens_ref[0, 2]
    e4 = e3 + lens_ref[0, 3]
    not_start, not_last = [], []
    for k in range(NBLK):
        at = first + k
        start = (at == 0) | (at == e1) | (at == e2) | (at == e3)
        last = (at == e1 - 1) | (at == e2 - 1) | (at == e3 - 1) | (at == e4 - 1)
        not_start.append(jnp.where(start, 0.0, 1.0).astype(F32))
        not_last.append(jnp.where(last, 0.0, 1.0).astype(F32))
    return not_start, not_last


def blockrows(k):
    return slice(BLOCK * k, BLOCK * (k + 1))


def gather(table, index):
    return jnp.take_along_axis(table, index, axis=1)


def half_heads(pair, rows):
    return 2 * pair + iota((rows, 128), 1) // 64


def prepare(step_ref, rate_ref, la_v, t1_v, t2_v):
    step = step_ref[...]
    same = iota((HEADS, HEADS), 0) == iota((HEADS, HEADS), 1)
    spread = jnp.broadcast_to(rate_ref[...], (HEADS, HEADS))
    rate = jnp.sum(jnp.where(same, spread, 0.0), axis=1, keepdims=True)
    la = -step * rate
    place = iota((HEADS, TOK), 1) % BLOCK
    shift = 1
    while shift < BLOCK:
        la = la + jnp.where(place >= shift, pltpu.roll(la, shift, 1), 0.0)
        shift *= 2
    la = la * LOG2E
    la_v[...] = la
    ends = [la[:, BLOCK * (k + 1) - 1 : BLOCK * (k + 1)] for k in range(NBLK)]
    end = jnp.concatenate([jnp.broadcast_to(e, (HEADS, BLOCK)) for e in ends], axis=1)
    empty = jnp.zeros((8, TOK), F32)
    t1_v[...] = jnp.concatenate([la, step, jnp.exp2(end - la) * step, empty], axis=0).T
    t2_v[...] = jnp.concatenate([jnp.exp2(la), jnp.zeros((88, TOK), F32)], axis=0).T


def device_coefficients(ns, nl, t1_v):
    dec = [jnp.exp2(t1_v[BLOCK * (k + 1) - 1 : BLOCK * (k + 1), :]) for k in range(NBLK)]
    af = ab = jnp.ones((1, 128), F32)
    pc = jnp.zeros((1, 128), F32)
    for k in range(NBLK):
        af = af * (dec[k] * ns[k])
        pc = dec[k] * (pc * ns[k] + (1.0 - ns[k]))
        ab = ab * (dec[k] * nl[k])
    rows = jnp.concatenate([af, pc, ab, jnp.zeros((5, 128), F32)], axis=0)
    return jnp.where(iota((8, 128), 1) < HEADS, rows, 0.0)


def phase_decays(la_v, j):
    la = la_v[pl.ds(pl.multiple_of(PHEADS * j, PHEADS), PHEADS), :]
    out = []
    for k in range(NBLK):
        at = BLOCK * (k + 1) - 1
        out.append(jnp.broadcast_to(jnp.exp2(la[:, at : at + 1]), (PHEADS, 128))[:, None, :])
    return out


def summarize(j, ns, nl, xg_v, b_ref, c_ref, la_v, t1_v, t2_v, sx_v, sg_v, loc_v, mine):
    ls, lg = [], []
    for k in range(NBLK):
        rows = blockrows(k)
        sx, sg = [], []
        for p in range(PPAIRS):
            lanes = pl.ds(pl.multiple_of(PLANES * j + 128 * p, 128), 128)
            heads = half_heads(PPAIRS * j + p, BLOCK)
            sx.append((xg_v[0, rows, lanes].astype(F32) * gather(t1_v[rows, :], heads + 2 * HEADS)).astype(BF16))
            sg.append((xg_v[1, rows, lanes].astype(F32) * gather(t2_v[rows, :], heads)).astype(BF16))
            sx_v[rows, lanes] = sx[p]
            sg_v[rows, lanes] = sg[p]
        ls.append(dot(jnp.concatenate(sx, axis=1), b_ref[rows, :], TN).reshape(PHEADS, 64, 128))
        lg.append(dot(jnp.concatenate(sg, axis=1), c_ref[rows, :], TN).reshape(PHEADS, 64, 128))
    for n, value in enumerate((ls[0], ls[1], lg[0], lg[1], lg[2])):
        loc_v[j, n] = value
    dec = phase_decays(la_v, j)
    f = ls[0]
    for k in range(1, NBLK):
        f = (dec[k] * ns[k]) * f + ls[k]
    r = lg[2]
    for k in (1, 0):
        r = (dec[k] * nl[k]) * r + lg[k]
    mine[j, :, :, 0:16, :] = f.reshape(16, 2, 16, 128)
    mine[j, :, :, 16:32, :] = r.reshape(16, 2, 16, 128)


def inside_unit(j, k, xg_v, la_v, t1_v, inner_v, pt_v, dx_v):
    r = pl.ds(pl.multiple_of(k * BLOCK, BLOCK), BLOCK)
    table = t1_v[r, :]
    lane = iota((1, 128), 1)
    masks = [jnp.where((lane >= 64) == bool(n), 1.0, 0.0).astype(BF16) for n in range(2)]
    a00, a01, a11 = [], [], []
    for m in range(PPAIRS):
        pair = PPAIRS * j + m
        l = pl.ds(pl.multiple_of(pair * 128, 128), 128)
        g = xg_v[1, r, l]
        xs = (xg_v[0, r, l].astype(F32) * gather(table, half_heads(pair, BLOCK) + HEADS)).astype(BF16)
        gs = [g * m for m in masks]
        low = jnp.concatenate([gs[0][128:], gs[1][128:]], axis=0)
        p0 = dot(jnp.concatenate([xs[:128] * masks[0], xs[:128] * masks[1]], axis=0), g, NT)
        p1 = dot(xs[128:], low, NT)
        w11, d0 = [], []
        for n in range(2):
            row = la_v[pl.ds(2 * pair + n, 1), r]
            col = gather(table, jnp.full((BLOCK, 128), 2 * pair + n, jnp.int32))
            pn = p0[128 * n : 128 * (n + 1)]
            q00 = jnp.exp2(jnp.minimum(row[:, :128] - col[:128], 0.0))
            q01 = jnp.exp2(jnp.minimum(row[:, 128:] - col[:128], 0.0))
            q11 = jnp.exp2(jnp.minimum(row[:, 128:] - col[128:], 0.0))
            a00.append(q00 * pn[:, :128])
            a01.append(q01 * pn[:, 128:])
            a11.append(q11 * p1[:, 128 * n : 128 * (n + 1)])
            w00 = (q00 * inner_v[k, :128, :128]).astype(BF16)
            w01 = (q01 * inner_v[k, :128, 128:]).astype(BF16)
            w11.append((q11 * inner_v[k, 128:, 128:]).astype(BF16))
            d0.append(dot(jnp.concatenate([w00, w01], axis=1), gs[n]))
        d1 = dot(jnp.concatenate(w11, axis=1), low)
        dx_v[r, l] = jnp.concatenate([d0[0] + d0[1], d1], axis=0).astype(BF16)
    pt_v[k, :128, :128] += sum(a00[1:], a00[0])
    pt_v[k, :128, 128:] += sum(a01[1:], a01[0])
    pt_v[k, 128:, 128:] += sum(a11[1:], a11[0])


def gradients(j, ns, nl, b_ref, la_v, t1_v, sx_v, sg_v, loc_v, prompt, el_v, dx_v, acc_v):
    dec = phase_decays(la_v, j)
    el = el_v[j]
    shape = (PHEADS, 64, 128)
    prompt = prompt.reshape(shape)
    state = el[:, :, 0:16].reshape(shape)
    entering = []
    for k in range(NBLK):
        state = state * ns[k] + prompt * (1.0 - ns[k])
        entering.append(state.reshape(PLANES, 128).astype(BF16))
        if k < NBLK - 1:
            state = dec[k] * state + loc_v[j, k]
    state = el[:, :, 16:32].reshape(shape)
    leaving = [None] * NBLK
    total = None
    for k in reversed(range(NBLK)):
        state = state * nl[k]
        leaving[k] = state.reshape(PLANES, 128).astype(BF16)
        state = dec[k] * state + loc_v[j, 2 + k]
        at_start = state * (1.0 - ns[k])
        total = at_start if total is None else total + at_start
    lanes = pl.ds(pl.multiple_of(PLANES * j, PLANES), PLANES)
    for k in range(NBLK):
        rows = blockrows(k)
        outer = dot(b_ref[rows, :], leaving[k], NT)
        table = t1_v[rows, :]
        for p in range(PPAIRS):
            at = pl.ds(pl.multiple_of(PLANES * j + 128 * p, 128), 128)
            heads = half_heads(PPAIRS * j + p, BLOCK)
            near = gather(table, heads + HEADS) * dx_v[rows, at].astype(F32)
            far = gather(table, heads + 2 * HEADS) * outer[:, 128 * p : 128 * (p + 1)]
            dx_v[rows, at] = (near + far).astype(BF16)
        acc_v[rows, :128] += dot(sx_v[rows, lanes], leaving[k])
        acc_v[rows, 128:] += dot(sg_v[rows, lanes], entering[k])
    return total.reshape(32, 16, 128)


TICKS = PHASES + 8


def layer_kernel(
    lens_ref, step_ref, rate_ref, x_hbm, g_hbm, b_ref, c_ref, p_ref, li_hbm,
    xg_hbm, pg_ref, wg_ref,
    xg_v, dx_v, sx_v, sg_v, la_v, t1_v, t2_v, inner_v, pt_v, acc_v, loc_v, bc_v,
    cf_mine, cf_sib, cf_chip, cf_all, mine, sib_in, comb, got, back, ret, sib_out, el_v, prompts,
    pterm, sib_p, hp, pr1a, pr1b, ps1a, ps1b, pr2a, pr2b,
    part, sib, r1a, r1b, r1c, s1a, s1b, s1c, r2a, r2b, r2c, s2a, s2b, s2c, r3a, r3b, r3c,
    x_sem, g_sem, o_sem, c_send, c_recv, f_send, f_recv, l_send, l_recv, p_send, p_recv,
    a_send, a_recv, b_send, b_recv, li_sem, s_send, s_recv, w_send, w_recv, q_send, q_recv,
    w1_send, w1_recv,
):
    group, seq = lax.axis_index("group"), lax.axis_index("seq")
    core = seq % 2
    chip = seq // 2
    y, z = chip // 4, chip % 4
    sibling = (group, chip * 2 + (1 - core))
    is0 = core == 0

    def chip_at(d):
        return ((y + d // 4) % 4) * 4 + (z + d % 4) % 4

    def in_plane(d):
        return (group, chip_at(d) * 2 + core)

    def to_x(d):
        return ((group + d) % 4, seq)

    def to_y(d):
        return in_plane(4 * d)

    def to_z(d):
        return in_plane(d)

    def send(src, dst, s, r, to):
        return pltpu.make_async_remote_copy(
            src_ref=src, dst_ref=dst, send_sem=s, recv_sem=r, device_id=to, device_id_type=MESH
        )

    def lanes(j):
        return pl.ds(pl.multiple_of(PLANES * j, PLANES), PLANES)

    def load_x(j):
        return pltpu.make_async_copy(x_hbm.at[:, lanes(j)], xg_v.at[0, :, lanes(j)], x_sem.at[j])

    def load_g(j):
        return pltpu.make_async_copy(g_hbm.at[:, lanes(j)], xg_v.at[1, :, lanes(j)], g_sem.at[j])

    def load_li(n):
        return pltpu.make_async_copy(li_hbm.at[:, WIDTH * n : WIDTH * (n + 1)], xg_v.at[n], li_sem.at[n])

    def store(j):
        return pltpu.make_async_copy(dx_v.at[:, lanes(j)], xg_hbm.at[:, lanes(j)], o_sem.at[j])

    def each(lo, hi, f):
        def step(i, _):
            f(i)
            return 0

        lax.fori_loop(lo, hi, step, 0)

    def begin(j):
        load_x(j).start()
        load_g(j).start()

    each(0, PHASES, begin)

    barrier = pltpu.get_barrier_semaphore()

    def greet(to):
        pl.semaphore_signal(barrier, inc=1, device_id=to, device_id_type=MESH)

    greet(sibling)
    each(1, 16, lambda d: greet(in_plane(d)))
    each(1, 4, lambda d: greet(to_x(d)))

    prepare(step_ref, rate_ref, la_v, t1_v, t2_v)
    ns, nl = flags(lens_ref)
    cf_mine[...] = device_coefficients(ns, nl, t1_v)

    pl.semaphore_wait(barrier, 19)

    def prompt_copy(d):
        return send(p_ref, prompts.at[chip, core], p_send.at[d], p_recv.at[d], in_plane(d))

    def prompt_pass():
        half = prompts.at[:, core]
        return send(half, half, p_send.at[0], p_recv.at[0], sibling)

    def coefficient_pass():
        return send(cf_mine, cf_sib, c_send.at[0], c_recv.at[0], sibling)

    def coefficient_copy(d):
        return send(cf_chip, cf_all.at[chip], c_send.at[d], c_recv.at[d], in_plane(d))

    def chip_copy(j):
        return send(mine.at[j, :, 1 - core], sib_in.at[j], f_send.at[j], f_recv.at[j], sibling)

    def out_copy(j, d):
        return send(comb.at[j, chip_at(d)], got.at[j, chip], a_send.at[j, d], a_recv.at[j, d], in_plane(d))

    def back_copy(j, d):
        return send(back.at[j, chip_at(d)], ret.at[j, chip], b_send.at[j, d], b_recv.at[j, d], in_plane(d))

    def last_copy(j):
        return send(sib_out.at[j], el_v.at[j, :, core], l_send.at[j], l_recv.at[j], sibling)

    coefficient_pass().start()
    each(1, 16, lambda d: prompt_copy(d).start())
    prompts[chip, core] = p_ref[...]

    def pick(a, b):
        return jnp.where(is0, a, b), jnp.where(is0, b, a)

    def both(j):
        heads = PHEADS * j + iota((16, 128), 0) // 2

        def spread(tile):
            return [
                gather(jnp.broadcast_to(tile[n : n + 1], (16, 128)), heads)[:, None, :] for n in range(3)
            ]

        a, b = pick(mine[j, :, core], sib_in[j])
        t0, t1 = pick(cf_mine[...], cf_sib[...])
        return a, b, spread(t0), spread(t1)

    def combine(j):
        a, b, (_, _, ab0), (af1, _, _) = both(j)
        comb[j, :, 0:16, :] = b[:, 0:16] + af1 * a[:, 0:16]
        comb[j, :, 16:32, :] = a[:, 16:32] + ab0 * b[:, 16:32]

    def piece(j, owner):
        at = 32 * j + owner
        return at // 10, (at // 5) % 2, pl.ds(pl.multiple_of(16 * (at % 5), 16), 16)

    def prompt_rows(j, owner):
        a, b, rows = piece(j, owner)
        return prompts[a, b, rows, :]

    def scan(j):
        own = prompt_rows(j, seq)
        head = jnp.full((128, 128), PHEADS * j + seq // 4, jnp.int32)
        cf = gather(cf_all[...].reshape(128, 128), head)
        e = jnp.zeros((16, 128), F32)
        for q in range(16):
            back[j, q, 0:16, :] = e
            e = cf[8 * q : 8 * q + 1] * e + (cf[8 * q + 1 : 8 * q + 2] * own + got[j, q, 0:16, :])
        lv = jnp.zeros((16, 128), F32)
        for q in reversed(range(16)):
            back[j, q, 16:32, :] = lv
            lv = cf[8 * q + 2 : 8 * q + 3] * lv + got[j, q, 16:32, :]

    def finish(j):
        a, b, (af0, pc0, _), (_, _, ab1) = both(j)
        e0, l1 = ret[j, :, 0:16, :], ret[j, :, 16:32, :]
        prompt = jnp.stack([prompt_rows(j, 2 * q + core) for q in range(16)], axis=0)
        e1 = af0 * e0 + (pc0 * prompt + a[:, 0:16])
        l0 = ab1 * l1 + b[:, 16:32]
        e_mine, e_other = pick(e0, e1)
        l_mine, l_other = pick(l0, l1)
        el_v[j, :, core, 0:16, :] = e_mine
        el_v[j, :, core, 16:32, :] = l_mine
        sib_out[j, :, 0:16, :] = e_other
        sib_out[j, :, 16:32, :] = l_other

    keep = iota((BLOCK, BLOCK), 1) >= iota((BLOCK, BLOCK), 0)

    def tick(t):
        @pl.when(t < PHASES)
        def _():
            load_x(t).wait()
            load_g(t).wait()
            summarize(t, ns, nl, xg_v, b_ref, c_ref, la_v, t1_v, t2_v, sx_v, sg_v, loc_v, mine)
            chip_copy(t).start()

        @pl.when(t == 0)
        def _():
            coefficient_pass().wait()
            t0, t1 = pick(cf_mine[...], cf_sib[...])
            cf_chip[...] = jnp.concatenate(
                [t0[0:1] * t1[0:1], t1[1:2] + t1[0:1] * t0[1:2], t0[2:3] * t1[2:3], t0[3:8]], axis=0
            )
            each(1, 16, lambda d: coefficient_copy(d).start())
            cf_all[chip] = cf_chip[...]

        @pl.when((t >= 1) & (t < PHASES + 1))
        def _():
            j = t - 1
            chip_copy(j).wait()
            combine(j)
            each(1, 16, lambda d: out_copy(j, d).start())
            got[j, chip] = comb[j, chip]

        @pl.when(t == 1)
        def _():
            each(1, 16, lambda d: prompt_copy(d).wait())
            prompt_pass().start()

        @pl.when(t == 3)
        def _():
            prompt_pass().wait()
            each(1, 16, lambda d: coefficient_copy(d).wait())

        @pl.when(t == 4)
        def _():
            for k in range(NBLK):
                rows = blockrows(k)
                inner_v[k] = jnp.where(keep, dot(b_ref[rows, :], c_ref[rows, :], NT), 0.0)
                pt_v[k] = jnp.zeros((BLOCK, BLOCK), F32)
            acc_v[...] = jnp.zeros_like(acc_v)

        @pl.when((t >= 5) & (t < PHASES + 5))
        def _():
            each(0, NBLK, lambda k: inside_unit(t - 5, k, xg_v, la_v, t1_v, inner_v, pt_v, dx_v))

        @pl.when((t >= 4) & (t < PHASES + 4))
        def _():
            j = t - 4
            each(1, 16, lambda d: out_copy(j, d).wait())
            scan(j)
            each(1, 16, lambda d: back_copy(j, d).start())
            ret[j, chip] = back[j, chip]

        @pl.when(t == PHASES + 4)
        def _():
            for n in range(2):
                load_li(n).start()

        @pl.when((t >= 7) & (t < PHASES + 7))
        def _():
            j = t - 7
            each(1, 16, lambda d: back_copy(j, d).wait())
            finish(j)
            last_copy(j).start()

        @pl.when(t >= 8)
        def _():
            j = t - 8
            last_copy(j).wait()
            prompt = jnp.stack([prompt_rows(j, o) for o in range(32)], axis=0)
            total = gradients(j, ns, nl, b_ref, la_v, t1_v, sx_v, sg_v, loc_v, prompt, el_v, dx_v, acc_v)
            store(j).start()
            for o in range(32):
                a, b, rows = piece(j, o)
                pterm[a, b, rows, :] = total[o]

    each(0, TICKS, tick)

    def p_copy(n, stage, d, src, dst, to):
        return send(src, dst, q_send.at[n, stage, d], q_recv.at[n, stage, d], to)

    def p_chip():
        return p_copy(0, 0, 0, pterm.at[:, 1 - core], sib_p, sibling)

    def p_first(n, d):
        if n == 0:
            return p_copy(n, 0, d, hp.at[(y + d) % 4, :, 0:40], pr1a.at[d], to_y(d))
        return p_copy(n, 0, d, hp.at[:, (z + d) % 4, 40:80], pr1b.at[d], to_z(d))

    def p_second(n, d):
        if n == 0:
            return p_copy(n, 1, d, ps1a.at[(z + d) % 4], pr2a.at[d], to_z(d))
        return p_copy(n, 1, d, ps1b.at[(y + d) % 4], pr2b.at[d], to_y(d))

    p_chip().start()
    for k in range(NBLK):
        rows = blockrows(k)
        pt = jnp.where(keep, pt_v[k], 0.0).astype(BF16)
        bc_v[rows, :128] = (acc_v[rows, :128] + dot(pt, c_ref[rows, :])).astype(BF16)
        bc_v[rows, 128:] = (acc_v[rows, 128:] + dot(pt, b_ref[rows, :], TN)).astype(BF16)
    p_chip().wait()
    hp[...] = (pterm[:, core] + sib_p[...]).reshape(4, 4, 80, 128)
    for d in (1, 3, 2):
        for n in range(2):
            p_first(n, d).start()

    def w_copy(n, stage, d, src, dst, to):
        return send(src, dst, w_send.at[n, stage, d], w_recv.at[n, stage, d], to)

    def cut(n):
        return pl.ds(ROWS[n][0], ROWS[n][1] - ROWS[n][0]), pl.ds(COLS[n][0], COLS[n][1] - COLS[n][0])

    def slab_x(s):
        return (group + s) % 4

    def sib_copy(s, n):
        at = slab_x(s)
        return send(
            part.at[at, pl.ds(2 * n, 2), :, 1 - core], sib.at[at, pl.ds(2 * n, 2)],
            s_send.at[s, n], s_recv.at[s, n], sibling,
        )

    def first_x(d):
        return w_copy(0, 0, d, part.at[slab_x(d), :, :, core, *cut(0)], r1a.at[d], to_x(d))

    def first_y(s, d):
        at = slab_x(s)
        return send(
            part.at[at, (y + d) % 4, :, core, *cut(1)], r1b.at[d, at],
            w1_send.at[0, s, d], w1_recv.at[0, s, d], to_y(d),
        )

    def first_z(s, d):
        at = slab_x(s)
        return send(
            part.at[at, :, (z + d) % 4, core, *cut(2)], r1c.at[d, at],
            w1_send.at[1, s, d], w1_recv.at[1, s, d], to_z(d),
        )

    def settle(s):
        at = slab_x(s)
        for n in range(2):
            sib_copy(s, n).wait()
        part[at, :, :, core] = part[at, :, :, core] + sib[at]
        if s > 0:
            first_x(s).start()
        for d in (1, 3, 2):
            first_y(s, d).start()
            first_z(s, d).start()

    for n in range(2):
        load_li(n).wait()
    bc = bc_v[...]
    order = (1, 3, 2, 0)
    for i, s in enumerate(order):
        at = slab_x(s)
        for n in range(2):
            m = at * 2 + n
            cols = pl.ds(pl.multiple_of(SLAB * (m % 4), SLAB), SLAB)
            out = dot(xg_v[m // 4, :, cols], bc, TN)
            part[at, 2 * n : 2 * n + 2] = out.reshape(2, 4, 2, 40, 256)
            sib_copy(s, n).start()
        if i > 0:
            settle(order[i - 1])
    settle(0)

    def second(n, d):
        if n == 0:
            return w_copy(n, 1, d, s1a.at[(y + d) % 4], r2a.at[d], to_y(d))
        if n == 1:
            return w_copy(n, 1, d, s1b.at[:, (z + d) % 4], r2b.at[d], to_z(d))
        return w_copy(n, 1, d, s1c.at[(group + d) % 4], r2c.at[d], to_x(d))

    def third(n, d):
        if n == 0:
            return w_copy(n, 2, d, s2a.at[(z + d) % 4], r3a.at[d], to_z(d))
        if n == 1:
            return w_copy(n, 2, d, s2b.at[(group + d) % 4], r3b.at[d], to_x(d))
        return w_copy(n, 2, d, s2c.at[(y + d) % 4], r3c.at[d], to_y(d))

    for n in range(2):
        for d in (1, 2, 3):
            p_first(n, d).wait()
    ps1a[...] = hp[y, :, 0:40] + pr1a[1] + pr1a[2] + pr1a[3]
    ps1b[...] = hp[:, z, 40:80] + pr1b[1] + pr1b[2] + pr1b[3]
    for d in (1, 3, 2):
        for n in range(2):
            p_second(n, d).start()

    for n in range(3):
        if n == 0:
            for d in (1, 2, 3):
                first_x(d).wait()
            s1a[...] = part[group, :, :, core, 0:16] + r1a[1] + r1a[2] + r1a[3]
        elif n == 1:
            for s in order:
                for d in (1, 2, 3):
                    first_y(s, d).wait()
            s1b[...] = part[:, y, :, core, 16:40, 0:128] + r1b[1] + r1b[2] + r1b[3]
        else:
            for s in order:
                for d in (1, 2, 3):
                    first_z(s, d).wait()
            s1c[...] = part[:, :, z, core, 16:40, 128:256] + r1c[1] + r1c[2] + r1c[3]
        for d in (1, 3, 2):
            second(n, d).start()
    for n in range(3):
        for d in (1, 2, 3):
            second(n, d).wait()
        if n == 0:
            s2a[...] = s1a[y] + r2a[1] + r2a[2] + r2a[3]
        elif n == 1:
            s2b[...] = s1b[:, z] + r2b[1] + r2b[2] + r2b[3]
        else:
            s2c[...] = s1c[group] + r2c[1] + r2c[2] + r2c[3]
        for d in (1, 3, 2):
            third(n, d).start()
    for n in range(2):
        for d in (1, 2, 3):
            p_second(n, d).wait()
    pg_ref[0:40, :] = ps1a[z] + pr2a[1] + pr2a[2] + pr2a[3]
    pg_ref[40:80, :] = ps1b[y] + pr2b[1] + pr2b[2] + pr2b[3]
    for n, (own, r, at) in enumerate(((s2a, r3a, z), (s2b, r3b, group), (s2c, r3c, y))):
        for d in (1, 2, 3):
            third(n, d).wait()
        wg_ref[ROWS[n][0] : ROWS[n][1], COLS[n][0] : COLS[n][1]] = own[at] + r[1] + r[2] + r[3]
    each(0, PHASES, lambda j: store(j).wait())


def layer(lens, step, rates, x, g, b, c, p, li):
    v = pl.BlockSpec(memory_space=pltpu.VMEM)
    a = pl.BlockSpec(memory_space=pl.ANY)
    wide = pltpu.VMEM((TOK, WIDTH), BF16)
    square = pltpu.VMEM((NBLK, BLOCK, BLOCK), F32)
    f = lambda *shape: pltpu.VMEM(shape, F32)
    dma = lambda *n: pltpu.SemaphoreType.DMA(n)
    half = f(PHASES, 16, 32, 128)
    return pl.pallas_call(
        layer_kernel,
        in_specs=[pl.BlockSpec(memory_space=pltpu.SMEM), v, v, a, a, v, v, v, a],
        out_specs=[a, v, v],
        out_shape=[
            jax.ShapeDtypeStruct((TOK, WIDTH), BF16),
            jax.ShapeDtypeStruct((80, 128), F32),
            jax.ShapeDtypeStruct((40, 256), F32),
        ],
        scratch_shapes=[
            pltpu.VMEM((2, TOK, WIDTH), BF16), wide, wide, wide,
            f(HEADS, TOK), f(TOK, 128), f(TOK, 128), square, square, f(TOK, 256),
            f(PHASES, 5, PHEADS, 64, 128), pltpu.VMEM((TOK, 256), BF16),
            f(8, 128), f(8, 128), f(8, 128), f(16, 8, 128),
            f(PHASES, 16, 2, 32, 128), half, half, half, half, half, half,
            f(PHASES, 16, 2, 32, 128), f(16, 2, 80, 128),
            f(16, 2, 80, 128), f(16, 80, 128), f(4, 4, 80, 128), f(4, 4, 40, 128), f(4, 4, 40, 128),
            f(4, 40, 128), f(4, 40, 128), f(4, 40, 128), f(4, 40, 128),
            f(4, 4, 4, 2, 40, 256), f(4, 4, 4, 40, 256),
            f(4, 4, 4, 16, 256), f(4, 4, 4, 24, 128), f(4, 4, 4, 24, 128),
            f(4, 4, 16, 256), f(4, 4, 24, 128), f(4, 4, 24, 128),
            f(4, 4, 16, 256), f(4, 4, 24, 128), f(4, 4, 24, 128),
            f(4, 16, 256), f(4, 24, 128), f(4, 24, 128),
            f(4, 16, 256), f(4, 24, 128), f(4, 24, 128),
            dma(PHASES), dma(PHASES), dma(PHASES), dma(16), dma(16), dma(PHASES), dma(PHASES),
            dma(PHASES), dma(PHASES), dma(16), dma(16), dma(PHASES, 16), dma(PHASES, 16),
            dma(PHASES, 16), dma(PHASES, 16), dma(2), dma(4, 2), dma(4, 2), dma(3, 3, 4), dma(3, 3, 4),
            dma(2, 2, 4), dma(2, 2, 4), dma(2, 4, 4), dma(2, 4, 4),
        ],
        compiler_params=pltpu.CompilerParams(
            collective_id=0, has_side_effects=True, vmem_limit_bytes=VMEM_LIMIT
        ),
    )(lens, step, rates, x, g, b, c, p, li)


def body(li, x, g, b, c, step, rates, prompt, lens):
    li, x, g, b, c, step, prompt = li[0], x[0], g[0], b[0], c[0], step[0], prompt[0]
    x_grad, prompt_grad, weight_grad = layer(
        lens, step, rates.reshape(1, HEADS), x, g, b, c, prompt, li
    )
    return x_grad[None], prompt_grad[None], weight_grad


def solution(mesh):
    in_specs = (
        P("group", "seq", None),
        P("group", "seq", None),
        P("group", "seq", None),
        P("group", "seq", None),
        P("group", "seq", None),
        P("group", None, "seq"),
        P(),
        P("group", "seq", None),
        P("group", None),
    )
    out_specs = (P("group", "seq", None), P("group", "seq", None), P(("group", "seq"), None))
    return jax.shard_map(body, mesh=mesh, in_specs=in_specs, out_specs=out_specs, check_vma=False)
```

```python
from functools import partial

import jax
import jax.numpy as jnp
from jax import lax
from jax.experimental import pallas as pl
from jax.experimental.pallas import tpu as pltpu
from jax.sharding import PartitionSpec as P

BLOCK = 256
NBLK = 3
TOK = BLOCK * NBLK
HEADS = 40
STATE = 128
WIDTH = 2560
DMODEL = 5120
PHASES = 5
PHEADS = HEADS // PHASES
PLANES = PHEADS * 64
PPAIRS = PHEADS // 2
ROWS = ((0, 16), (16, 40), (16, 40))
COLS = ((0, 256), (0, 128), (128, 256))
SLAB = 640
F32 = jnp.float32
BF16 = jnp.bfloat16
MESH = pl.DeviceIdType.MESH
NN = (((1,), (0,)), ((), ()))
TN = (((0,), (0,)), ((), ()))
NT = (((1,), (1,)), ((), ()))
LOG2E = 1.4426950408889634
VMEM_LIMIT = 62 * 1024 * 1024


def dot(a, b, dims=NN):
    return lax.dot_general(a, b, dims, preferred_element_type=F32)


def iota(shape, dim):
    return lax.broadcasted_iota(jnp.int32, shape, dim)


def flags(lens_ref):
    first = lax.axis_index("seq") * NBLK
    e1 = lens_ref[0, 0]
    e2 = e1 + lens_ref[0, 1]
    e3 = e2 + lens_ref[0, 2]
    e4 = e3 + lens_ref[0, 3]
    not_start, not_last = [], []
    for k in range(NBLK):
        at = first + k
        start = (at == 0) | (at == e1) | (at == e2) | (at == e3)
        last = (at == e1 - 1) | (at == e2 - 1) | (at == e3 - 1) | (at == e4 - 1)
        not_start.append(jnp.where(start, 0.0, 1.0).astype(F32))
        not_last.append(jnp.where(last, 0.0, 1.0).astype(F32))
    return not_start, not_last


def blockrows(k):
    return slice(BLOCK * k, BLOCK * (k + 1))


def gather(table, index):
    return jnp.take_along_axis(table, index, axis=1)


def half_heads(pair, rows):
    return 2 * pair + iota((rows, 128), 1) // 64


def prepare(step_ref, rate_ref, la_v, t1_v, t1b_v, t2b_v):
    step = step_ref[...]
    same = iota((HEADS, HEADS), 0) == iota((HEADS, HEADS), 1)
    spread = jnp.broadcast_to(rate_ref[...], (HEADS, HEADS))
    rate = jnp.sum(jnp.where(same, spread, 0.0), axis=1, keepdims=True)
    la = -step * rate
    place = iota((HEADS, TOK), 1) % BLOCK
    shift = 1
    while shift < BLOCK:
        la = la + jnp.where(place >= shift, pltpu.roll(la, shift, 1), 0.0)
        shift *= 2
    la = la * LOG2E
    la_v[...] = la
    ends = [la[:, BLOCK * (k + 1) - 1 : BLOCK * (k + 1)] for k in range(NBLK)]
    end = jnp.concatenate([jnp.broadcast_to(e, (HEADS, BLOCK)) for e in ends], axis=1)
    empty = jnp.zeros((8, TOK), F32)
    t1 = jnp.concatenate([la, step, jnp.exp2(end - la) * step, empty], axis=0).T
    t1_v[...] = t1
    t1b_v[...] = halves(t1)
    t2b_v[...] = halves(jnp.concatenate([jnp.exp2(la), jnp.zeros((88, TOK), F32)], axis=0).T)


def device_coefficients(ns, nl, t1_v):
    dec = [jnp.exp2(t1_v[BLOCK * (k + 1) - 1 : BLOCK * (k + 1), :]) for k in range(NBLK)]
    af = ab = jnp.ones((1, 128), F32)
    pc = jnp.zeros((1, 128), F32)
    for k in range(NBLK):
        af = af * (dec[k] * ns[k])
        pc = dec[k] * (pc * ns[k] + (1.0 - ns[k]))
        ab = ab * (dec[k] * nl[k])
    rows = jnp.concatenate([af, pc, ab, jnp.zeros((5, 128), F32)], axis=0)
    return jnp.where(iota((8, 128), 1) < HEADS, rows, 0.0)


def halves(table):
    high = table.astype(BF16)
    return jnp.concatenate([high, (table - high.astype(F32)).astype(BF16)], axis=1)


def selector(first):
    row, lane = iota((256, PLANES), 0), iota((256, PLANES), 1)
    return jnp.where(row % 128 == first + lane // 64, 1.0, 0.0).astype(BF16)


def phase_decays(la_v, j):
    la = la_v[pl.ds(pl.multiple_of(PHEADS * j, PHEADS), PHEADS), :]
    out = []
    for k in range(NBLK):
        at = BLOCK * (k + 1) - 1
        out.append(jnp.broadcast_to(jnp.exp2(la[:, at : at + 1]), (PHEADS, 128))[:, None, :])
    return out


def summarize(j, ns, nl, xg_v, b_ref, c_ref, la_v, t1b_v, t2b_v, sx_v, sg_v, loc_v, mine):
    ls, lg = [], []
    for k in range(NBLK):
        rows = blockrows(k)
        sx, sg = [], []
        ex = dot(t1b_v[rows, :], selector(2 * HEADS + PHEADS * j))
        eg = dot(t2b_v[rows, :], selector(PHEADS * j))
        for p in range(PPAIRS):
            lanes = pl.ds(pl.multiple_of(PLANES * j + 128 * p, 128), 128)
            heads = half_heads(PPAIRS * j + p, BLOCK)
            wx, wg = ex[:, 128 * p : 128 * (p + 1)], eg[:, 128 * p : 128 * (p + 1)]
            sx.append((xg_v[0, rows, lanes].astype(F32) * wx).astype(BF16))
            sg.append((xg_v[1, rows, lanes].astype(F32) * wg).astype(BF16))
            sx_v[rows, lanes] = sx[p]
            sg_v[rows, lanes] = sg[p]
        ls.append(dot(jnp.concatenate(sx, axis=1), b_ref[rows, :], TN).reshape(PHEADS, 64, 128))
        lg.append(dot(jnp.concatenate(sg, axis=1), c_ref[rows, :], TN).reshape(PHEADS, 64, 128))
    for n, value in enumerate((ls[0], ls[1], lg[0], lg[1], lg[2])):
        loc_v[j, n] = value
    dec = phase_decays(la_v, j)
    f = ls[0]
    for k in range(1, NBLK):
        f = (dec[k] * ns[k]) * f + ls[k]
    r = lg[2]
    for k in (1, 0):
        r = (dec[k] * nl[k]) * r + lg[k]
    mine[j, :, :, 0:16, :] = f.reshape(16, 2, 16, 128)
    mine[j, :, :, 16:32, :] = r.reshape(16, 2, 16, 128)


def inside_unit(j, k, xg_v, la_v, t1_v, inner_v, pt_v, dx_v):
    r = pl.ds(pl.multiple_of(k * BLOCK, BLOCK), BLOCK)
    table = t1_v[r, :]
    lane = iota((1, 128), 1)
    masks = [jnp.where((lane >= 64) == bool(n), 1.0, 0.0).astype(BF16) for n in range(2)]
    a00, a01, a11 = [], [], []
    for m in range(PPAIRS):
        pair = PPAIRS * j + m
        l = pl.ds(pl.multiple_of(pair * 128, 128), 128)
        g = xg_v[1, r, l]
        xs = (xg_v[0, r, l].astype(F32) * gather(table, half_heads(pair, BLOCK) + HEADS)).astype(BF16)
        gs = [g * m for m in masks]
        low = jnp.concatenate([gs[0][128:], gs[1][128:]], axis=0)
        p0 = dot(jnp.concatenate([xs[:128] * masks[0], xs[:128] * masks[1]], axis=0), g, NT)
        p1 = dot(xs[128:], low, NT)
        w11, d0 = [], []
        for n in range(2):
            row = la_v[pl.ds(2 * pair + n, 1), r]
            col = gather(table, jnp.full((BLOCK, 128), 2 * pair + n, jnp.int32))
            pn = p0[128 * n : 128 * (n + 1)]
            q00 = jnp.exp2(jnp.minimum(row[:, :128] - col[:128], 0.0))
            q01 = jnp.exp2(jnp.minimum(row[:, 128:] - col[:128], 0.0))
            q11 = jnp.exp2(jnp.minimum(row[:, 128:] - col[128:], 0.0))
            a00.append(q00 * pn[:, :128])
            a01.append(q01 * pn[:, 128:])
            a11.append(q11 * p1[:, 128 * n : 128 * (n + 1)])
            w00 = (q00 * inner_v[k, :128, :128]).astype(BF16)
            w01 = (q01 * inner_v[k, :128, 128:]).astype(BF16)
            w11.append((q11 * inner_v[k, 128:, 128:]).astype(BF16))
            d0.append(dot(jnp.concatenate([w00, w01], axis=1), gs[n]))
        d1 = dot(jnp.concatenate(w11, axis=1), low)
        dx_v[r, l] = jnp.concatenate([d0[0] + d0[1], d1], axis=0).astype(BF16)
    pt_v[k, :128, :128] += sum(a00[1:], a00[0])
    pt_v[k, :128, 128:] += sum(a01[1:], a01[0])
    pt_v[k, 128:, 128:] += sum(a11[1:], a11[0])


def gradients(j, ns, nl, b_ref, la_v, t1b_v, sx_v, sg_v, loc_v, prompt, el_v, dx_v, acc_v):
    dec = phase_decays(la_v, j)
    el = el_v[j]
    shape = (PHEADS, 64, 128)
    prompt = prompt.reshape(shape)
    state = el[:, :, 0:16].reshape(shape)
    entering = []
    for k in range(NBLK):
        state = state * ns[k] + prompt * (1.0 - ns[k])
        entering.append(state.reshape(PLANES, 128).astype(BF16))
        if k < NBLK - 1:
            state = dec[k] * state + loc_v[j, k]
    state = el[:, :, 16:32].reshape(shape)
    leaving = [None] * NBLK
    total = None
    for k in reversed(range(NBLK)):
        state = state * nl[k]
        leaving[k] = state.reshape(PLANES, 128).astype(BF16)
        state = dec[k] * state + loc_v[j, 2 + k]
        at_start = state * (1.0 - ns[k])
        total = at_start if total is None else total + at_start
    lanes = pl.ds(pl.multiple_of(PLANES * j, PLANES), PLANES)
    for k in range(NBLK):
        rows = blockrows(k)
        outer = dot(b_ref[rows, :], leaving[k], NT)
        near_w = dot(t1b_v[rows, :], selector(HEADS + PHEADS * j))
        far_w = dot(t1b_v[rows, :], selector(2 * HEADS + PHEADS * j))
        for p in range(PPAIRS):
            cut = slice(128 * p, 128 * (p + 1))
            at = pl.ds(pl.multiple_of(PLANES * j + 128 * p, 128), 128)
            heads = half_heads(PPAIRS * j + p, BLOCK)
            near = near_w[:, cut] * dx_v[rows, at].astype(F32)
            far = far_w[:, cut] * outer[:, cut]
            dx_v[rows, at] = (near + far).astype(BF16)
        acc_v[rows, :128] += dot(sx_v[rows, lanes], leaving[k])
        acc_v[rows, 128:] += dot(sg_v[rows, lanes], entering[k])
    return total.reshape(32, 16, 128)


TICKS = PHASES + 8


def layer_kernel(
    lens_ref, step_ref, rate_ref, x_hbm, g_hbm, b_ref, c_ref, p_ref, li_hbm,
    xg_hbm, pg_ref, wg_ref,
    xg_v, dx_v, sx_v, sg_v, la_v, t1_v, t1b_v, t2b_v, inner_v, pt_v, acc_v, loc_v, bc_v,
    cf_mine, cf_sib, cf_chip, cf_all, mine, sib_in, comb, got, back, ret, sib_out, el_v, prompts,
    pterm, sib_p, pr1a, pr1b, ps1a, ps1b, pr2a, pr2b,
    part, sib, r1a, r1b, r1c, s1a, s1b, s1c, r2a, r2b, r2c, s2a, s2b, s2c, r3a, r3b, r3c,
    x_sem, g_sem, o_sem, c_send, c_recv, f_send, f_recv, l_send, l_recv, p_send, p_recv,
    a_send, a_recv, b_send, b_recv, li_sem, s_send, s_recv, w_send, w_recv, q_send, q_recv,
):
    group, seq = lax.axis_index("group"), lax.axis_index("seq")
    core = seq % 2
    chip = seq // 2
    y, z = chip // 4, chip % 4
    sibling = (group, chip * 2 + (1 - core))
    is0 = core == 0

    def chip_at(d):
        return ((y + d // 4) % 4) * 4 + (z + d % 4) % 4

    def in_plane(d):
        return (group, chip_at(d) * 2 + core)

    def to_x(d):
        return ((group + d) % 4, seq)

    def to_y(d):
        return in_plane(4 * d)

    def to_z(d):
        return in_plane(d)

    def send(src, dst, s, r, to):
        return pltpu.make_async_remote_copy(
            src_ref=src, dst_ref=dst, send_sem=s, recv_sem=r, device_id=to, device_id_type=MESH
        )

    def lanes(j):
        return pl.ds(pl.multiple_of(PLANES * j, PLANES), PLANES)

    def load_x(j):
        return pltpu.make_async_copy(x_hbm.at[:, lanes(j)], xg_v.at[0, :, lanes(j)], x_sem.at[j])

    def load_g(j):
        return pltpu.make_async_copy(g_hbm.at[:, lanes(j)], xg_v.at[1, :, lanes(j)], g_sem.at[j])

    def load_li(n):
        return pltpu.make_async_copy(li_hbm.at[:, WIDTH * n : WIDTH * (n + 1)], xg_v.at[n], li_sem.at[n])

    def store(j):
        return pltpu.make_async_copy(dx_v.at[:, lanes(j)], xg_hbm.at[:, lanes(j)], o_sem.at[0])

    def each(lo, hi, f):
        def step(i, _):
            f(i)
            return 0

        lax.fori_loop(lo, hi, step, 0)

    def begin(j):
        load_x(j).start()
        load_g(j).start()

    each(0, PHASES, begin)

    barrier = pltpu.get_barrier_semaphore()

    def greet(to):
        pl.semaphore_signal(barrier, inc=1, device_id=to, device_id_type=MESH)

    greet(sibling)
    each(1, 16, lambda d: greet(in_plane(d)))
    each(1, 4, lambda d: greet(to_x(d)))

    prepare(step_ref, rate_ref, la_v, t1_v, t1b_v, t2b_v)
    ns, nl = flags(lens_ref)
    cf_mine[...] = device_coefficients(ns, nl, t1_v)

    def start_phase(t):
        load_x(t).wait()
        load_g(t).wait()
        summarize(t, ns, nl, xg_v, b_ref, c_ref, la_v, t1b_v, t2b_v, sx_v, sg_v, loc_v, mine)

    start_phase(0)
    pl.semaphore_wait(barrier, 19)

    def prompt_copy(d):
        return send(p_ref, prompts.at[chip, core], p_send.at[1], p_recv.at[1], in_plane(d))

    def prompt_all():
        some = prompts.at[pl.ds(0, 15), 0]
        return send(some, some, p_send.at[1], p_recv.at[1], sibling)

    def prompt_pass():
        half = prompts.at[:, core]
        return send(half, half, p_send.at[0], p_recv.at[0], sibling)

    def coefficient_pass():
        return send(cf_mine, cf_sib, c_send.at[0], c_recv.at[0], sibling)

    def coefficient_copy(d):
        return send(cf_chip, cf_all.at[chip], c_send.at[1], c_recv.at[1], in_plane(d))

    def coefficient_all():
        some = cf_all.at[pl.ds(0, 15)]
        return send(some, some, c_send.at[1], c_recv.at[1], sibling)

    def chip_copy(j):
        return send(mine.at[j, :, 1 - core], sib_in.at[j], f_send.at[j], f_recv.at[j], sibling)

    def out_copy(j, d):
        return send(comb.at[j, chip_at(d)], got.at[j, chip], a_send.at[j], a_recv.at[j], in_plane(d))

    def out_all(j):
        some = pl.ds(0, 15)
        return send(comb.at[j, some], got.at[j, some], a_send.at[j], a_recv.at[j], sibling)

    def back_copy(j, d):
        return send(back.at[j, chip_at(d)], ret.at[j, chip], b_send.at[j], b_recv.at[j], in_plane(d))

    def back_all(j):
        some = pl.ds(0, 15)
        return send(back.at[j, some], ret.at[j, some], b_send.at[j], b_recv.at[j], sibling)

    def last_copy(j):
        return send(sib_out.at[j], el_v.at[j, :, core], l_send.at[j], l_recv.at[j], sibling)

    coefficient_pass().start()
    chip_copy(0).start()
    each(1, 16, lambda d: prompt_copy(d).start())
    prompts[chip, core] = p_ref[...]

    def pick(a, b):
        return jnp.where(is0, a, b), jnp.where(is0, b, a)

    def both(j):
        heads = PHEADS * j + iota((16, 128), 0) // 2

        def spread(tile):
            return [
                gather(jnp.broadcast_to(tile[n : n + 1], (16, 128)), heads)[:, None, :] for n in range(3)
            ]

        a, b = pick(mine[j, :, core], sib_in[j])
        t0, t1 = pick(cf_mine[...], cf_sib[...])
        return a, b, spread(t0), spread(t1)

    def combine(j):
        a, b, (_, _, ab0), (af1, _, _) = both(j)
        comb[j, :, 0:16, :] = b[:, 0:16] + af1 * a[:, 0:16]
        comb[j, :, 16:32, :] = a[:, 16:32] + ab0 * b[:, 16:32]

    def piece(j, owner):
        at = 32 * j + owner
        return at // 10, (at // 5) % 2, pl.ds(pl.multiple_of(16 * (at % 5), 16), 16)

    def prompt_rows(j, owner):
        a, b, rows = piece(j, owner)
        return prompts[a, b, rows, :]

    def scan(j):
        own = prompt_rows(j, seq)
        head = jnp.full((128, 128), PHEADS * j + seq // 4, jnp.int32)
        cf = gather(cf_all[...].reshape(128, 128), head)
        e = jnp.zeros((16, 128), F32)
        for q in range(16):
            back[j, q, 0:16, :] = e
            e = cf[8 * q : 8 * q + 1] * e + (cf[8 * q + 1 : 8 * q + 2] * own + got[j, q, 0:16, :])
        lv = jnp.zeros((16, 128), F32)
        for q in reversed(range(16)):
            back[j, q, 16:32, :] = lv
            lv = cf[8 * q + 2 : 8 * q + 3] * lv + got[j, q, 16:32, :]

    def finish(j):
        a, b, (af0, pc0, _), (_, _, ab1) = both(j)
        e0, l1 = ret[j, :, 0:16, :], ret[j, :, 16:32, :]
        prompt = jnp.stack([prompt_rows(j, 2 * q + core) for q in range(16)], axis=0)
        e1 = af0 * e0 + (pc0 * prompt + a[:, 0:16])
        l0 = ab1 * l1 + b[:, 16:32]
        e_mine, e_other = pick(e0, e1)
        l_mine, l_other = pick(l0, l1)
        el_v[j, :, core, 0:16, :] = e_mine
        el_v[j, :, core, 16:32, :] = l_mine
        sib_out[j, :, 0:16, :] = e_other
        sib_out[j, :, 16:32, :] = l_other

    keep = iota((BLOCK, BLOCK), 1) >= iota((BLOCK, BLOCK), 0)

    def tick(t):
        @pl.when(t < PHASES)
        def _():
            start_phase(t)
            chip_copy(t).start()

        @pl.when(t == 1)
        def _():
            coefficient_pass().wait()
            t0, t1 = pick(cf_mine[...], cf_sib[...])
            cf_chip[...] = jnp.concatenate(
                [t0[0:1] * t1[0:1], t1[1:2] + t1[0:1] * t0[1:2], t0[2:3] * t1[2:3], t0[3:8]], axis=0
            )
            each(1, 16, lambda d: coefficient_copy(d).start())
            cf_all[chip] = cf_chip[...]

        @pl.when(t < PHASES + 1)
        def _():
            j = t - 1
            chip_copy(j).wait()
            combine(j)
            each(1, 16, lambda d: out_copy(j, d).start())
            got[j, chip] = comb[j, chip]

        @pl.when(t == 2)
        def _():
            prompt_all().wait()
            prompt_pass().start()

        @pl.when(t == 3)
        def _():
            prompt_pass().wait()
            coefficient_all().wait()

        @pl.when(t == 4)
        def _():
            for k in range(NBLK):
                rows = blockrows(k)
                inner_v[k] = jnp.where(keep, dot(b_ref[rows, :], c_ref[rows, :], NT), 0.0)
                pt_v[k] = jnp.zeros((BLOCK, BLOCK), F32)
            acc_v[...] = jnp.zeros_like(acc_v)

        @pl.when((t >= 5) & (t < PHASES + 5))
        def _():
            each(0, NBLK, lambda k: inside_unit(t - 5, k, xg_v, la_v, t1_v, inner_v, pt_v, dx_v))

        @pl.when((t >= 4) & (t < PHASES + 4))
        def _():
            j = t - 4
            out_all(j).wait()
            scan(j)
            each(1, 16, lambda d: back_copy(j, d).start())
            ret[j, chip] = back[j, chip]

        @pl.when(t == PHASES + 4)
        def _():
            for n in range(2):
                load_li(n).start()

        @pl.when((t >= 7) & (t < PHASES + 7))
        def _():
            j = t - 7
            back_all(j).wait()
            finish(j)
            last_copy(j).start()

        @pl.when(t >= 8)
        def _():
            j = t - 8
            last_copy(j).wait()
            prompt = jnp.stack([prompt_rows(j, o) for o in range(32)], axis=0)
            total = gradients(j, ns, nl, b_ref, la_v, t1b_v, sx_v, sg_v, loc_v, prompt, el_v, dx_v, acc_v)
            store(j).start()
            for o in range(32):
                a, b, rows = piece(j, o)
                pterm[a // 4, a % 4, b, rows, :] = total[o]

    each(1, TICKS, tick)

    def p_copy(n, stage, d, src, dst, to):
        return send(src, dst, q_send.at[n, stage], q_recv.at[n, stage], to)

    def p_chip():
        return p_copy(2, 0, 0, pterm.at[:, :, 1 - core], sib_p, sibling)

    def p_first(n, d):
        if n == 0:
            return p_copy(n, 0, d, pterm.at[(y + d) % 4, :, core, 0:40], pr1a.at[d], to_y(d))
        return p_copy(n, 0, d, pterm.at[:, (z + d) % 4, core, 40:80], pr1b.at[d], to_z(d))

    def p_second(n, d):
        if n == 0:
            return p_copy(n, 1, d, ps1a.at[(z + d) % 4], pr2a.at[d], to_z(d))
        return p_copy(n, 1, d, ps1b.at[(y + d) % 4], pr2b.at[d], to_y(d))

    p_chip().start()
    for k in range(NBLK):
        rows = blockrows(k)
        pt = jnp.where(keep, pt_v[k], 0.0).astype(BF16)
        bc_v[rows, :128] = (acc_v[rows, :128] + dot(pt, c_ref[rows, :])).astype(BF16)
        bc_v[rows, 128:] = (acc_v[rows, 128:] + dot(pt, b_ref[rows, :], TN)).astype(BF16)
    def w_copy(n, stage, d, src, dst, to):
        return send(src, dst, w_send.at[n, stage], w_recv.at[n, stage], to)

    def cut(n):
        return pl.ds(ROWS[n][0], ROWS[n][1] - ROWS[n][0]), pl.ds(COLS[n][0], COLS[n][1] - COLS[n][0])

    def slab_x(s):
        return (group + s) % 4

    def sib_copy(s, n):
        at = slab_x(s)
        return send(
            part.at[at, pl.ds(2 * n, 2), :, 1 - core], sib.at[at, pl.ds(2 * n, 2)],
            s_send.at[s], s_recv.at[s], sibling,
        )

    def sib_all(s):
        at = slab_x(s)
        return send(part.at[at, :, :, 1 - core], sib.at[at], s_send.at[s], s_recv.at[s], sibling)

    def first_x(d):
        return w_copy(0, 0, d, part.at[slab_x(d), :, :, core, *cut(0)], r1a.at[d - 1], to_x(d))

    def first_y(s, d):
        at = slab_x(s)
        return send(
            part.at[at, (y + d) % 4, :, core, *cut(1)], r1b.at[d - 1, at],
            w_send.at[1, 0], w_recv.at[1, 0], to_y(d),
        )

    def first_z(s, d):
        at = slab_x(s)
        return send(
            part.at[at, :, (z + d) % 4, core, *cut(2)], r1c.at[d - 1, at],
            w_send.at[2, 0], w_recv.at[2, 0], to_z(d),
        )

    def settle(s):
        at = slab_x(s)
        sib_all(s).wait()
        part[at, :, :, core] = part[at, :, :, core] + sib[at]
        if s > 0:
            first_x(s).start()
        for d in (1, 3, 2):
            first_y(s, d).start()
            first_z(s, d).start()

    for n in range(2):
        load_li(n).wait()
    bc = bc_v[...]
    order = (1, 3, 2, 0)
    for i, s in enumerate(order):
        at = slab_x(s)
        for n in range(2):
            m = at * 2 + n
            cols = pl.ds(pl.multiple_of(SLAB * (m % 4), SLAB), SLAB)
            out = dot(xg_v[m // 4, :, cols], bc, TN)
            part[at, 2 * n : 2 * n + 2] = out.reshape(2, 4, 2, 40, 256)
            sib_copy(s, n).start()
        if i == 0:
            p_chip().wait()
            pterm[:, :, core] = pterm[:, :, core] + sib_p[...]
            for d in (1, 3, 2):
                for q in range(2):
                    p_first(q, d).start()
        else:
            settle(order[i - 1])
    settle(0)

    def second(n, d):
        if n == 0:
            return w_copy(n, 1, d, s1a.at[(y + d) % 4], r2a.at[d], to_y(d))
        if n == 1:
            return w_copy(n, 1, d, s1b.at[:, (z + d) % 4], r2b.at[d], to_z(d))
        return w_copy(n, 1, d, s1c.at[(group + d) % 4], r2c.at[d], to_x(d))

    def third(n, d):
        if n == 0:
            return w_copy(n, 2, d, s2a.at[(z + d) % 4], r3a.at[d], to_z(d))
        if n == 1:
            return w_copy(n, 2, d, s2b.at[(group + d) % 4], r3b.at[d], to_x(d))
        return w_copy(n, 2, d, s2c.at[(y + d) % 4], r3c.at[d], to_y(d))

    three = pl.ds(1, 3)
    peers = pl.ds(0, 3)
    p_copy(0, 0, 1, pterm.at[peers, :, 0, 0:40], pr1a.at[three], sibling).wait()
    p_copy(1, 0, 1, pterm.at[peers, :, 0, 40:80], pr1b.at[three], sibling).wait()
    ps1a[...] = pterm[y, :, core, 0:40] + pr1a[1] + pr1a[2] + pr1a[3]
    ps1b[...] = pterm[:, z, core, 40:80] + pr1b[1] + pr1b[2] + pr1b[3]
    for d in (1, 3, 2):
        for n in range(2):
            p_second(n, d).start()

    for n in range(3):
        if n == 0:
            w_copy(0, 0, 1, r1a, r1a, sibling).wait()
            s1a[...] = part[group, :, :, core, 0:16] + r1a[0] + r1a[1] + r1a[2]
        elif n == 1:
            w_copy(1, 0, 1, r1b, r1b, sibling).wait()
            s1b[...] = part[:, y, :, core, 16:40, 0:128] + r1b[0] + r1b[1] + r1b[2]
        else:
            w_copy(2, 0, 1, r1c, r1c, sibling).wait()
            s1c[...] = part[:, :, z, core, 16:40, 128:256] + r1c[0] + r1c[1] + r1c[2]
        for d in (1, 3, 2):
            second(n, d).start()
    for n, r in enumerate((r2a, r2b, r2c)):
        w_copy(n, 1, 1, r.at[three], r.at[three], sibling).wait()
        if n == 0:
            s2a[...] = s1a[y] + r2a[1] + r2a[2] + r2a[3]
        elif n == 1:
            s2b[...] = s1b[:, z] + r2b[1] + r2b[2] + r2b[3]
        else:
            s2c[...] = s1c[group] + r2c[1] + r2c[2] + r2c[3]
        for d in (1, 3, 2):
            third(n, d).start()
    p_copy(0, 1, 1, pr2a.at[three], pr2a.at[three], sibling).wait()
    p_copy(1, 1, 1, pr2b.at[three], pr2b.at[three], sibling).wait()
    pg_ref[0:40, :] = ps1a[z] + pr2a[1] + pr2a[2] + pr2a[3]
    pg_ref[40:80, :] = ps1b[y] + pr2b[1] + pr2b[2] + pr2b[3]
    for n, (own, r, at) in enumerate(((s2a, r3a, z), (s2b, r3b, group), (s2c, r3c, y))):
        w_copy(n, 2, 1, r.at[three], r.at[three], sibling).wait()
        wg_ref[ROWS[n][0] : ROWS[n][1], COLS[n][0] : COLS[n][1]] = own[at] + r[1] + r[2] + r[3]
    pltpu.make_async_copy(dx_v, xg_hbm, o_sem.at[0]).wait()


def layer(lens, step, rates, x, g, b, c, p, li):
    v = pl.BlockSpec(memory_space=pltpu.VMEM)
    a = pl.BlockSpec(memory_space=pl.ANY)
    wide = pltpu.VMEM((TOK, WIDTH), BF16)
    square = pltpu.VMEM((NBLK, BLOCK, BLOCK), F32)
    f = lambda *shape: pltpu.VMEM(shape, F32)
    dma = lambda *n: pltpu.SemaphoreType.DMA(n)
    half = f(PHASES, 16, 32, 128)
    return pl.pallas_call(
        layer_kernel,
        in_specs=[pl.BlockSpec(memory_space=pltpu.SMEM), v, v, a, a, v, v, v, a],
        out_specs=[a, v, v],
        out_shape=[
            jax.ShapeDtypeStruct((TOK, WIDTH), BF16),
            jax.ShapeDtypeStruct((80, 128), F32),
            jax.ShapeDtypeStruct((40, 256), F32),
        ],
        scratch_shapes=[
            pltpu.VMEM((2, TOK, WIDTH), BF16), wide, wide, wide,
            f(HEADS, TOK), f(TOK, 128), pltpu.VMEM((TOK, 256), BF16), pltpu.VMEM((TOK, 256), BF16), square, square, f(TOK, 256),
            f(PHASES, 5, PHEADS, 64, 128), pltpu.VMEM((TOK, 256), BF16),
            f(8, 128), f(8, 128), f(8, 128), f(16, 8, 128),
            f(PHASES, 16, 2, 32, 128), half, half, half, half, half, half,
            f(PHASES, 16, 2, 32, 128), f(16, 2, 80, 128),
            f(4, 4, 2, 80, 128), f(4, 4, 80, 128), f(4, 4, 40, 128), f(4, 4, 40, 128),
            f(4, 40, 128), f(4, 40, 128), f(4, 40, 128), f(4, 40, 128),
            f(4, 4, 4, 2, 40, 256), f(4, 4, 4, 40, 256),
            f(3, 4, 4, 16, 256), f(3, 4, 4, 24, 128), f(3, 4, 4, 24, 128),
            f(4, 4, 16, 256), f(4, 4, 24, 128), f(4, 4, 24, 128),
            f(4, 4, 16, 256), f(4, 4, 24, 128), f(4, 4, 24, 128),
            f(4, 16, 256), f(4, 24, 128), f(4, 24, 128),
            f(4, 16, 256), f(4, 24, 128), f(4, 24, 128),
            dma(PHASES), dma(PHASES), dma(1), dma(2), dma(2), dma(PHASES), dma(PHASES),
            dma(PHASES), dma(PHASES), dma(2), dma(2), dma(PHASES), dma(PHASES),
            dma(PHASES), dma(PHASES), dma(2), dma(4), dma(4), dma(3, 3), dma(3, 3), dma(3, 2), dma(3, 2),
        ],
        compiler_params=pltpu.CompilerParams(
            collective_id=0, has_side_effects=True, vmem_limit_bytes=VMEM_LIMIT
        ),
    )(lens, step, rates, x, g, b, c, p, li)


def deliver_kernel(x_hbm, p_ref, w_ref, xo_hbm, po_ref, wo_ref, hold, sems):
    def into(n):
        rows = pl.ds(n * PIECE, PIECE)
        return pltpu.make_async_copy(x_hbm.at[rows], hold.at[n], sems.at[0, n])

    def out(n):
        rows = pl.ds(n * PIECE, PIECE)
        return pltpu.make_async_copy(hold.at[n], xo_hbm.at[rows], sems.at[1, n])

    count = TOK // PIECE
    for n in range(count):
        into(n).start()
    po_ref[...] = p_ref[...]
    wo_ref[...] = w_ref[...]
    for n in range(count):
        into(n).wait()
        out(n).start()
    for n in range(count):
        out(n).wait()


PIECE = 96


def deliver(x, p, w):
    v = pl.BlockSpec(memory_space=pltpu.VMEM)
    a = pl.BlockSpec(memory_space=pl.ANY)
    return pl.pallas_call(
        deliver_kernel,
        in_specs=[a, v, v],
        out_specs=[a, v, v],
        out_shape=[jax.ShapeDtypeStruct(t.shape, t.dtype) for t in (x, p, w)],
        scratch_shapes=[
            pltpu.VMEM((TOK // PIECE, PIECE, WIDTH), BF16), pltpu.SemaphoreType.DMA((2, TOK // PIECE))
        ],
        compiler_params=pltpu.CompilerParams(vmem_limit_bytes=16 * 1024 * 1024),
    )(x, p, w)


def body(li, x, g, b, c, step, rates, prompt, lens):
    li, x, g, b, c, step, prompt = li[0], x[0], g[0], b[0], c[0], step[0], prompt[0]
    x_grad, prompt_grad, weight_grad = layer(
        lens, step, rates.reshape(1, HEADS), x, g, b, c, prompt, li
    )
    x_grad, prompt_grad, weight_grad = deliver(x_grad, prompt_grad, weight_grad)
    return x_grad[None], prompt_grad[None], weight_grad


def solution(mesh):
    in_specs = (
        P("group", "seq", None),
        P("group", "seq", None),
        P("group", "seq", None),
        P("group", "seq", None),
        P("group", "seq", None),
        P("group", None, "seq"),
        P(),
        P("group", "seq", None),
        P("group", None),
    )
    out_specs = (P("group", "seq", None), P("group", "seq", None), P(("group", "seq"), None))
    return jax.shard_map(body, mesh=mesh, in_specs=in_specs, out_specs=out_specs, check_vma=False)
```

```python
from functools import partial

import jax
import jax.numpy as jnp
from jax import lax
from jax.experimental import pallas as pl
from jax.experimental.pallas import tpu as pltpu
from jax.sharding import PartitionSpec as P

BLOCK = 256
NBLK = 3
TOK = BLOCK * NBLK
HEADS = 40
STATE = 128
WIDTH = 2560
DMODEL = 5120
PHASES = 5
PHEADS = HEADS // PHASES
PLANES = PHEADS * 64
PPAIRS = PHEADS // 2
ROWS = ((0, 16), (16, 40), (16, 40))
COLS = ((0, 256), (0, 128), (128, 256))
SLAB = 640
F32 = jnp.float32
BF16 = jnp.bfloat16
MESH = pl.DeviceIdType.MESH
NN = (((1,), (0,)), ((), ()))
TN = (((0,), (0,)), ((), ()))
NT = (((1,), (1,)), ((), ()))
LOG2E = 1.4426950408889634
VMEM_LIMIT = 62 * 1024 * 1024


def dot(a, b, dims=NN):
    return lax.dot_general(a, b, dims, preferred_element_type=F32)


def iota(shape, dim):
    return lax.broadcasted_iota(jnp.int32, shape, dim)


def flags(lens_ref):
    first = lax.axis_index("seq") * NBLK
    e1 = lens_ref[0, 0]
    e2 = e1 + lens_ref[0, 1]
    e3 = e2 + lens_ref[0, 2]
    e4 = e3 + lens_ref[0, 3]
    not_start, not_last = [], []
    for k in range(NBLK):
        at = first + k
        start = (at == 0) | (at == e1) | (at == e2) | (at == e3)
        last = (at == e1 - 1) | (at == e2 - 1) | (at == e3 - 1) | (at == e4 - 1)
        not_start.append(jnp.where(start, 0.0, 1.0).astype(F32))
        not_last.append(jnp.where(last, 0.0, 1.0).astype(F32))
    return not_start, not_last


def blockrows(k):
    return slice(BLOCK * k, BLOCK * (k + 1))


def gather(table, index):
    return jnp.take_along_axis(table, index, axis=1)


def half_heads(pair, rows):
    return 2 * pair + iota((rows, 128), 1) // 64


def prepare(step_ref, rate_ref, la_v, t1_v, t1b_v, t2b_v):
    step = step_ref[...]
    same = iota((HEADS, HEADS), 0) == iota((HEADS, HEADS), 1)
    spread = jnp.broadcast_to(rate_ref[...], (HEADS, HEADS))
    rate = jnp.sum(jnp.where(same, spread, 0.0), axis=1, keepdims=True)
    la = -step * rate
    place = iota((HEADS, TOK), 1) % BLOCK
    shift = 1
    while shift < BLOCK:
        la = la + jnp.where(place >= shift, pltpu.roll(la, shift, 1), 0.0)
        shift *= 2
    la = la * LOG2E
    la_v[...] = la
    ends = [la[:, BLOCK * (k + 1) - 1 : BLOCK * (k + 1)] for k in range(NBLK)]
    end = jnp.concatenate([jnp.broadcast_to(e, (HEADS, BLOCK)) for e in ends], axis=1)
    empty = jnp.zeros((8, TOK), F32)
    t1 = jnp.concatenate([la, step, jnp.exp2(end - la) * step, empty], axis=0).T
    t1_v[...] = t1
    t1b_v[...] = halves(t1)
    t2b_v[...] = halves(jnp.concatenate([jnp.exp2(la), jnp.zeros((88, TOK), F32)], axis=0).T)


def device_coefficients(ns, nl, t1_v):
    dec = [jnp.exp2(t1_v[BLOCK * (k + 1) - 1 : BLOCK * (k + 1), :]) for k in range(NBLK)]
    af = ab = jnp.ones((1, 128), F32)
    pc = jnp.zeros((1, 128), F32)
    for k in range(NBLK):
        af = af * (dec[k] * ns[k])
        pc = dec[k] * (pc * ns[k] + (1.0 - ns[k]))
        ab = ab * (dec[k] * nl[k])
    rows = jnp.concatenate([af, pc, ab, jnp.zeros((5, 128), F32)], axis=0)
    return jnp.where(iota((8, 128), 1) < HEADS, rows, 0.0)


def halves(table):
    high = table.astype(BF16)
    return jnp.concatenate([high, (table - high.astype(F32)).astype(BF16)], axis=1)


def selector(first):
    row, lane = iota((256, PLANES), 0), iota((256, PLANES), 1)
    return jnp.where(row % 128 == first + lane // 64, 1.0, 0.0).astype(BF16)


def phase_decays(la_v, j):
    la = la_v[pl.ds(pl.multiple_of(PHEADS * j, PHEADS), PHEADS), :]
    out = []
    for k in range(NBLK):
        at = BLOCK * (k + 1) - 1
        out.append(jnp.broadcast_to(jnp.exp2(la[:, at : at + 1]), (PHEADS, 128))[:, None, :])
    return out


def summarize(j, ns, nl, xg_v, b_ref, c_ref, la_v, t1b_v, t2b_v, sx_v, sg_v, loc_v, mine):
    ls, lg = [], []
    for k in range(NBLK):
        rows = blockrows(k)
        sx, sg = [], []
        ex = dot(t1b_v[rows, :], selector(2 * HEADS + PHEADS * j))
        eg = dot(t2b_v[rows, :], selector(PHEADS * j))
        for p in range(PPAIRS):
            lanes = pl.ds(pl.multiple_of(PLANES * j + 128 * p, 128), 128)
            heads = half_heads(PPAIRS * j + p, BLOCK)
            wx, wg = ex[:, 128 * p : 128 * (p + 1)], eg[:, 128 * p : 128 * (p + 1)]
            sx.append((xg_v[0, rows, lanes].astype(F32) * wx).astype(BF16))
            sg.append((xg_v[1, rows, lanes].astype(F32) * wg).astype(BF16))
            sx_v[rows, lanes] = sx[p]
            sg_v[rows, lanes] = sg[p]
        ls.append(dot(jnp.concatenate(sx, axis=1), b_ref[rows, :], TN).reshape(PHEADS, 64, 128))
        lg.append(dot(jnp.concatenate(sg, axis=1), c_ref[rows, :], TN).reshape(PHEADS, 64, 128))
    for n, value in enumerate((ls[0], ls[1], lg[0], lg[1], lg[2])):
        loc_v[j, n] = value
    dec = phase_decays(la_v, j)
    f = ls[0]
    for k in range(1, NBLK):
        f = (dec[k] * ns[k]) * f + ls[k]
    r = lg[2]
    for k in (1, 0):
        r = (dec[k] * nl[k]) * r + lg[k]
    mine[j, :, :, 0:16, :] = f.reshape(16, 2, 16, 128)
    mine[j, :, :, 16:32, :] = r.reshape(16, 2, 16, 128)


def inside_unit(j, k, xg_v, la_v, t1_v, inner_v, pt_v, dx_v):
    r = pl.ds(pl.multiple_of(k * BLOCK, BLOCK), BLOCK)
    table = t1_v[r, :]
    lane = iota((1, 128), 1)
    masks = [jnp.where((lane >= 64) == bool(n), 1.0, 0.0).astype(BF16) for n in range(2)]
    a00, a01, a11 = [], [], []
    for m in range(PPAIRS):
        pair = PPAIRS * j + m
        l = pl.ds(pl.multiple_of(pair * 128, 128), 128)
        g = xg_v[1, r, l]
        xs = (xg_v[0, r, l].astype(F32) * gather(table, half_heads(pair, BLOCK) + HEADS)).astype(BF16)
        gs = [g * m for m in masks]
        low = jnp.concatenate([gs[0][128:], gs[1][128:]], axis=0)
        p0 = dot(jnp.concatenate([xs[:128] * masks[0], xs[:128] * masks[1]], axis=0), g, NT)
        p1 = dot(xs[128:], low, NT)
        w11, d0 = [], []
        for n in range(2):
            row = la_v[pl.ds(2 * pair + n, 1), r]
            col = gather(table, jnp.full((BLOCK, 128), 2 * pair + n, jnp.int32))
            pn = p0[128 * n : 128 * (n + 1)]
            q00 = jnp.exp2(jnp.minimum(row[:, :128] - col[:128], 0.0))
            q01 = jnp.exp2(jnp.minimum(row[:, 128:] - col[:128], 0.0))
            q11 = jnp.exp2(jnp.minimum(row[:, 128:] - col[128:], 0.0))
            a00.append(q00 * pn[:, :128])
            a01.append(q01 * pn[:, 128:])
            a11.append(q11 * p1[:, 128 * n : 128 * (n + 1)])
            w00 = (q00 * inner_v[k, :128, :128]).astype(BF16)
            w01 = (q01 * inner_v[k, :128, 128:]).astype(BF16)
            w11.append((q11 * inner_v[k, 128:, 128:]).astype(BF16))
            d0.append(dot(jnp.concatenate([w00, w01], axis=1), gs[n]))
        d1 = dot(jnp.concatenate(w11, axis=1), low)
        dx_v[r, l] = jnp.concatenate([d0[0] + d0[1], d1], axis=0).astype(BF16)
    pt_v[k, :128, :128] += sum(a00[1:], a00[0])
    pt_v[k, :128, 128:] += sum(a01[1:], a01[0])
    pt_v[k, 128:, 128:] += sum(a11[1:], a11[0])


def gradients(j, ns, nl, b_ref, la_v, t1b_v, sx_v, sg_v, loc_v, prompt, el_v, dx_v, acc_v):
    dec = phase_decays(la_v, j)
    el = el_v[j]
    shape = (PHEADS, 64, 128)
    prompt = prompt.reshape(shape)
    state = el[:, :, 0:16].reshape(shape)
    entering = []
    for k in range(NBLK):
        state = state * ns[k] + prompt * (1.0 - ns[k])
        entering.append(state.reshape(PLANES, 128).astype(BF16))
        if k < NBLK - 1:
            state = dec[k] * state + loc_v[j, k]
    state = el[:, :, 16:32].reshape(shape)
    leaving = [None] * NBLK
    total = None
    for k in reversed(range(NBLK)):
        state = state * nl[k]
        leaving[k] = state.reshape(PLANES, 128).astype(BF16)
        state = dec[k] * state + loc_v[j, 2 + k]
        at_start = state * (1.0 - ns[k])
        total = at_start if total is None else total + at_start
    lanes = pl.ds(pl.multiple_of(PLANES * j, PLANES), PLANES)
    for k in range(NBLK):
        rows = blockrows(k)
        outer = dot(b_ref[rows, :], leaving[k], NT)
        near_w = dot(t1b_v[rows, :], selector(HEADS + PHEADS * j))
        far_w = dot(t1b_v[rows, :], selector(2 * HEADS + PHEADS * j))
        for p in range(PPAIRS):
            cut = slice(128 * p, 128 * (p + 1))
            at = pl.ds(pl.multiple_of(PLANES * j + 128 * p, 128), 128)
            heads = half_heads(PPAIRS * j + p, BLOCK)
            near = near_w[:, cut] * dx_v[rows, at].astype(F32)
            far = far_w[:, cut] * outer[:, cut]
            dx_v[rows, at] = (near + far).astype(BF16)
        acc_v[rows, :128] += dot(sx_v[rows, lanes], leaving[k])
        acc_v[rows, 128:] += dot(sg_v[rows, lanes], entering[k])
    return total.reshape(32, 16, 128)


TICKS = PHASES + 8


def layer_kernel(
    lens_ref, step_ref, rate_ref, x_hbm, g_hbm, b_ref, c_ref, p_ref, li_hbm,
    xg_hbm, pg_ref, wg_ref,
    xg_v, dx_v, sx_v, sg_v, la_v, t1_v, t1b_v, t2b_v, inner_v, pt_v, acc_v, loc_v, bc_v,
    cf_mine, cf_sib, cf_chip, cf_all, mine, sib_in, comb, got, back, ret, sib_out, el_v, prompts,
    pterm, sib_p, pr1a, pr1b, ps1a, ps1b, pr2a, pr2b,
    part, sib, r1a, r1b, r1c, s1a, s1b, s1c, r2a, r2b, r2c, s2a, s2b, s2c, r3a, r3b, r3c,
    x_sem, g_sem, o_sem, c_send, c_recv, f_send, f_recv, l_send, l_recv, p_send, p_recv,
    a_send, a_recv, b_send, b_recv, li_sem, s_send, s_recv, w_send, w_recv, q_send, q_recv,
):
    group, seq = lax.axis_index("group"), lax.axis_index("seq")
    core = seq % 2
    chip = seq // 2
    y, z = chip // 4, chip % 4
    sibling = (group, chip * 2 + (1 - core))
    is0 = core == 0

    def chip_at(d):
        return ((y + d // 4) % 4) * 4 + (z + d % 4) % 4

    def in_plane(d):
        return (group, chip_at(d) * 2 + core)

    def to_x(d):
        return ((group + d) % 4, seq)

    def to_y(d):
        return in_plane(4 * d)

    def to_z(d):
        return in_plane(d)

    def send(src, dst, s, r, to):
        return pltpu.make_async_remote_copy(
            src_ref=src, dst_ref=dst, send_sem=s, recv_sem=r, device_id=to, device_id_type=MESH
        )

    def lanes(j):
        return pl.ds(pl.multiple_of(PLANES * j, PLANES), PLANES)

    def load_x(j):
        return pltpu.make_async_copy(x_hbm.at[:, lanes(j)], xg_v.at[0, :, lanes(j)], x_sem.at[j])

    def load_g(j):
        return pltpu.make_async_copy(g_hbm.at[:, lanes(j)], xg_v.at[1, :, lanes(j)], g_sem.at[j])

    def load_li(n):
        return pltpu.make_async_copy(li_hbm.at[:, WIDTH * n : WIDTH * (n + 1)], xg_v.at[n], li_sem.at[n])

    def store(j):
        return pltpu.make_async_copy(dx_v.at[:, lanes(j)], xg_hbm.at[:, lanes(j)], o_sem.at[0])

    def each(lo, hi, f):
        def step(i, _):
            f(i)
            return 0

        lax.fori_loop(lo, hi, step, 0)

    def begin(j):
        load_x(j).start()
        load_g(j).start()

    each(0, PHASES, begin)

    barrier = pltpu.get_barrier_semaphore()

    def greet(to):
        pl.semaphore_signal(barrier, inc=1, device_id=to, device_id_type=MESH)

    greet(sibling)
    each(1, 16, lambda d: greet(in_plane(d)))
    each(1, 4, lambda d: greet(to_x(d)))

    prepare(step_ref, rate_ref, la_v, t1_v, t1b_v, t2b_v)
    ns, nl = flags(lens_ref)
    cf_mine[...] = device_coefficients(ns, nl, t1_v)

    def start_phase(t):
        load_x(t).wait()
        load_g(t).wait()
        summarize(t, ns, nl, xg_v, b_ref, c_ref, la_v, t1b_v, t2b_v, sx_v, sg_v, loc_v, mine)

    start_phase(0)
    pl.semaphore_wait(barrier, 19)

    def prompt_copy(d):
        return send(p_ref, prompts.at[chip, core], p_send.at[1], p_recv.at[1], in_plane(d))

    def prompt_all():
        some = prompts.at[pl.ds(0, 15), 0]
        return send(some, some, p_send.at[1], p_recv.at[1], sibling)

    def prompt_pass():
        half = prompts.at[:, core]
        return send(half, half, p_send.at[0], p_recv.at[0], sibling)

    def coefficient_pass():
        return send(cf_mine, cf_sib, c_send.at[0], c_recv.at[0], sibling)

    def coefficient_copy(d):
        return send(cf_chip, cf_all.at[chip], c_send.at[1], c_recv.at[1], in_plane(d))

    def coefficient_all():
        some = cf_all.at[pl.ds(0, 15)]
        return send(some, some, c_send.at[1], c_recv.at[1], sibling)

    def chip_copy(j):
        return send(mine.at[j, :, 1 - core], sib_in.at[j], f_send.at[j], f_recv.at[j], sibling)

    def out_copy(j, d):
        return send(comb.at[j, chip_at(d)], got.at[j, chip], a_send.at[j], a_recv.at[j], in_plane(d))

    def out_all(j):
        some = pl.ds(0, 15)
        return send(comb.at[j, some], got.at[j, some], a_send.at[j], a_recv.at[j], sibling)

    def back_copy(j, d):
        return send(back.at[j, chip_at(d)], ret.at[j, chip], b_send.at[j], b_recv.at[j], in_plane(d))

    def back_all(j):
        some = pl.ds(0, 15)
        return send(back.at[j, some], ret.at[j, some], b_send.at[j], b_recv.at[j], sibling)

    def last_copy(j):
        return send(sib_out.at[j], el_v.at[j, :, core], l_send.at[j], l_recv.at[j], sibling)

    coefficient_pass().start()
    chip_copy(0).start()
    each(1, 16, lambda d: prompt_copy(d).start())
    prompts[chip, core] = p_ref[...]

    def pick(a, b):
        return jnp.where(is0, a, b), jnp.where(is0, b, a)

    def both(j):
        heads = PHEADS * j + iota((16, 128), 0) // 2

        def spread(tile):
            return [
                gather(jnp.broadcast_to(tile[n : n + 1], (16, 128)), heads)[:, None, :] for n in range(3)
            ]

        a, b = pick(mine[j, :, core], sib_in[j])
        t0, t1 = pick(cf_mine[...], cf_sib[...])
        return a, b, spread(t0), spread(t1)

    def combine(j):
        a, b, (_, _, ab0), (af1, _, _) = both(j)
        comb[j, :, 0:16, :] = b[:, 0:16] + af1 * a[:, 0:16]
        comb[j, :, 16:32, :] = a[:, 16:32] + ab0 * b[:, 16:32]

    def piece(j, owner):
        at = 32 * j + owner
        return at // 10, (at // 5) % 2, pl.ds(pl.multiple_of(16 * (at % 5), 16), 16)

    def prompt_rows(j, owner):
        a, b, rows = piece(j, owner)
        return prompts[a, b, rows, :]

    def scan(j):
        own = prompt_rows(j, seq)
        head = jnp.full((128, 128), PHEADS * j + seq // 4, jnp.int32)
        cf = gather(cf_all[...].reshape(128, 128), head)
        e = jnp.zeros((16, 128), F32)
        for q in range(16):
            back[j, q, 0:16, :] = e
            e = cf[8 * q : 8 * q + 1] * e + (cf[8 * q + 1 : 8 * q + 2] * own + got[j, q, 0:16, :])
        lv = jnp.zeros((16, 128), F32)
        for q in reversed(range(16)):
            back[j, q, 16:32, :] = lv
            lv = cf[8 * q + 2 : 8 * q + 3] * lv + got[j, q, 16:32, :]

    def finish(j):
        a, b, (af0, pc0, _), (_, _, ab1) = both(j)
        e0, l1 = ret[j, :, 0:16, :], ret[j, :, 16:32, :]
        prompt = jnp.stack([prompt_rows(j, 2 * q + core) for q in range(16)], axis=0)
        e1 = af0 * e0 + (pc0 * prompt + a[:, 0:16])
        l0 = ab1 * l1 + b[:, 16:32]
        e_mine, e_other = pick(e0, e1)
        l_mine, l_other = pick(l0, l1)
        el_v[j, :, core, 0:16, :] = e_mine
        el_v[j, :, core, 16:32, :] = l_mine
        sib_out[j, :, 0:16, :] = e_other
        sib_out[j, :, 16:32, :] = l_other

    keep = iota((BLOCK, BLOCK), 1) >= iota((BLOCK, BLOCK), 0)

    def tick(t):
        @pl.when(t < PHASES)
        def _():
            start_phase(t)
            chip_copy(t).start()

        @pl.when(t == 1)
        def _():
            coefficient_pass().wait()
            t0, t1 = pick(cf_mine[...], cf_sib[...])
            cf_chip[...] = jnp.concatenate(
                [t0[0:1] * t1[0:1], t1[1:2] + t1[0:1] * t0[1:2], t0[2:3] * t1[2:3], t0[3:8]], axis=0
            )
            each(1, 16, lambda d: coefficient_copy(d).start())
            cf_all[chip] = cf_chip[...]

        @pl.when(t < PHASES + 1)
        def _():
            j = t - 1
            chip_copy(j).wait()
            combine(j)
            each(1, 16, lambda d: out_copy(j, d).start())
            got[j, chip] = comb[j, chip]

        @pl.when(t == 2)
        def _():
            prompt_all().wait()
            prompt_pass().start()

        @pl.when(t == 3)
        def _():
            prompt_pass().wait()
            coefficient_all().wait()

        @pl.when(t == 4)
        def _():
            for k in range(NBLK):
                rows = blockrows(k)
                inner_v[k] = jnp.where(keep, dot(b_ref[rows, :], c_ref[rows, :], NT), 0.0)
                pt_v[k] = jnp.zeros((BLOCK, BLOCK), F32)
            acc_v[...] = jnp.zeros_like(acc_v)

        @pl.when((t >= 5) & (t < PHASES + 5))
        def _():
            each(0, NBLK, lambda k: inside_unit(t - 5, k, xg_v, la_v, t1_v, inner_v, pt_v, dx_v))

        @pl.when((t >= 4) & (t < PHASES + 4))
        def _():
            j = t - 4
            out_all(j).wait()
            scan(j)
            each(1, 16, lambda d: back_copy(j, d).start())
            ret[j, chip] = back[j, chip]

        @pl.when(t == PHASES + 4)
        def _():
            for n in range(2):
                load_li(n).start()

        @pl.when((t >= 7) & (t < PHASES + 7))
        def _():
            j = t - 7
            back_all(j).wait()
            finish(j)
            last_copy(j).start()

        @pl.when(t >= 8)
        def _():
            j = t - 8
            last_copy(j).wait()
            prompt = jnp.stack([prompt_rows(j, o) for o in range(32)], axis=0)
            total = gradients(j, ns, nl, b_ref, la_v, t1b_v, sx_v, sg_v, loc_v, prompt, el_v, dx_v, acc_v)
            store(j).start()
            for o in range(32):
                a, b, rows = piece(j, o)
                pterm[a // 4, a % 4, b, rows, :] = total[o]

    each(1, TICKS, tick)

    def p_copy(n, stage, d, src, dst, to):
        return send(src, dst, q_send.at[n, stage], q_recv.at[n, stage], to)

    def p_chip():
        return p_copy(2, 0, 0, pterm.at[:, :, 1 - core], sib_p, sibling)

    def p_first(n, d):
        if n == 0:
            return p_copy(n, 0, d, pterm.at[(y + d) % 4, :, core, 0:40], pr1a.at[d], to_y(d))
        return p_copy(n, 0, d, pterm.at[:, (z + d) % 4, core, 40:80], pr1b.at[d], to_z(d))

    def p_second(n, d):
        if n == 0:
            return p_copy(n, 1, d, ps1a.at[(z + d) % 4], pr2a.at[d], to_z(d))
        return p_copy(n, 1, d, ps1b.at[(y + d) % 4], pr2b.at[d], to_y(d))

    p_chip().start()
    for k in range(NBLK):
        rows = blockrows(k)
        pt = jnp.where(keep, pt_v[k], 0.0).astype(BF16)
        bc_v[rows, :128] = (acc_v[rows, :128] + dot(pt, c_ref[rows, :])).astype(BF16)
        bc_v[rows, 128:] = (acc_v[rows, 128:] + dot(pt, b_ref[rows, :], TN)).astype(BF16)
    def w_copy(n, stage, d, src, dst, to):
        return send(src, dst, w_send.at[n, stage], w_recv.at[n, stage], to)

    def cut(n):
        return pl.ds(ROWS[n][0], ROWS[n][1] - ROWS[n][0]), pl.ds(COLS[n][0], COLS[n][1] - COLS[n][0])

    def slab_x(s):
        return (group + s) % 4

    def sib_copy(s, n):
        at = slab_x(s)
        return send(
            part.at[at, pl.ds(2 * n, 2), :, 1 - core], sib.at[at, pl.ds(2 * n, 2)],
            s_send.at[s], s_recv.at[s], sibling,
        )

    def sib_all(s):
        at = slab_x(s)
        return send(part.at[at, :, :, 1 - core], sib.at[at], s_send.at[s], s_recv.at[s], sibling)

    def first_x(d):
        return w_copy(0, 0, d, part.at[slab_x(d), :, :, core, *cut(0)], r1a.at[d - 1], to_x(d))

    def first_y(s, d):
        at = slab_x(s)
        return send(
            part.at[at, (y + d) % 4, :, core, *cut(1)], r1b.at[d - 1, at],
            w_send.at[1, 0], w_recv.at[1, 0], to_y(d),
        )

    def first_z(s, d):
        at = slab_x(s)
        return send(
            part.at[at, :, (z + d) % 4, core, *cut(2)], r1c.at[d - 1, at],
            w_send.at[2, 0], w_recv.at[2, 0], to_z(d),
        )

    def settle(s):
        at = slab_x(s)
        sib_all(s).wait()
        part[at, :, :, core] = part[at, :, :, core] + sib[at]
        if s > 0:
            first_x(s).start()
        for d in (1, 3, 2):
            first_y(s, d).start()
            first_z(s, d).start()

    for n in range(2):
        load_li(n).wait()
    bc = bc_v[...]
    order = (1, 3, 2, 0)
    for i, s in enumerate(order):
        at = slab_x(s)
        for n in range(2):
            m = at * 2 + n
            cols = pl.ds(pl.multiple_of(SLAB * (m % 4), SLAB), SLAB)
            out = dot(xg_v[m // 4, :, cols], bc, TN)
            part[at, 2 * n : 2 * n + 2] = out.reshape(2, 4, 2, 40, 256)
            sib_copy(s, n).start()
        if i == 0:
            p_chip().wait()
            pterm[:, :, core] = pterm[:, :, core] + sib_p[...]
            for d in (1, 3, 2):
                for q in range(2):
                    p_first(q, d).start()
        else:
            settle(order[i - 1])
    settle(0)

    def second(n, d):
        if n == 0:
            return w_copy(n, 1, d, s1a.at[(y + d) % 4], r2a.at[d], to_y(d))
        if n == 1:
            return w_copy(n, 1, d, s1b.at[:, (z + d) % 4], r2b.at[d], to_z(d))
        return w_copy(n, 1, d, s1c.at[(group + d) % 4], r2c.at[d], to_x(d))

    def third(n, d):
        if n == 0:
            return w_copy(n, 2, d, s2a.at[(z + d) % 4], r3a.at[d], to_z(d))
        if n == 1:
            return w_copy(n, 2, d, s2b.at[(group + d) % 4], r3b.at[d], to_x(d))
        return w_copy(n, 2, d, s2c.at[(y + d) % 4], r3c.at[d], to_y(d))

    three = pl.ds(1, 3)
    peers = pl.ds(0, 3)
    p_copy(0, 0, 1, pterm.at[peers, :, 0, 0:40], pr1a.at[three], sibling).wait()
    p_copy(1, 0, 1, pterm.at[peers, :, 0, 40:80], pr1b.at[three], sibling).wait()
    ps1a[...] = pterm[y, :, core, 0:40] + pr1a[1] + pr1a[2] + pr1a[3]
    ps1b[...] = pterm[:, z, core, 40:80] + pr1b[1] + pr1b[2] + pr1b[3]
    for d in (1, 3, 2):
        for n in range(2):
            p_second(n, d).start()

    for n in range(3):
        if n == 0:
            w_copy(0, 0, 1, r1a, r1a, sibling).wait()
            s1a[...] = part[group, :, :, core, 0:16] + r1a[0] + r1a[1] + r1a[2]
        elif n == 1:
            w_copy(1, 0, 1, r1b, r1b, sibling).wait()
            s1b[...] = part[:, y, :, core, 16:40, 0:128] + r1b[0] + r1b[1] + r1b[2]
        else:
            w_copy(2, 0, 1, r1c, r1c, sibling).wait()
            s1c[...] = part[:, :, z, core, 16:40, 128:256] + r1c[0] + r1c[1] + r1c[2]
        for d in (1, 3, 2):
            second(n, d).start()
    for n, r in enumerate((r2a, r2b, r2c)):
        w_copy(n, 1, 1, r.at[three], r.at[three], sibling).wait()
        if n == 0:
            s2a[...] = s1a[y] + r2a[1] + r2a[2] + r2a[3]
        elif n == 1:
            s2b[...] = s1b[:, z] + r2b[1] + r2b[2] + r2b[3]
        else:
            s2c[...] = s1c[group] + r2c[1] + r2c[2] + r2c[3]
        for d in (1, 3, 2):
            third(n, d).start()
    p_copy(0, 1, 1, pr2a.at[three], pr2a.at[three], sibling).wait()
    p_copy(1, 1, 1, pr2b.at[three], pr2b.at[three], sibling).wait()
    pg_ref[0:40, :] = ps1a[z] + pr2a[1] + pr2a[2] + pr2a[3]
    pg_ref[40:80, :] = ps1b[y] + pr2b[1] + pr2b[2] + pr2b[3]
    for n, (own, r, at) in enumerate(((s2a, r3a, z), (s2b, r3b, group), (s2c, r3c, y))):
        w_copy(n, 2, 1, r.at[three], r.at[three], sibling).wait()
        wg_ref[ROWS[n][0] : ROWS[n][1], COLS[n][0] : COLS[n][1]] = own[at] + r[1] + r[2] + r[3]
    pltpu.make_async_copy(dx_v, xg_hbm, o_sem.at[0]).wait()


def layer(lens, step, rates, x, g, b, c, p, li):
    v = pl.BlockSpec(memory_space=pltpu.VMEM)
    a = pl.BlockSpec(memory_space=pl.ANY)
    wide = pltpu.VMEM((TOK, WIDTH), BF16)
    square = pltpu.VMEM((NBLK, BLOCK, BLOCK), F32)
    f = lambda *shape: pltpu.VMEM(shape, F32)
    dma = lambda *n: pltpu.SemaphoreType.DMA(n)
    half = f(PHASES, 16, 32, 128)
    return pl.pallas_call(
        layer_kernel,
        in_specs=[pl.BlockSpec(memory_space=pltpu.SMEM), v, v, a, a, v, v, v, a],
        out_specs=[a, v, v],
        out_shape=[
            jax.ShapeDtypeStruct((TOK, WIDTH), BF16),
            jax.ShapeDtypeStruct((80, 128), F32),
            jax.ShapeDtypeStruct((40, 256), F32),
        ],
        scratch_shapes=[
            pltpu.VMEM((2, TOK, WIDTH), BF16), wide, wide, wide,
            f(HEADS, TOK), f(TOK, 128), pltpu.VMEM((TOK, 256), BF16), pltpu.VMEM((TOK, 256), BF16), square, square, f(TOK, 256),
            f(PHASES, 5, PHEADS, 64, 128), pltpu.VMEM((TOK, 256), BF16),
            f(8, 128), f(8, 128), f(8, 128), f(16, 8, 128),
            f(PHASES, 16, 2, 32, 128), half, half, half, half, half, half,
            f(PHASES, 16, 2, 32, 128), f(16, 2, 80, 128),
            f(4, 4, 2, 80, 128), f(4, 4, 80, 128), f(4, 4, 40, 128), f(4, 4, 40, 128),
            f(4, 40, 128), f(4, 40, 128), f(4, 40, 128), f(4, 40, 128),
            f(4, 4, 4, 2, 40, 256), f(4, 4, 4, 40, 256),
            f(3, 4, 4, 16, 256), f(3, 4, 4, 24, 128), f(3, 4, 4, 24, 128),
            f(4, 4, 16, 256), f(4, 4, 24, 128), f(4, 4, 24, 128),
            f(4, 4, 16, 256), f(4, 4, 24, 128), f(4, 4, 24, 128),
            f(4, 16, 256), f(4, 24, 128), f(4, 24, 128),
            f(4, 16, 256), f(4, 24, 128), f(4, 24, 128),
            dma(PHASES), dma(PHASES), dma(1), dma(2), dma(2), dma(PHASES), dma(PHASES),
            dma(PHASES), dma(PHASES), dma(2), dma(2), dma(PHASES), dma(PHASES),
            dma(PHASES), dma(PHASES), dma(2), dma(4), dma(4), dma(3, 3), dma(3, 3), dma(3, 2), dma(3, 2),
        ],
        compiler_params=pltpu.CompilerParams(
            collective_id=0, has_side_effects=True, vmem_limit_bytes=VMEM_LIMIT
        ),
    )(lens, step, rates, x, g, b, c, p, li)


def deliver_kernel(x_hbm, p_ref, w_ref, xo_hbm, po_ref, wo_ref, hold, sems):
    def into(n):
        rows = pl.ds(n * PIECE, PIECE)
        return pltpu.make_async_copy(x_hbm.at[rows], hold.at[n], sems.at[0, n])

    def out(n):
        rows = pl.ds(n * PIECE, PIECE)
        return pltpu.make_async_copy(hold.at[n], xo_hbm.at[rows], sems.at[1, n])

    count = TOK // PIECE
    for n in range(count):
        into(n).start()
    po_ref[...] = p_ref[...]
    wo_ref[...] = w_ref[...]
    for n in range(count):
        into(n).wait()
        out(n).start()
    for n in range(count):
        out(n).wait()


PIECE = 96


def deliver(x, p, w):
    v = pl.BlockSpec(memory_space=pltpu.VMEM)
    a = pl.BlockSpec(memory_space=pl.ANY)
    return pl.pallas_call(
        deliver_kernel,
        in_specs=[a, v, v],
        out_specs=[a, v, v],
        out_shape=[jax.ShapeDtypeStruct(t.shape, t.dtype) for t in (x, p, w)],
        scratch_shapes=[
            pltpu.VMEM((TOK // PIECE, PIECE, WIDTH), BF16), pltpu.SemaphoreType.DMA((2, TOK // PIECE))
        ],
        compiler_params=pltpu.CompilerParams(vmem_limit_bytes=VMEM_LIMIT),
    )(x, p, w)


def body(li, x, g, b, c, step, rates, prompt, lens):
    li, x, g, b, c, step, prompt = li[0], x[0], g[0], b[0], c[0], step[0], prompt[0]
    x_grad, prompt_grad, weight_grad = layer(
        lens, step, rates.reshape(1, HEADS), x, g, b, c, prompt, li
    )
    x_grad, prompt_grad, weight_grad = deliver(x_grad, prompt_grad, weight_grad)
    return x_grad[None], prompt_grad[None], weight_grad


def solution(mesh):
    in_specs = (
        P("group", "seq", None),
        P("group", "seq", None),
        P("group", "seq", None),
        P("group", "seq", None),
        P("group", "seq", None),
        P("group", None, "seq"),
        P(),
        P("group", "seq", None),
        P("group", None),
    )
    out_specs = (P("group", "seq", None), P("group", "seq", None), P(("group", "seq"), None))
    return jax.shard_map(body, mesh=mesh, in_specs=in_specs, out_specs=out_specs, check_vma=False)
```

```python
from functools import partial

import jax
import jax.numpy as jnp
from jax import lax
from jax.experimental import pallas as pl
from jax.experimental.pallas import tpu as pltpu
from jax.sharding import PartitionSpec as P

BLOCK = 256
NBLK = 3
TOK = BLOCK * NBLK
HEADS = 40
STATE = 128
WIDTH = 2560
DMODEL = 5120
PHASES = 5
PHEADS = HEADS // PHASES
PLANES = PHEADS * 64
PPAIRS = PHEADS // 2
ROWS = ((16, 40), (16, 40), (0, 16))
COLS = ((0, 128), (128, 256), (0, 256))
SLAB = 640
F32 = jnp.float32
BF16 = jnp.bfloat16
MESH = pl.DeviceIdType.MESH
NN = (((1,), (0,)), ((), ()))
TN = (((0,), (0,)), ((), ()))
NT = (((1,), (1,)), ((), ()))
LOG2E = 1.4426950408889634
VMEM_LIMIT = 62 * 1024 * 1024


def dot(a, b, dims=NN):
    return lax.dot_general(a, b, dims, preferred_element_type=F32)


def iota(shape, dim):
    return lax.broadcasted_iota(jnp.int32, shape, dim)


def flags(lens_ref):
    first = lax.axis_index("seq") * NBLK
    e1 = lens_ref[0, 0]
    e2 = e1 + lens_ref[0, 1]
    e3 = e2 + lens_ref[0, 2]
    e4 = e3 + lens_ref[0, 3]
    not_start, not_last = [], []
    for k in range(NBLK):
        at = first + k
        start = (at == 0) | (at == e1) | (at == e2) | (at == e3)
        last = (at == e1 - 1) | (at == e2 - 1) | (at == e3 - 1) | (at == e4 - 1)
        not_start.append(jnp.where(start, 0.0, 1.0).astype(F32))
        not_last.append(jnp.where(last, 0.0, 1.0).astype(F32))
    return not_start, not_last


def blockrows(k):
    return slice(BLOCK * k, BLOCK * (k + 1))


def gather(table, index):
    return jnp.take_along_axis(table, index, axis=1)


def half_heads(pair, rows):
    return 2 * pair + iota((rows, 128), 1) // 64


def prepare(step_ref, rate_ref, la_v, t1_v, t1b_v, t2b_v):
    step = step_ref[...]
    same = iota((HEADS, HEADS), 0) == iota((HEADS, HEADS), 1)
    spread = jnp.broadcast_to(rate_ref[...], (HEADS, HEADS))
    rate = jnp.sum(jnp.where(same, spread, 0.0), axis=1, keepdims=True)
    la = -step * rate
    place = iota((HEADS, TOK), 1) % BLOCK
    shift = 1
    while shift < BLOCK:
        la = la + jnp.where(place >= shift, pltpu.roll(la, shift, 1), 0.0)
        shift *= 2
    la = la * LOG2E
    la_v[...] = la
    ends = [la[:, BLOCK * (k + 1) - 1 : BLOCK * (k + 1)] for k in range(NBLK)]
    end = jnp.concatenate([jnp.broadcast_to(e, (HEADS, BLOCK)) for e in ends], axis=1)
    empty = jnp.zeros((8, TOK), F32)
    t1 = jnp.concatenate([la, step, jnp.exp2(end - la) * step, empty], axis=0).T
    t1_v[...] = t1
    t1b_v[...] = halves(t1)
    t2b_v[...] = halves(jnp.concatenate([jnp.exp2(la), jnp.zeros((88, TOK), F32)], axis=0).T)


def device_coefficients(ns, nl, t1_v):
    dec = [jnp.exp2(t1_v[BLOCK * (k + 1) - 1 : BLOCK * (k + 1), :]) for k in range(NBLK)]
    af = ab = jnp.ones((1, 128), F32)
    pc = jnp.zeros((1, 128), F32)
    for k in range(NBLK):
        af = af * (dec[k] * ns[k])
        pc = dec[k] * (pc * ns[k] + (1.0 - ns[k]))
        ab = ab * (dec[k] * nl[k])
    rows = jnp.concatenate([af, pc, ab, jnp.zeros((5, 128), F32)], axis=0)
    return jnp.where(iota((8, 128), 1) < HEADS, rows, 0.0)


def halves(table):
    high = table.astype(BF16)
    return jnp.concatenate([high, (table - high.astype(F32)).astype(BF16)], axis=1)


def selector(first):
    row, lane = iota((256, PLANES), 0), iota((256, PLANES), 1)
    return jnp.where(row % 128 == first + lane // 64, 1.0, 0.0).astype(BF16)


def phase_decays(la_v, j):
    la = la_v[pl.ds(pl.multiple_of(PHEADS * j, PHEADS), PHEADS), :]
    out = []
    for k in range(NBLK):
        at = BLOCK * (k + 1) - 1
        out.append(jnp.broadcast_to(jnp.exp2(la[:, at : at + 1]), (PHEADS, 128))[:, None, :])
    return out


def summarize(j, ns, nl, xg_v, b_ref, c_ref, la_v, t1b_v, t2b_v, sx_v, sg_v, loc_v, mine):
    ls, lg = [], []
    for k in range(NBLK):
        rows = blockrows(k)
        sx, sg = [], []
        ex = dot(t1b_v[rows, :], selector(2 * HEADS + PHEADS * j))
        eg = dot(t2b_v[rows, :], selector(PHEADS * j))
        for p in range(PPAIRS):
            lanes = pl.ds(pl.multiple_of(PLANES * j + 128 * p, 128), 128)
            heads = half_heads(PPAIRS * j + p, BLOCK)
            wx, wg = ex[:, 128 * p : 128 * (p + 1)], eg[:, 128 * p : 128 * (p + 1)]
            sx.append((xg_v[0, rows, lanes].astype(F32) * wx).astype(BF16))
            sg.append((xg_v[1, rows, lanes].astype(F32) * wg).astype(BF16))
            sx_v[rows, lanes] = sx[p]
            sg_v[rows, lanes] = sg[p]
        ls.append(dot(jnp.concatenate(sx, axis=1), b_ref[rows, :], TN).reshape(PHEADS, 64, 128))
        lg.append(dot(jnp.concatenate(sg, axis=1), c_ref[rows, :], TN).reshape(PHEADS, 64, 128))
    for n, value in enumerate((ls[0], ls[1], lg[0], lg[1], lg[2])):
        loc_v[j, n] = value
    dec = phase_decays(la_v, j)
    f = ls[0]
    for k in range(1, NBLK):
        f = (dec[k] * ns[k]) * f + ls[k]
    r = lg[2]
    for k in (1, 0):
        r = (dec[k] * nl[k]) * r + lg[k]
    mine[j, :, :, 0:16, :] = f.reshape(16, 2, 16, 128)
    mine[j, :, :, 16:32, :] = r.reshape(16, 2, 16, 128)


def inside_unit(j, k, xg_v, la_v, t1_v, inner_v, pt_v, dx_v):
    r = pl.ds(pl.multiple_of(k * BLOCK, BLOCK), BLOCK)
    table = t1_v[r, :]
    lane = iota((1, 128), 1)
    masks = [jnp.where((lane >= 64) == bool(n), 1.0, 0.0).astype(BF16) for n in range(2)]
    a00, a01, a11 = [], [], []
    for m in range(PPAIRS):
        pair = PPAIRS * j + m
        l = pl.ds(pl.multiple_of(pair * 128, 128), 128)
        g = xg_v[1, r, l]
        xs = (xg_v[0, r, l].astype(F32) * gather(table, half_heads(pair, BLOCK) + HEADS)).astype(BF16)
        gs = [g * m for m in masks]
        low = jnp.concatenate([gs[0][128:], gs[1][128:]], axis=0)
        p0 = dot(jnp.concatenate([xs[:128] * masks[0], xs[:128] * masks[1]], axis=0), g, NT)
        p1 = dot(xs[128:], low, NT)
        w11, d0 = [], []
        for n in range(2):
            row = la_v[pl.ds(2 * pair + n, 1), r]
            col = gather(table, jnp.full((BLOCK, 128), 2 * pair + n, jnp.int32))
            pn = p0[128 * n : 128 * (n + 1)]
            q00 = jnp.exp2(jnp.minimum(row[:, :128] - col[:128], 0.0))
            q01 = jnp.exp2(jnp.minimum(row[:, 128:] - col[:128], 0.0))
            q11 = jnp.exp2(jnp.minimum(row[:, 128:] - col[128:], 0.0))
            a00.append(q00 * pn[:, :128])
            a01.append(q01 * pn[:, 128:])
            a11.append(q11 * p1[:, 128 * n : 128 * (n + 1)])
            w00 = (q00 * inner_v[k, :128, :128]).astype(BF16)
            w01 = (q01 * inner_v[k, :128, 128:]).astype(BF16)
            w11.append((q11 * inner_v[k, 128:, 128:]).astype(BF16))
            d0.append(dot(jnp.concatenate([w00, w01], axis=1), gs[n]))
        d1 = dot(jnp.concatenate(w11, axis=1), low)
        dx_v[r, l] = jnp.concatenate([d0[0] + d0[1], d1], axis=0).astype(BF16)
    pt_v[k, :128, :128] += sum(a00[1:], a00[0])
    pt_v[k, :128, 128:] += sum(a01[1:], a01[0])
    pt_v[k, 128:, 128:] += sum(a11[1:], a11[0])


def gradients(j, ns, nl, b_ref, la_v, t1b_v, sx_v, sg_v, loc_v, prompt, el_v, dx_v, acc_v):
    dec = phase_decays(la_v, j)
    el = el_v[j]
    shape = (PHEADS, 64, 128)
    prompt = prompt.reshape(shape)
    state = el[:, :, 0:16].reshape(shape)
    entering = []
    for k in range(NBLK):
        state = state * ns[k] + prompt * (1.0 - ns[k])
        entering.append(state.reshape(PLANES, 128).astype(BF16))
        if k < NBLK - 1:
            state = dec[k] * state + loc_v[j, k]
    state = el[:, :, 16:32].reshape(shape)
    leaving = [None] * NBLK
    total = None
    for k in reversed(range(NBLK)):
        state = state * nl[k]
        leaving[k] = state.reshape(PLANES, 128).astype(BF16)
        state = dec[k] * state + loc_v[j, 2 + k]
        at_start = state * (1.0 - ns[k])
        total = at_start if total is None else total + at_start
    lanes = pl.ds(pl.multiple_of(PLANES * j, PLANES), PLANES)
    for k in range(NBLK):
        rows = blockrows(k)
        outer = dot(b_ref[rows, :], leaving[k], NT)
        near_w = dot(t1b_v[rows, :], selector(HEADS + PHEADS * j))
        far_w = dot(t1b_v[rows, :], selector(2 * HEADS + PHEADS * j))
        for p in range(PPAIRS):
            cut = slice(128 * p, 128 * (p + 1))
            at = pl.ds(pl.multiple_of(PLANES * j + 128 * p, 128), 128)
            heads = half_heads(PPAIRS * j + p, BLOCK)
            near = near_w[:, cut] * dx_v[rows, at].astype(F32)
            far = far_w[:, cut] * outer[:, cut]
            dx_v[rows, at] = (near + far).astype(BF16)
        acc_v[rows, :128] += dot(sx_v[rows, lanes], leaving[k])
        acc_v[rows, 128:] += dot(sg_v[rows, lanes], entering[k])
    return total.reshape(32, 16, 128)


TICKS = PHASES + 8


def layer_kernel(
    lens_ref, step_ref, rate_ref, x_hbm, g_hbm, b_ref, c_ref, p_ref, li_hbm,
    xg_hbm, pg_ref, wg_ref,
    xg_v, dx_v, sx_v, sg_v, la_v, t1_v, t1b_v, t2b_v, inner_v, pt_v, acc_v, loc_v, bc_v,
    cf_mine, cf_sib, cf_chip, cf_all, mine, sib_in, comb, got, back, ret, sib_out, el_v, prompts,
    pterm, sib_p, pr1a, pr1b, ps1a, ps1b, pr2a, pr2b,
    part, sib, r1a, r1b, r1c, s1a, s1b, s1c, r2a, r2b, r2c, s2a, s2b, s2c, r3a, r3b, r3c,
    x_sem, g_sem, o_sem, c_send, c_recv, f_send, f_recv, l_send, l_recv, p_send, p_recv,
    a_send, a_recv, b_send, b_recv, li_sem, s_send, s_recv, w_send, w_recv, q_send, q_recv,
):
    group, seq = lax.axis_index("group"), lax.axis_index("seq")
    core = seq % 2
    chip = seq // 2
    y, z = chip // 4, chip % 4
    sibling = (group, chip * 2 + (1 - core))
    is0 = core == 0

    def chip_at(d):
        return ((y + d // 4) % 4) * 4 + (z + d % 4) % 4

    def in_plane(d):
        return (group, chip_at(d) * 2 + core)

    def to_x(d):
        return ((group + d) % 4, seq)

    def to_y(d):
        return in_plane(4 * d)

    def to_z(d):
        return in_plane(d)

    def send(src, dst, s, r, to):
        return pltpu.make_async_remote_copy(
            src_ref=src, dst_ref=dst, send_sem=s, recv_sem=r, device_id=to, device_id_type=MESH
        )

    def lanes(j):
        return pl.ds(pl.multiple_of(PLANES * j, PLANES), PLANES)

    def load_x(j):
        return pltpu.make_async_copy(x_hbm.at[:, lanes(j)], xg_v.at[0, :, lanes(j)], x_sem.at[j])

    def load_g(j):
        return pltpu.make_async_copy(g_hbm.at[:, lanes(j)], xg_v.at[1, :, lanes(j)], g_sem.at[j])

    def load_li(n):
        return pltpu.make_async_copy(li_hbm.at[:, WIDTH * n : WIDTH * (n + 1)], xg_v.at[n], li_sem.at[n])

    def store(j):
        return pltpu.make_async_copy(dx_v.at[:, lanes(j)], xg_hbm.at[:, lanes(j)], o_sem.at[0])

    def each(lo, hi, f):
        def step(i, _):
            f(i)
            return 0

        lax.fori_loop(lo, hi, step, 0)

    def begin(j):
        load_x(j).start()
        load_g(j).start()

    each(0, PHASES, begin)

    barrier = pltpu.get_barrier_semaphore()

    def greet(to):
        pl.semaphore_signal(barrier, inc=1, device_id=to, device_id_type=MESH)

    greet(sibling)
    each(1, 16, lambda d: greet(in_plane(d)))
    each(1, 4, lambda d: greet(to_x(d)))

    prepare(step_ref, rate_ref, la_v, t1_v, t1b_v, t2b_v)
    ns, nl = flags(lens_ref)
    cf_mine[...] = device_coefficients(ns, nl, t1_v)

    def start_phase(t):
        load_x(t).wait()
        load_g(t).wait()
        summarize(t, ns, nl, xg_v, b_ref, c_ref, la_v, t1b_v, t2b_v, sx_v, sg_v, loc_v, mine)

    start_phase(0)
    pl.semaphore_wait(barrier, 19)

    def prompt_copy(d):
        return send(p_ref, prompts.at[chip, core], p_send.at[1], p_recv.at[1], in_plane(d))

    def prompt_all():
        some = prompts.at[pl.ds(0, 15), 0]
        return send(some, some, p_send.at[1], p_recv.at[1], sibling)

    def prompt_pass():
        half = prompts.at[:, core]
        return send(half, half, p_send.at[0], p_recv.at[0], sibling)

    def coefficient_pass():
        return send(cf_mine, cf_sib, c_send.at[0], c_recv.at[0], sibling)

    def coefficient_copy(d):
        return send(cf_chip, cf_all.at[chip], c_send.at[1], c_recv.at[1], in_plane(d))

    def coefficient_all():
        some = cf_all.at[pl.ds(0, 15)]
        return send(some, some, c_send.at[1], c_recv.at[1], sibling)

    def chip_copy(j):
        return send(mine.at[j, :, 1 - core], sib_in.at[j], f_send.at[j], f_recv.at[j], sibling)

    def out_copy(j, d):
        return send(comb.at[j, chip_at(d)], got.at[j, chip], a_send.at[j], a_recv.at[j], in_plane(d))

    def out_all(j):
        some = pl.ds(0, 15)
        return send(comb.at[j, some], got.at[j, some], a_send.at[j], a_recv.at[j], sibling)

    def back_copy(j, d):
        return send(back.at[j, chip_at(d)], ret.at[j, chip], b_send.at[j], b_recv.at[j], in_plane(d))

    def back_all(j):
        some = pl.ds(0, 15)
        return send(back.at[j, some], ret.at[j, some], b_send.at[j], b_recv.at[j], sibling)

    def last_copy(j):
        return send(sib_out.at[j], el_v.at[j, :, core], l_send.at[j], l_recv.at[j], sibling)

    coefficient_pass().start()
    chip_copy(0).start()
    each(1, 16, lambda d: prompt_copy(d).start())
    prompts[chip, core] = p_ref[...]

    def pick(a, b):
        return jnp.where(is0, a, b), jnp.where(is0, b, a)

    def both(j):
        heads = PHEADS * j + iota((16, 128), 0) // 2

        def spread(tile):
            return [
                gather(jnp.broadcast_to(tile[n : n + 1], (16, 128)), heads)[:, None, :] for n in range(3)
            ]

        a, b = pick(mine[j, :, core], sib_in[j])
        t0, t1 = pick(cf_mine[...], cf_sib[...])
        return a, b, spread(t0), spread(t1)

    def combine(j):
        a, b, (_, _, ab0), (af1, _, _) = both(j)
        comb[j, :, 0:16, :] = b[:, 0:16] + af1 * a[:, 0:16]
        comb[j, :, 16:32, :] = a[:, 16:32] + ab0 * b[:, 16:32]

    def piece(j, owner):
        at = 32 * j + owner
        return at // 10, (at // 5) % 2, pl.ds(pl.multiple_of(16 * (at % 5), 16), 16)

    def prompt_rows(j, owner):
        a, b, rows = piece(j, owner)
        return prompts[a, b, rows, :]

    def scan(j):
        own = prompt_rows(j, seq)
        head = jnp.full((128, 128), PHEADS * j + seq // 4, jnp.int32)
        cf = gather(cf_all[...].reshape(128, 128), head)
        e = jnp.zeros((16, 128), F32)
        for q in range(16):
            back[j, q, 0:16, :] = e
            e = cf[8 * q : 8 * q + 1] * e + (cf[8 * q + 1 : 8 * q + 2] * own + got[j, q, 0:16, :])
        lv = jnp.zeros((16, 128), F32)
        for q in reversed(range(16)):
            back[j, q, 16:32, :] = lv
            lv = cf[8 * q + 2 : 8 * q + 3] * lv + got[j, q, 16:32, :]

    def finish(j):
        a, b, (af0, pc0, _), (_, _, ab1) = both(j)
        e0, l1 = ret[j, :, 0:16, :], ret[j, :, 16:32, :]
        prompt = jnp.stack([prompt_rows(j, 2 * q + core) for q in range(16)], axis=0)
        e1 = af0 * e0 + (pc0 * prompt + a[:, 0:16])
        l0 = ab1 * l1 + b[:, 16:32]
        e_mine, e_other = pick(e0, e1)
        l_mine, l_other = pick(l0, l1)
        el_v[j, :, core, 0:16, :] = e_mine
        el_v[j, :, core, 16:32, :] = l_mine
        sib_out[j, :, 0:16, :] = e_other
        sib_out[j, :, 16:32, :] = l_other

    keep = iota((BLOCK, BLOCK), 1) >= iota((BLOCK, BLOCK), 0)

    def tick(t):
        @pl.when(t < PHASES)
        def _():
            start_phase(t)
            chip_copy(t).start()

        @pl.when(t == 1)
        def _():
            coefficient_pass().wait()
            t0, t1 = pick(cf_mine[...], cf_sib[...])
            cf_chip[...] = jnp.concatenate(
                [t0[0:1] * t1[0:1], t1[1:2] + t1[0:1] * t0[1:2], t0[2:3] * t1[2:3], t0[3:8]], axis=0
            )
            each(1, 16, lambda d: coefficient_copy(d).start())
            cf_all[chip] = cf_chip[...]

        @pl.when(t < PHASES + 1)
        def _():
            j = t - 1
            chip_copy(j).wait()
            combine(j)
            for d in range(1, 16):
                out_copy(j, d).start()
            got[j, chip] = comb[j, chip]

        @pl.when(t == 2)
        def _():
            prompt_all().wait()
            prompt_pass().start()

        @pl.when(t == 3)
        def _():
            prompt_pass().wait()
            coefficient_all().wait()

        @pl.when(t == 4)
        def _():
            for k in range(NBLK):
                rows = blockrows(k)
                inner_v[k] = jnp.where(keep, dot(b_ref[rows, :], c_ref[rows, :], NT), 0.0)
                pt_v[k] = jnp.zeros((BLOCK, BLOCK), F32)
            acc_v[...] = jnp.zeros_like(acc_v)

        @pl.when((t >= 5) & (t < PHASES + 5))
        def _():
            each(0, NBLK, lambda k: inside_unit(t - 5, k, xg_v, la_v, t1_v, inner_v, pt_v, dx_v))

        @pl.when((t >= 4) & (t < PHASES + 4))
        def _():
            j = t - 4
            out_all(j).wait()
            scan(j)
            for d in range(1, 16):
                back_copy(j, d).start()
            ret[j, chip] = back[j, chip]

        @pl.when(t == PHASES + 4)
        def _():
            for n in range(2):
                load_li(n).start()

        @pl.when((t >= 7) & (t < PHASES + 7))
        def _():
            j = t - 7
            back_all(j).wait()
            finish(j)
            last_copy(j).start()

        @pl.when(t >= 8)
        def _():
            j = t - 8
            last_copy(j).wait()
            prompt = jnp.stack([prompt_rows(j, o) for o in range(32)], axis=0)
            total = gradients(j, ns, nl, b_ref, la_v, t1b_v, sx_v, sg_v, loc_v, prompt, el_v, dx_v, acc_v)
            store(j).start()
            for o in range(32):
                a, b, rows = piece(j, o)
                pterm[a // 4, a % 4, b, rows, :] = total[o]

    each(1, TICKS, tick)

    def p_copy(n, stage, d, src, dst, to):
        return send(src, dst, q_send.at[n, stage], q_recv.at[n, stage], to)

    def p_chip():
        return p_copy(2, 0, 0, pterm.at[:, :, 1 - core], sib_p, sibling)

    def p_first(n, d):
        if n == 0:
            return p_copy(n, 0, d, pterm.at[(y + d) % 4, :, core, 0:40], pr1a.at[d], to_y(d))
        return p_copy(n, 0, d, pterm.at[:, (z + d) % 4, core, 40:80], pr1b.at[d], to_z(d))

    def p_second(n, d):
        if n == 0:
            return p_copy(n, 1, d, ps1a.at[(z + d) % 4], pr2a.at[d], to_z(d))
        return p_copy(n, 1, d, ps1b.at[(y + d) % 4], pr2b.at[d], to_y(d))

    p_chip().start()
    for k in range(NBLK):
        rows = blockrows(k)
        pt = jnp.where(keep, pt_v[k], 0.0).astype(BF16)
        bc_v[rows, :128] = (acc_v[rows, :128] + dot(pt, c_ref[rows, :])).astype(BF16)
        bc_v[rows, 128:] = (acc_v[rows, 128:] + dot(pt, b_ref[rows, :], TN)).astype(BF16)
    def w_copy(n, stage, d, src, dst, to):
        return send(src, dst, w_send.at[n, stage], w_recv.at[n, stage], to)

    def cut(n):
        return pl.ds(ROWS[n][0], ROWS[n][1] - ROWS[n][0]), pl.ds(COLS[n][0], COLS[n][1] - COLS[n][0])

    def slab_x(s):
        return (group + s) % 4

    def sib_copy(s, n):
        at = slab_x(s)
        return send(
            part.at[at, pl.ds(2 * n, 2), :, 1 - core], sib.at[at, pl.ds(2 * n, 2)],
            s_send.at[s], s_recv.at[s], sibling,
        )

    def sib_all(s):
        at = slab_x(s)
        return send(part.at[at, :, :, 1 - core], sib.at[at], s_send.at[s], s_recv.at[s], sibling)

    def first_x(d):
        return w_copy(0, 0, d, part.at[slab_x(d), :, :, core, *cut(0)], r1a.at[d - 1], to_x(d))

    def first_y(s, d):
        at = slab_x(s)
        return send(
            part.at[at, (y + d) % 4, :, core, *cut(1)], r1b.at[d - 1, at],
            w_send.at[1, 0], w_recv.at[1, 0], to_y(d),
        )

    def first_z(s, d):
        at = slab_x(s)
        return send(
            part.at[at, :, (z + d) % 4, core, *cut(2)], r1c.at[d - 1, at],
            w_send.at[2, 0], w_recv.at[2, 0], to_z(d),
        )

    def settle(s):
        at = slab_x(s)
        sib_all(s).wait()
        part[at, :, :, core] = part[at, :, :, core] + sib[at]
        if s > 0:
            first_x(s).start()
        for d in (2, 1, 3):
            first_y(s, d).start()
            first_z(s, d).start()

    for n in range(2):
        load_li(n).wait()
    bc = bc_v[...]
    order = (2, 1, 3, 0)
    for i, s in enumerate(order):
        at = slab_x(s)
        for n in range(2):
            m = at * 2 + n
            cols = pl.ds(pl.multiple_of(SLAB * (m % 4), SLAB), SLAB)
            out = dot(xg_v[m // 4, :, cols], bc, TN)
            part[at, 2 * n : 2 * n + 2] = out.reshape(2, 4, 2, 40, 256)
            sib_copy(s, n).start()
        if i > 0:
            settle(order[i - 1])
    settle(0)
    p_chip().wait()
    pterm[:, :, core] = pterm[:, :, core] + sib_p[...]
    for d in (1, 3, 2):
        for n in range(2):
            p_first(n, d).start()

    def second(n, d):
        if n == 0:
            return w_copy(n, 1, d, s1a.at[(y + d) % 4], r2a.at[d], to_y(d))
        if n == 1:
            return w_copy(n, 1, d, s1b.at[:, (z + d) % 4], r2b.at[d], to_z(d))
        return w_copy(n, 1, d, s1c.at[(group + d) % 4], r2c.at[d], to_x(d))

    def third(n, d):
        if n == 0:
            return w_copy(n, 2, d, s2a.at[(z + d) % 4], r3a.at[d], to_z(d))
        if n == 1:
            return w_copy(n, 2, d, s2b.at[(group + d) % 4], r3b.at[d], to_x(d))
        return w_copy(n, 2, d, s2c.at[(y + d) % 4], r3c.at[d], to_y(d))

    three = pl.ds(1, 3)
    peers = pl.ds(0, 3)
    for n in range(3):
        if n == 0:
            w_copy(0, 0, 1, r1a, r1a, sibling).wait()
            s1a[...] = part[group, :, :, core, 16:40, 0:128] + r1a[0] + r1a[1] + r1a[2]
        elif n == 1:
            w_copy(1, 0, 1, r1b, r1b, sibling).wait()
            s1b[...] = part[:, y, :, core, 16:40, 128:256] + r1b[0] + r1b[1] + r1b[2]
        else:
            w_copy(2, 0, 1, r1c, r1c, sibling).wait()
            s1c[...] = part[:, :, z, core, 0:16] + r1c[0] + r1c[1] + r1c[2]
        for d in (1, 3, 2):
            second(n, d).start()
    p_copy(0, 0, 1, pterm.at[peers, :, 0, 0:40], pr1a.at[three], sibling).wait()
    p_copy(1, 0, 1, pterm.at[peers, :, 0, 40:80], pr1b.at[three], sibling).wait()
    ps1a[...] = pterm[y, :, core, 0:40] + pr1a[1] + pr1a[2] + pr1a[3]
    ps1b[...] = pterm[:, z, core, 40:80] + pr1b[1] + pr1b[2] + pr1b[3]
    for d in (1, 3, 2):
        for n in range(2):
            p_second(n, d).start()

    for n, r in enumerate((r2a, r2b, r2c)):
        w_copy(n, 1, 1, r.at[three], r.at[three], sibling).wait()
        if n == 0:
            s2a[...] = s1a[y] + r2a[1] + r2a[2] + r2a[3]
        elif n == 1:
            s2b[...] = s1b[:, z] + r2b[1] + r2b[2] + r2b[3]
        else:
            s2c[...] = s1c[group] + r2c[1] + r2c[2] + r2c[3]
        for d in (1, 3, 2):
            third(n, d).start()
    p_copy(0, 1, 1, pr2a.at[three], pr2a.at[three], sibling).wait()
    p_copy(1, 1, 1, pr2b.at[three], pr2b.at[three], sibling).wait()
    pg_ref[0:40, :] = ps1a[z] + pr2a[1] + pr2a[2] + pr2a[3]
    pg_ref[40:80, :] = ps1b[y] + pr2b[1] + pr2b[2] + pr2b[3]
    for n, (own, r, at) in enumerate(((s2a, r3a, z), (s2b, r3b, group), (s2c, r3c, y))):
        w_copy(n, 2, 1, r.at[three], r.at[three], sibling).wait()
        wg_ref[ROWS[n][0] : ROWS[n][1], COLS[n][0] : COLS[n][1]] = own[at] + r[1] + r[2] + r[3]
    pltpu.make_async_copy(dx_v, xg_hbm, o_sem.at[0]).wait()


def layer(lens, step, rates, x, g, b, c, p, li):
    v = pl.BlockSpec(memory_space=pltpu.VMEM)
    a = pl.BlockSpec(memory_space=pl.ANY)
    wide = pltpu.VMEM((TOK, WIDTH), BF16)
    square = pltpu.VMEM((NBLK, BLOCK, BLOCK), F32)
    f = lambda *shape: pltpu.VMEM(shape, F32)
    dma = lambda *n: pltpu.SemaphoreType.DMA(n)
    half = f(PHASES, 16, 32, 128)
    return pl.pallas_call(
        layer_kernel,
        in_specs=[pl.BlockSpec(memory_space=pltpu.SMEM), v, v, a, a, v, v, v, a],
        out_specs=[a, v, v],
        out_shape=[
            jax.ShapeDtypeStruct((TOK, WIDTH), BF16),
            jax.ShapeDtypeStruct((80, 128), F32),
            jax.ShapeDtypeStruct((40, 256), F32),
        ],
        scratch_shapes=[
            pltpu.VMEM((2, TOK, WIDTH), BF16), wide, wide, wide,
            f(HEADS, TOK), f(TOK, 128), pltpu.VMEM((TOK, 256), BF16), pltpu.VMEM((TOK, 256), BF16), square, square, f(TOK, 256),
            f(PHASES, 5, PHEADS, 64, 128), pltpu.VMEM((TOK, 256), BF16),
            f(8, 128), f(8, 128), f(8, 128), f(16, 8, 128),
            f(PHASES, 16, 2, 32, 128), half, half, half, half, half, half,
            f(PHASES, 16, 2, 32, 128), f(16, 2, 80, 128),
            f(4, 4, 2, 80, 128), f(4, 4, 80, 128), f(4, 4, 40, 128), f(4, 4, 40, 128),
            f(4, 40, 128), f(4, 40, 128), f(4, 40, 128), f(4, 40, 128),
            f(4, 4, 4, 2, 40, 256), f(4, 4, 4, 40, 256),
            f(3, 4, 4, 24, 128), f(3, 4, 4, 24, 128), f(3, 4, 4, 16, 256),
            f(4, 4, 24, 128), f(4, 4, 24, 128), f(4, 4, 16, 256),
            f(4, 4, 24, 128), f(4, 4, 24, 128), f(4, 4, 16, 256),
            f(4, 24, 128), f(4, 24, 128), f(4, 16, 256),
            f(4, 24, 128), f(4, 24, 128), f(4, 16, 256),
            dma(PHASES), dma(PHASES), dma(1), dma(2), dma(2), dma(PHASES), dma(PHASES),
            dma(PHASES), dma(PHASES), dma(2), dma(2), dma(PHASES), dma(PHASES),
            dma(PHASES), dma(PHASES), dma(2), dma(4), dma(4), dma(3, 3), dma(3, 3), dma(3, 2), dma(3, 2),
        ],
        compiler_params=pltpu.CompilerParams(
            collective_id=0, has_side_effects=True, vmem_limit_bytes=VMEM_LIMIT
        ),
    )(lens, step, rates, x, g, b, c, p, li)


def deliver_kernel(x_hbm, p_ref, w_ref, xo_hbm, po_ref, wo_ref, hold, sems):
    def into(n):
        rows = pl.ds(n * PIECE, PIECE)
        return pltpu.make_async_copy(x_hbm.at[rows], hold.at[n], sems.at[0, n])

    def out(n):
        rows = pl.ds(n * PIECE, PIECE)
        return pltpu.make_async_copy(hold.at[n], xo_hbm.at[rows], sems.at[1, n])

    count = TOK // PIECE
    for n in range(count):
        into(n).start()
    po_ref[...] = p_ref[...]
    wo_ref[...] = w_ref[...]
    for n in range(count):
        into(n).wait()
        out(n).start()
    for n in range(count):
        out(n).wait()


PIECE = 96


def deliver(x, p, w):
    v = pl.BlockSpec(memory_space=pltpu.VMEM)
    a = pl.BlockSpec(memory_space=pl.ANY)
    return pl.pallas_call(
        deliver_kernel,
        in_specs=[a, v, v],
        out_specs=[a, v, v],
        out_shape=[jax.ShapeDtypeStruct(t.shape, t.dtype) for t in (x, p, w)],
        scratch_shapes=[
            pltpu.VMEM((TOK // PIECE, PIECE, WIDTH), BF16), pltpu.SemaphoreType.DMA((2, TOK // PIECE))
        ],
        compiler_params=pltpu.CompilerParams(vmem_limit_bytes=VMEM_LIMIT),
    )(x, p, w)


def body(li, x, g, b, c, step, rates, prompt, lens):
    li, x, g, b, c, step, prompt = li[0], x[0], g[0], b[0], c[0], step[0], prompt[0]
    x_grad, prompt_grad, weight_grad = layer(
        lens, step, rates.reshape(1, HEADS), x, g, b, c, prompt, li
    )
    x_grad, prompt_grad, weight_grad = deliver(x_grad, prompt_grad, weight_grad)
    return x_grad[None], prompt_grad[None], weight_grad


def solution(mesh):
    in_specs = (
        P("group", "seq", None),
        P("group", "seq", None),
        P("group", "seq", None),
        P("group", "seq", None),
        P("group", "seq", None),
        P("group", None, "seq"),
        P(),
        P("group", "seq", None),
        P("group", None),
    )
    out_specs = (P("group", "seq", None), P("group", "seq", None), P(("group", "seq"), None))
    return jax.shard_map(body, mesh=mesh, in_specs=in_specs, out_specs=out_specs, check_vma=False)
```
